32 devices in a mesh: sec: 4 (over y, core), tile: 8 (over z, x).
Axes of the slice: x: 2, y: 2, z: 4, core: 2. Of those that a mesh axis runs over, the one named last changes fastest.
Arguments:
- parent_old: float32 [128, 24, 4096], P('tile', None, 'sec'), may hold values from -6 to 6
- nest_state: float32 [4, 128, 24, 512], P('sec', 'tile'), may hold values from -6 to 6
- diffusion: float32 [24], replicated, may hold values from 0.04 to 0.1
- wind_speed: float32 [2, 24], replicated, may hold values from 0.05 to 0.25
- conversion: float32 [2, 8], replicated, may hold values from 0.05 to 0.4
- vert_mix: float32 [3], replicated, may hold values from 0.5 to 4
- nest_box: int32 [4, 4], replicated, may hold values from 0 to 3968, as said below
Outputs:
- parent_new: float32 [128, 24, 4096], P('tile', None, 'sec')
- nest_new: float32 [4, 128, 24, 512], P('sec', 'tile')
The draws below stay inside these ranges and needn't reach their ends.
Inputs may be any that keep to these rules, and one draw needn't show every extreme that they name: `nest_box`: row n belongs to nest n, which lives on section n. Anchors are parent cells and keep the footprint of 32 by 128 parent cells inside the parent grid; live rows lie between 64 and 128, live columns between 256 and 512; some nest is live everywhere.
All inputs are finite; a program needn't handle non-finite values.
Results may differ from the reference program's by a relative error of at most 0.00002.
Values sent between devices are 32-bit elements; how exact they have to be, the bound alone decides.
No kernel may reach another device: no remote copies, remote signals or barrier semaphores. Data moves between devices by JAX's collectives and lax.ppermute only.
A program may use at most 64 MiB of HBM per device.

```python
import math
import jax
import jax.numpy as jnp
from jax import lax

NY = 512
LEV = 8
NSTEP = 4
CHAN = 24
NNEST = 4
PX = 128
PY = 4096
NX = 128


def draw_nest_box(key, part):
    quarter_x = NX // 4
    quarter_y = NY // 4
    anchor_x = jax.random.randint(jax.random.fold_in(key, 11), (NNEST,), 0, PX - quarter_x + 1)
    anchor_y = jax.random.randint(jax.random.fold_in(key, 12), (NNEST,), 0, PY - quarter_y + 1)
    extent_x = jax.random.randint(jax.random.fold_in(key, 13), (NNEST,), NX // 2, NX + 1)
    extent_y = jax.random.randint(jax.random.fold_in(key, 14), (NNEST,), NY // 2, NY + 1)
    shuffled = jax.random.permutation(jax.random.fold_in(key, 15), NNEST)
    nest_ids = jnp.arange(NNEST)
    extent_x = jnp.where(nest_ids == shuffled[0], NX, extent_x)
    extent_y = jnp.where(nest_ids == shuffled[0], NY, extent_y)
    anchor_y = jnp.where(nest_ids == shuffled[1], PY - quarter_y, anchor_y)
    anchor_x = jnp.where(nest_ids == shuffled[2], PX - quarter_x, anchor_x)
    return jnp.stack([anchor_x, anchor_y, extent_x, extent_y], axis=1).astype(jnp.int32)


def block_scale(rng, dims, pieces, least, largest):
    factor_of = 1.0
    for position, parts in pieces:
        draws = jax.random.uniform(jax.random.fold_in(jax.random.fold_in(rng, 6), position), (parts,), jnp.float32, least / len(pieces), largest / len(pieces))
        factor_of = factor_of * jnp.repeat(jnp.exp(draws), dims[position] // parts).reshape((-1,) + (1,) * (len(dims) - 1 - position))
    return factor_of


def noise(own_key, dims, deviation, bound, split=(), kind=jnp.bfloat16):
    array = deviation * jax.random.normal(own_key, dims, jnp.float32)
    if split:
        array = array * block_scale(own_key, dims, split, -0.22, 0.18)
    return jnp.clip(array, -bound, bound).astype(kind)


def setup_inputs(seed: int = 0) -> dict:
    key_of = jax.random.split(jax.random.key(seed), 8)
    parent_old = noise(key_of[0], (PX, CHAN, PY), 1.0, 6.0, ((0, 8), (2, 4)), jnp.float32)
    nest_state = noise(key_of[1], (NNEST, NX, CHAN, NY), 1.0, 6.0, ((0, 4), (1, 8)), jnp.float32)
    diffusion = jnp.clip(jax.random.uniform(key_of[2], (CHAN,), jnp.float32, 0.04, 0.1), 0.04, 0.1)
    wind_speed = jnp.clip(jax.random.uniform(key_of[3], (2, CHAN), jnp.float32, 0.05, 0.25), 0.05, 0.25)
    conversion = jnp.clip(jnp.exp(jax.random.uniform(key_of[4], (2, LEV), jnp.float32, math.log(0.05), math.log(0.4))), 0.05, 0.4)
    vert_mix = jnp.clip(jnp.exp(jax.random.uniform(key_of[5], (3,), jnp.float32, math.log(0.5), math.log(4.0))), 0.5, 4.0)
    nest_box = draw_nest_box(jax.random.fold_in(key_of[7], 71), 0)
    return dict(parent_old=parent_old, nest_state=nest_state, diffusion=diffusion, wind_speed=wind_speed, conversion=conversion, vert_mix=vert_mix, nest_box=nest_box)


def horizontal(padded, diffusion, wind_speed):
    center = padded[1:-1, :, 1:-1]
    above_row = padded[:-2, :, 1:-1]
    below_row = padded[2:, :, 1:-1]
    left_col = padded[1:-1, :, :-2]
    right_col = padded[1:-1, :, 2:]
    spread = diffusion[:, None]
    drift_x = wind_speed[0][:, None]
    drift_y = wind_speed[1][:, None]
    return (center + spread * (above_row + below_row + left_col + right_col - 4.0 * center)
            - drift_x * (center - above_row) - drift_y * (center - left_col))


def vertical(column_data, mixing):
    levels = column_data.shape[1]
    off_diag = -mixing
    ratios = []
    partials = []
    for level_idx in range(levels):
        neighbours = 1.0 if level_idx in (0, levels - 1) else 2.0
        pivot_val = 1.0 + neighbours * mixing
        rhs_now = column_data[:, level_idx]
        if level_idx > 0:
            pivot_val = pivot_val - off_diag * ratios[-1]
            rhs_now = rhs_now - off_diag * partials[-1]
        ratios.append(off_diag / pivot_val)
        partials.append(rhs_now / pivot_val)
    solved = [partials[-1]]
    for level_idx in range(levels - 2, -1, -1):
        solved.insert(0, partials[level_idx] - ratios[level_idx] * solved[0])
    return jnp.stack(solved, axis=1)


def physics(fields, conversion, vert_mix):
    row_count, chan_count, col_count = fields.shape
    levels = conversion.shape[1]
    grouped = fields.reshape(row_count, 3, levels, col_count)
    vapour = grouped[:, 0]
    cloud = grouped[:, 1]
    rain_water = grouped[:, 2]
    condense = conversion[0][:, None] * vapour
    vapour = vapour - condense
    cloud = cloud + condense
    fallout = conversion[1][:, None] * cloud
    cloud = cloud - fallout
    rain_water = rain_water + fallout
    solved = [vertical(vapour, vert_mix[0]), vertical(cloud, vert_mix[1]), vertical(rain_water, vert_mix[2])]
    return jnp.stack(solved, axis=1).reshape(row_count, chan_count, col_count)


def upsample(coarse, base, targets, foot_rows, foot_cols, nest_cols):
    low_row = jnp.floor_divide(targets, 4)
    weight_row = ((targets - 4 * low_row).astype(jnp.float32) / 4.0)[:, None, None]
    first_row = jnp.clip(low_row, 0, foot_rows - 1)
    second_row = jnp.clip(low_row + 1, 0, foot_rows - 1)
    lower_vals = jnp.take(coarse, (first_row - base).astype(jnp.int32), axis=0)
    upper_vals = jnp.take(coarse, (second_row - base).astype(jnp.int32), axis=0)
    row_mix = lower_vals + weight_row * (upper_vals - lower_vals)
    col_ids = jnp.arange(nest_cols, dtype=jnp.int32)
    first_col = jnp.floor_divide(col_ids, 4)
    second_col = jnp.minimum(first_col + 1, foot_cols - 1)
    weight_col = (col_ids - 4 * first_col).astype(jnp.float32) / 4.0
    left_vals = jnp.take(row_mix, first_col, axis=2)
    right_vals = jnp.take(row_mix, second_col, axis=2)
    return left_vals + weight_col * (right_vals - left_vals)


def nest_fields(targets, nest_cols, extent_x, extent_y):
    row_ids = targets[:, None]
    col_ids = jnp.arange(nest_cols, dtype=jnp.int32)[None, :]
    live_mask = ((row_ids >= 0) & (row_ids < extent_x) & (col_ids < extent_y)).astype(jnp.float32)
    distance = jnp.minimum(jnp.minimum(row_ids, col_ids),
                           jnp.minimum(extent_x - 1 - row_ids, extent_y - 1 - col_ids))
    distance = jnp.maximum(distance, 0).astype(jnp.float32)
    nudging = 0.1 + 0.4 * jnp.exp(-distance / 3.0)
    return live_mask[:, None, :], nudging[:, None, :]


def nest_step(rows_padded, live_mask, nudging, forcing_now, diffusion, wind_speed, conversion, vert_mix):
    padded = jnp.pad(rows_padded, ((0, 0), (0, 0), (1, 1)))
    moved = physics(horizontal(padded, diffusion, wind_speed), conversion, vert_mix)
    moved = moved + nudging * (forcing_now - moved)
    return moved * live_mask


def reference(parent_old, nest_state, diffusion, wind_speed, conversion, vert_mix, nest_box):
    padded = jnp.pad(parent_old, ((1, 1), (0, 0), (1, 1)))
    parent_new = physics(horizontal(padded, diffusion, wind_speed), conversion, vert_mix)
    foot_rows = NX // 4
    foot_cols = NY // 4
    chan_count = parent_old.shape[1]
    results = []
    for nest_idx in range(NNEST):
        anchor_x = nest_box[nest_idx, 0].astype(jnp.int32)
        anchor_y = nest_box[nest_idx, 1].astype(jnp.int32)
        extent_x = nest_box[nest_idx, 2].astype(jnp.int32)
        extent_y = nest_box[nest_idx, 3].astype(jnp.int32)
        start = (anchor_x, jnp.int32(0), anchor_y)
        old_part = lax.dynamic_slice(parent_old, start, (foot_rows, chan_count, foot_cols))
        new_part = lax.dynamic_slice(parent_new, start, (foot_rows, chan_count, foot_cols))
        both_times = jnp.concatenate([old_part, new_part], axis=1)
        targets = jnp.arange(NX, dtype=jnp.int32)
        forcing = upsample(both_times, jnp.int32(0), targets, foot_rows, foot_cols, NY)
        live_mask, nudging = nest_fields(targets, NY, extent_x, extent_y)
        forcing_old = forcing[:, :chan_count]
        forcing_new = forcing[:, chan_count:]
        nest_now = nest_state[nest_idx] * live_mask
        for step_num in range(NSTEP):
            weight_now = (step_num + 1) / NSTEP
            forcing_now = forcing_old + weight_now * (forcing_new - forcing_old)
            rows_padded = jnp.pad(nest_now, ((1, 1), (0, 0), (0, 0)))
            nest_now = nest_step(rows_padded, live_mask, nudging, forcing_now,
                                 diffusion, wind_speed, conversion, vert_mix)
        results.append(nest_now)
    return parent_new, jnp.stack(results)
```

```python
import jax
import jax.numpy as jnp
from jax import lax
from jax.experimental import pallas as pl
from jax.experimental.pallas import tpu as pltpu
from jax.sharding import PartitionSpec as P

NSTEP = 4
RATIO = 4
LANES = 128
F32 = jnp.float32
VMEM = pl.BlockSpec(memory_space=pltpu.VMEM)
SMEM = pl.BlockSpec(memory_space=pltpu.SMEM)


def call(kernel, outs, args, specs, scratch=(), limit=16, flops=0):
    single = not isinstance(outs, (list, tuple))
    shapes = [outs] if single else list(outs)
    moved = sum(4 * a.size for a in args) + sum(4 * s.size for s in shapes)
    out = pl.pallas_call(
        kernel,
        out_shape=shapes,
        in_specs=list(specs),
        out_specs=[VMEM] * len(shapes),
        scratch_shapes=list(scratch),
        compiler_params=pltpu.CompilerParams(vmem_limit_bytes=limit << 20),
        cost_estimate=pl.CostEstimate(flops=flops, bytes_accessed=moved, transcendentals=0),
    )(*args)
    return out[0] if single else out


def shape(*dims):
    return jax.ShapeDtypeStruct(dims, F32)


def lane_ids():
    return lax.broadcasted_iota(jnp.int32, (8, LANES), 1)


def sublane_ids():
    return lax.broadcasted_iota(jnp.int32, (8, LANES), 0)


def exchange(block, axis, bit):
    return lax.ppermute(block, axis, [(i, i ^ bit) for i in range(lax.axis_size(axis))])


def extract(rows, chan, box, parent, keep, send):
    cols = parent.shape[1]
    blocks = cols // LANES
    sec = lax.axis_index("sec")
    half = lax.rem(sec, 2)
    lane = lane_ids()
    groups = chan // 8
    for which, dest in ((1 - half, send), (half, keep)):
        for i in range(dest.shape[0]):
            nest = 2 * i + which
            offset = box[nest, 1] - sec * cols
            first = lax.shift_right_arithmetic(offset, 7)
            shift = lax.bitwise_and(offset, LANES - 1)
            back = lax.bitwise_and(LANES - shift, LANES - 1)

            def place(k):
                start = pl.multiple_of(jnp.clip(k, 0, blocks - 1) * LANES, LANES)
                return start, jnp.where((k >= 0) & (k < blocks), 1.0, 0.0).astype(F32)

            start_a, on_a = place(first)
            start_b, on_b = place(first + 1)
            start_c, on_c = place(first - 1)
            is_low = jnp.where(nest == sec + 1, 1.0, 0.0).astype(F32)
            is_high = jnp.where(nest == sec - 1, 1.0, 0.0).astype(F32)
            extra = [jnp.zeros((8, LANES), F32) for _ in range(groups)]
            for row in range(rows):
                for g in range(groups):
                    at = pl.ds(row * chan + 8 * g, 8)
                    a = pltpu.roll(parent[at, pl.ds(start_a, LANES)] * on_a, back, axis=1)
                    b = pltpu.roll(parent[at, pl.ds(start_b, LANES)] * on_b, back, axis=1)
                    c = parent[at, pl.ds(start_c, LANES)] * on_c
                    dest[i, at, :] = jnp.where(lane < LANES - shift, a, b)
                    west = jnp.where(shift == 0, c, a)
                    last = parent[at, pl.ds(cols - LANES, LANES)] * is_low
                    head = parent[at, pl.ds(0, LANES)] * is_high
                    e = extra[g]
                    e = jnp.where(lane == row, pltpu.roll(west, row + 1, axis=1), e)
                    e = jnp.where(lane == rows + row, pltpu.roll(b, rows + row, axis=1), e)
                    e = jnp.where(lane == 2 * rows + row, pltpu.roll(last, 2 * rows + row + 1, axis=1), e)
                    e = jnp.where(lane == 3 * rows + row, pltpu.roll(head, 3 * rows + row, axis=1), e)
                    extra[g] = e
            for g in range(groups):
                dest[i, pl.ds(rows * chan + 8 * g, 8), :] = extra[g]


def combine(bit, own, got, keep, send):
    mine = lax.rem(lax.axis_index("sec") // bit, 2)
    for i in range(keep.shape[0]):
        send[i] = own[2 * i + 1 - mine] + got[2 * i + 1 - mine]
        keep[i] = own[2 * i + mine] + got[2 * i + mine]


def total(own, got, out):
    out[...] = own[0] + got[0]


def held_block(anchor, rows, own_rows, group):
    tile = lax.axis_index("tile")
    first = lax.div(tile, group) * group
    low = jnp.maximum(anchor + own_rows * first - 2, 0)
    base = lax.div(low, rows)
    return base + lax.bitwise_and(tile - base, group - 1)


def choose(rows, own_rows, group, count, box, own, got, out):
    anchor = box[lax.axis_index("sec"), 0]
    before = held_block(anchor, rows, own_rows, 2 * group)
    if 2 * group == count:
        before = lax.axis_index("tile")
    after = held_block(anchor, rows, own_rows, group)

    @pl.when(before == after)
    def _():
        out[...] = own[...]

    @pl.when(before != after)
    def _():
        out[...] = got[...]


def window(rows, chan, own_rows, box, block, out):
    tile = lax.bitwise_xor(lax.axis_index("tile"), 1)
    start = box[lax.axis_index("sec"), 0] + own_rows * tile - 2
    span = out.shape[0] // chan - 1
    for m in range(span):
        at = pl.multiple_of(lax.bitwise_and(start + m, rows - 1) * chan, 8)
        out[pl.ds(m * chan, chan), :] = block[pl.ds(at, chan), :]
    out[pl.ds(span * chan, chan), :] = block[pl.ds(rows * chan, chan), :]


def coefficients(levels, mix, coef):
    for f in range(3):
        m = jnp.full((8, LANES), mix[f], F32)
        ratio = None
        for l in range(levels):
            pivot = 1.0 + (1.0 if l in (0, levels - 1) else 2.0) * m
            if l:
                pivot = pivot - m * ratio
            inverse = 1.0 / pivot
            ratio = m * inverse
            coef[f, 0, l] = inverse
            coef[f, 1, l] = ratio


def step_block(levels, diff, wind, conv, mix, coef, loads, store):
    passed = None
    for f in range(3):
        m = mix[f]
        ys, carry = [], []
        for l in range(levels):
            c = f * levels + l
            v, n, s, w, e = loads(c)
            d, wx, wy = diff[c], wind[0, c], wind[1, c]
            h = (1.0 - 4.0 * d - wx - wy) * v + (d + wx) * n + (d + wy) * w + d * (s + e)
            if passed is not None:
                h = h + passed[l]
            if f < 2:
                out = conv[f, l] * h
                carry.append(out)
                h = h - out
            if l:
                h = h + coef[f, 1, l - 1] * ys[-1]
            ys.append(h)
        passed = carry
        x = None
        for l in range(levels - 1, -1, -1):
            x = coef[f, 0, l] * (ys[l] if x is None else ys[l] + m * x)
            store(f * levels + l, x)


def parent_step(rows, chan, diff, wind, conv, mix, parent, low, high, strip, out, ext, done, coef, sems):
    levels = conv.shape[1]
    blocks = parent.shape[1] // LANES
    coefficients(levels, mix, coef)
    lane = lane_ids()

    def columns(j):
        return pl.ds(pl.multiple_of(j * LANES, LANES), LANES)

    for row in range(rows):
        for g in range(chan // 8):
            packed = strip[pl.ds(rows * chan + 8 * g, 8), :]
            at = pl.ds((row + 1) * chan + 8 * g, 8)
            ext[0, at, :] = pltpu.roll(packed, LANES - 1 - (2 * rows + row), axis=1)
            ext[blocks + 1, at, :] = pltpu.roll(packed, LANES - (3 * rows + row), axis=1)

    @pl.loop(0, blocks)
    def _(j):
        ext[j + 1, pl.ds(0, chan), :] = low[:, columns(j)]
        ext[j + 1, pl.ds(chan, rows * chan), :] = parent[:, columns(j)]
        ext[j + 1, pl.ds((rows + 1) * chan, chan), :] = high[:, columns(j)]

    @pl.loop(0, blocks)
    def _(j):
        for first in range(0, rows, 8):
            def loads(c):
                def at(r):
                    return pl.ds((first + r) * chan + c, 8, stride=chan)

                v = ext[j + 1, at(1), :]
                w = pltpu.roll(jnp.where(lane == LANES - 1, ext[j, at(1), :], v), 1, axis=1)
                e = pltpu.roll(jnp.where(lane == 0, ext[j + 2, at(1), :], v), LANES - 1, axis=1)
                return v, ext[j + 1, at(0), :], ext[j + 1, at(2), :], w, e

            def store(c, x):
                done[j, pl.ds(first * chan + c, 8, stride=chan), :] = x

            step_block(levels, diff, wind, conv, mix, coef, loads, store)
        pltpu.make_async_copy(done.at[j], out.at[:, columns(j)], sems.at[j]).start()

    @pl.loop(0, blocks)
    def _(j):
        pltpu.make_async_copy(done.at[j], out.at[:, columns(j)], sems.at[j]).wait()


def nest_step(
    rows, chan, own_rows, tiles, parent_rows,
    box, diff, wind, conv, mix, block, got, nest, low, high, out,
    natural, foot, up, state, force, nudge, done, coef, sems,
):
    levels = conv.shape[1]
    nest_rows = nest.shape[0] // chan
    col_blocks = nest.shape[1] // LANES
    deep = low.shape[0] // chan
    ext_rows = nest_rows + 2 * deep
    sec, tile = lax.axis_index("sec"), lax.axis_index("tile")
    anchor, extent_x, extent_y = box[sec, 0], box[sec, 2], box[sec, 3]
    lane, sub = lane_ids(), sublane_ids()
    first_row = nest_rows * tile - deep
    zero = jnp.zeros((8, LANES), F32)

    def columns(j):
        return pl.ds(j * LANES, LANES)

    coefficients(levels, mix, coef)

    for j in range(col_blocks):
        natural[j, pl.ds(0, deep * chan), :] = low[:, columns(j)]
        natural[j, pl.ds(deep * chan, nest_rows * chan), :] = nest[:, columns(j)]
        natural[j, pl.ds((deep + nest_rows) * chan, deep * chan), :] = high[:, columns(j)]

    for j in range(col_blocks):
        for rb in range(0, ext_rows, 8):
            i = first_row + rb + sub
            col = j * LANES + lane
            live = jnp.where((i >= 0) & (i < extent_x) & (col < extent_y), 1.0, 0.0).astype(F32)
            dist = jnp.minimum(jnp.minimum(i, col), jnp.minimum(extent_x - 1 - i, extent_y - 1 - col))
            dist = jnp.maximum(dist, 0).astype(F32)
            rate = 0.1 + 0.4 * jnp.exp(-dist / 3.0)
            nudge[0, j, pl.ds(rb, 8), :] = live * (1.0 - rate)
            nudge[1, j, pl.ds(rb, 8), :] = live * rate
            nudge[2, j, pl.ds(rb, 8), :] = live

    @pl.loop(0, chan)
    def _(c):
        for k in range(2):
            for r in range(0, ext_rows + 16, 8):
                state[k, 0, c, pl.ds(r, 8), :] = zero
                state[k, col_blocks + 1, c, pl.ds(r, 8), :] = zero
            for j in range(col_blocks):
                state[k, j + 1, c, pl.ds(0, 8), :] = zero
                state[k, j + 1, c, pl.ds(ext_rows + 8, 8), :] = zero
        for j in range(col_blocks):
            for rb in range(0, ext_rows, 8):
                v = natural[j, pl.ds(rb * chan + c, 8, stride=chan), :]
                state[0, j + 1, c, pl.ds(8 + rb, 8), :] = v * nudge[2, j, pl.ds(rb, 8), :]

    span = got.shape[0] // chan - 1
    start = anchor + own_rows * tile - 2
    side = lax.rem(tile, 2)
    for m in range(span):
        row = start + m
        local = lax.bitwise_and(row, rows - 1)
        inside = jnp.where((row >= 0) & (row < parent_rows), 1.0, 0.0).astype(F32)
        ours = lax.rem(lax.div(jnp.maximum(row, 0), rows), 2) == side
        west_by = lax.bitwise_and(LANES - 1 - local, LANES - 1)
        east_by = lax.bitwise_and(LANES - rows - local, LANES - 1)
        for g in range(chan // 8):
            mine = block[pl.ds(pl.multiple_of(local * chan + 8 * g, 8), 8), :]
            theirs = got[pl.ds(m * chan + 8 * g, 8), :]
            edge_mine = block[pl.ds(rows * chan + 8 * g, 8), :]
            edge_theirs = got[pl.ds(span * chan + 8 * g, 8), :]
            edge = jnp.where(ours, edge_mine, edge_theirs) * inside
            at = pl.ds(m * chan + 8 * g, 8)
            foot[0, at, :] = pltpu.roll(edge, west_by, axis=1)
            foot[1, at, :] = jnp.where(ours, mine, theirs) * inside
            foot[2, at, :] = pltpu.roll(edge, east_by, axis=1)
    foot[:, pl.ds(span * chan, chan), :] = jnp.zeros((3, chan, LANES), F32)

    def foot_loads(c):
        def at(r):
            return pl.ds(r * chan + c, 8, stride=chan)

        v = foot[1, at(1), :]
        w = pltpu.roll(jnp.where(lane == LANES - 1, foot[0, at(1), :], v), 1, axis=1)
        e = pltpu.roll(jnp.where(lane == 0, foot[2, at(1), :], v), LANES - 1, axis=1)
        return v, foot[1, at(0), :], foot[1, at(2), :], w, e

    def foot_store(c, x):
        old = foot[1, pl.ds(chan + c, 8, stride=chan), :]
        per = LANES // RATIO
        q = lax.rem(lane, RATIO).astype(F32) / RATIO
        for j in range(col_blocks):
            left = j * per + lax.div(lane, RATIO)
            right = jnp.minimum(left + 1, LANES - 1)
            for k, value in enumerate((old, x - old)):
                a = jnp.take_along_axis(value, left, axis=1)
                b = jnp.take_along_axis(value, right, axis=1)
                up[k, j, c] = a + q * (b - a)

    step_block(levels, diff, wind, conv, mix, coef, foot_loads, foot_store)

    @pl.loop(0, chan)
    def _(c):
        for rb in range(0, ext_rows, 8):
            u = rb // RATIO
            i = first_row + rb + sub
            p = lax.rem(sub, RATIO).astype(F32) / RATIO
            p = jnp.where(i >= RATIO * (own_rows * tiles - 1), 0.0, p)
            for j in range(col_blocks):
                b = nudge[1, j, pl.ds(rb, 8), :]
                for k in range(2):
                    r0 = jnp.broadcast_to(up[k, j, c, pl.ds(u, 1), :], (8, LANES))
                    r1 = jnp.broadcast_to(up[k, j, c, pl.ds(u + 1, 1), :], (8, LANES))
                    r2 = jnp.broadcast_to(up[k, j, c, pl.ds(u + 2, 1), :], (8, LANES))
                    a0 = jnp.where(sub < RATIO, r0, r1)
                    a1 = jnp.where(sub < RATIO, r1, r2)
                    force[k, j, c, pl.ds(rb, 8), :] = b * (a0 + p * (a1 - a0))

    for step in range(NSTEP):
        weight = (step + 1) / NSTEP
        last = step == NSTEP - 1
        src, dst = step % 2, (step + 1) % 2

        @pl.loop(0, col_blocks)
        def _(j):
            for rb in range(deep, deep + nest_rows, 8) if last else range(0, ext_rows, 8):
                def loads(c):
                    v = state[src, j + 1, c, pl.ds(8 + rb, 8), :]
                    west = state[src, j, c, pl.ds(8 + rb, 8), :]
                    east = state[src, j + 2, c, pl.ds(8 + rb, 8), :]
                    w = pltpu.roll(jnp.where(lane == LANES - 1, west, v), 1, axis=1)
                    e = pltpu.roll(jnp.where(lane == 0, east, v), LANES - 1, axis=1)
                    n = state[src, j + 1, c, pl.ds(7 + rb, 8), :]
                    return v, n, state[src, j + 1, c, pl.ds(9 + rb, 8), :], w, e

                def store(c, x):
                    at = pl.ds(rb, 8)
                    g = force[0, j, c, at, :] + weight * force[1, j, c, at, :]
                    x = nudge[0, j, at, :] * x + g
                    if last:
                        done[j, pl.ds((rb - deep) * chan + c, 8, stride=chan), :] = x
                    else:
                        state[dst, j + 1, c, pl.ds(8 + rb, 8), :] = x

                step_block(levels, diff, wind, conv, mix, coef, loads, store)
            if last:
                at = pl.ds(pl.multiple_of(j * LANES, LANES), LANES)
                pltpu.make_async_copy(done.at[j], out.at[:, at], sems.at[j]).start()

    for j in range(col_blocks):
        pltpu.make_async_copy(done.at[j], out.at[:, columns(j)], sems.at[j]).wait()


def bound(kernel, *static):
    def run(*refs):
        return kernel(*static, *refs)

    return run


def body(parent_old, nest_state, diffusion, wind_speed, conversion, vert_mix, nest_box):
    rows, chan, cols = parent_old.shape
    nest_rows, nest_cols = nest_state.shape[1], nest_state.shape[3]
    secs, tiles = lax.axis_size("sec"), lax.axis_size("tile")
    own_rows = nest_rows // RATIO
    levels = conversion.shape[1]
    deep = NSTEP
    ext_rows = nest_rows + 2 * deep
    col_blocks = nest_cols // LANES
    blocks = cols // LANES
    span = (ext_rows // RATIO + 1) + 2
    strip_rows = (rows + 1) * chan
    parent = parent_old.reshape(rows * chan, cols)
    nest = nest_state.reshape(nest_rows * chan, nest_cols)
    params = (diffusion, wind_speed, conversion, vert_mix)

    def neighbours(block, axis, low, high):
        forward = [(i, i + 1) for i in range(lax.axis_size(axis) - 1)]
        backward = [(j, i) for i, j in forward]
        return lax.ppermute(high, axis, forward), lax.ppermute(low, axis, backward)

    half = shape(secs // 2, strip_rows, LANES)
    keep, send = call(
        bound(extract, rows, chan), [half, half], (nest_box, parent), (SMEM, VMEM)
    )
    got = exchange(send, "sec", 1)
    bit = 2
    while bit < secs:
        half = shape(secs // (2 * bit), strip_rows, LANES)
        keep, send = call(
            bound(combine, bit), [half, half], (keep, got), (VMEM, VMEM)
        )
        got = exchange(send, "sec", bit)
        bit *= 2
    strip = call(total, shape(strip_rows, LANES), (keep, got), (VMEM, VMEM))

    nest_low, nest_high = neighbours(nest, "tile", nest[: deep * chan], nest[-deep * chan :])
    parent_low, parent_high = neighbours(parent, "tile", parent[:chan], parent[-chan:])

    block = strip
    group = tiles // 2
    while group > 1:
        got = exchange(block, "tile", group)
        block = call(
            bound(choose, rows, own_rows, group, tiles), shape(strip_rows, LANES),
            (nest_box, block, got), (SMEM, VMEM, VMEM),
        )
        group //= 2
    message = call(
        bound(window, rows, chan, own_rows), shape((span + 1) * chan, LANES),
        (nest_box, block), (SMEM, VMEM),
    )
    got = exchange(message, "tile", 1)

    parent_new = pl.pallas_call(
        bound(parent_step, rows, chan),
        out_shape=shape(rows * chan, cols),
        in_specs=[SMEM] * 4 + [VMEM] * 4,
        out_specs=pl.BlockSpec(memory_space=pl.ANY),
        scratch_shapes=[
            pltpu.VMEM((blocks + 2, (rows + 2) * chan, LANES), F32),
            pltpu.VMEM((blocks, rows * chan, LANES), F32),
            pltpu.VMEM((3, 2, levels, 8, LANES), F32),
            pltpu.SemaphoreType.DMA((blocks,)),
        ],
        compiler_params=pltpu.CompilerParams(vmem_limit_bytes=16 << 20),
        cost_estimate=pl.CostEstimate(flops=30 * parent.size, bytes_accessed=8 * parent.size, transcendentals=0),
    )(*params, parent, parent_low, parent_high, strip)

    nest_new = pl.pallas_call(
        bound(nest_step, rows, chan, own_rows, tiles, rows * tiles),
        out_shape=shape(nest_rows * chan, nest_cols),
        in_specs=[SMEM] * 5 + [VMEM] * 5,
        out_specs=pl.BlockSpec(memory_space=pl.ANY),
        scratch_shapes=[
            pltpu.VMEM((col_blocks, ext_rows * chan, LANES), F32),
            pltpu.VMEM((3, (span + 1) * chan, LANES), F32),
            pltpu.VMEM((2, col_blocks, chan, 8, LANES), F32),
            pltpu.VMEM((2, col_blocks + 2, chan, ext_rows + 16, LANES), F32),
            pltpu.VMEM((2, col_blocks, chan, ext_rows, LANES), F32),
            pltpu.VMEM((3, col_blocks, ext_rows, LANES), F32),
            pltpu.VMEM((col_blocks, nest_rows * chan, LANES), F32),
            pltpu.VMEM((3, 2, levels, 8, LANES), F32),
            pltpu.SemaphoreType.DMA((col_blocks,)),
        ],
        compiler_params=pltpu.CompilerParams(vmem_limit_bytes=32 << 20),
        cost_estimate=pl.CostEstimate(flops=120 * nest.size, bytes_accessed=16 * nest.size, transcendentals=0),
    )(nest_box, *params, block, got, nest, nest_low, nest_high)

    return (
        parent_new.reshape(parent_old.shape),
        nest_new.reshape(nest_state.shape),
    )


def solution(mesh):
    placed = (P("tile", None, "sec"), P("sec", "tile", None, None), P(), P(), P(), P(), P())
    return jax.shard_map(
        body,
        mesh=mesh,
        in_specs=placed,
        out_specs=(P("tile", None, "sec"), P("sec", "tile", None, None)),
        check_vma=False,
    )
```

```python
import jax
import jax.numpy as jnp
from jax import lax
from jax.experimental import pallas as pl
from jax.experimental.pallas import tpu as pltpu
from jax.sharding import PartitionSpec as P

NSTEP = 4
RATIO = 4
LANES = 128
F32 = jnp.float32
VMEM = pl.BlockSpec(memory_space=pltpu.VMEM)
SMEM = pl.BlockSpec(memory_space=pltpu.SMEM)
ANY = pl.BlockSpec(memory_space=pl.ANY)


def call(kernel, outs, args, specs, scratch=(), limit=16, cost=0, out_specs=None, same=None):
    return pl.pallas_call(
        kernel,
        out_shape=list(outs),
        in_specs=list(specs),
        out_specs=[VMEM] * len(outs) if out_specs is None else out_specs,
        scratch_shapes=list(scratch),
        input_output_aliases=same or {},
        compiler_params=pltpu.CompilerParams(vmem_limit_bytes=limit << 20),
        cost_estimate=pl.CostEstimate(flops=0, bytes_accessed=cost, transcendentals=0),
    )(*args)


def shape(*dims, dtype=F32):
    return jax.ShapeDtypeStruct(dims, dtype)


def lane_ids():
    return lax.broadcasted_iota(jnp.int32, (8, LANES), 1)


def sublane_ids():
    return lax.broadcasted_iota(jnp.int32, (8, LANES), 0)


def one_if(condition):
    return jnp.where(condition, 1.0, 0.0).astype(F32)


def aligned(start, step):
    return pl.multiple_of(start, step)


def edge_rows(deep, chan, nest, parent, near, far, sems):
    odd = lax.rem(lax.axis_index("tile"), 2)
    cols = nest.shape[1]
    copies = []
    for k, (dest, last) in enumerate(((near, 1 - odd), (far, odd))):
        size = deep * chan
        at = aligned(last * (nest.shape[0] - size), 8)
        copies.append((nest.at[pl.ds(at, size), :], dest.at[pl.ds(0, size), :]))
        at = aligned(last * (parent.shape[0] - chan), 8)
        for part in range(parent.shape[1] // cols):
            source = parent.at[pl.ds(at, chan), pl.ds(part * cols, cols)]
            copies.append((source, dest.at[pl.ds(size + part * chan, chan), :]))
    made = [pltpu.make_async_copy(a, b, sems.at[i]) for i, (a, b) in enumerate(copies)]
    for copy in made:
        copy.start()
    for copy in made:
        copy.wait()


def extract(rows, chan, box, parent, keep, send, anchor):
    cols = parent.shape[1]
    blocks = cols // LANES
    groups = chan // 8
    sec = lax.axis_index("sec")
    half = lax.rem(sec, 2)
    lane = lane_ids()
    anchor[...] = jnp.full((8, LANES), box[sec, 0], jnp.int32)

    def at(row, g):
        return pl.ds(aligned(row * chan + 8 * g, 8), 8)

    lane_row = lax.div(lane, 2)
    together = 4

    def outer(step, packed):
        packed = list(packed)
        for k in range(together):
            row = step * together + k
            for g in range(groups):
                ends = jnp.where(
                    lane < LANES // 2,
                    parent[at(row, g), pl.ds(0, LANES)],
                    parent[at(row, g), pl.ds(cols - LANES, LANES)],
                )
                ends = pltpu.roll(ends, 2 * rows + 2 * row + 1, axis=1)
                packed[g] = jnp.where(lane_row == rows + row, ends, packed[g])
        return tuple(packed)

    zeros = (jnp.zeros((8, LANES), F32),) * groups
    halo = lax.fori_loop(0, rows // together, outer, zeros)

    for which, dest in ((1 - half, send), (half, keep)):

        @pl.loop(0, dest.shape[0])
        def _(i):
            nest = 2 * i + which
            offset = box[nest, 1] - sec * cols
            shift = lax.bitwise_and(offset, LANES - 1)
            back = lax.bitwise_and(LANES - shift, LANES - 1)

            def place(k):
                start = aligned(jnp.clip(k, 0, blocks - 1) * LANES, LANES)
                return pl.ds(start, LANES), one_if((k >= 0) & (k < blocks))

            first = lax.shift_right_arithmetic(offset, 7)
            at_a, on_a = place(first)
            at_b, on_b = place(first + 1)
            at_c, on_c = place(lax.shift_right_arithmetic(offset - 1, 7))
            before = lax.bitwise_and(lane - shift, LANES - 1) >= LANES // 2
            sent = jnp.where(lax.rem(lane, 2) == 0, one_if(nest == sec + 1), one_if(nest == sec - 1))

            def inner(step, packed):
                packed = list(packed)
                shifted = []
                for k in range(together):
                    row = step * together + k
                    turn = lax.bitwise_and(back + 2 * row + 1, LANES - 1)
                    for g in range(groups):
                        a = parent[at(row, g), at_a] * on_a
                        b = parent[at(row, g), at_b] * on_b
                        c = parent[at(row, g), at_c] * on_c
                        main = pltpu.roll(jnp.where(lane < shift, b, a), back, axis=1)
                        shifted.append((at(row, g), main))
                        side = pltpu.roll(jnp.where(before, c, b), turn, axis=1)
                        packed[g] = jnp.where(lane_row == row, side, packed[g])
                for where, main in shifted:
                    dest[i, where, :] = main
                return tuple(packed)

            packed = lax.fori_loop(0, rows // together, inner, tuple(h * sent for h in halo))
            for g in range(groups):
                dest[i, pl.ds(rows * chan + 8 * g, 8), :] = packed[g]


def combine(bit, own, got, keep, send):
    mine = lax.rem(lax.axis_index("sec") // bit, 2)
    for i in range(keep.shape[0]):
        send[i] = own[2 * i + 1 - mine] + got[2 * i + 1 - mine]
        keep[i] = own[2 * i + mine] + got[2 * i + mine]


def split(rows, chan, own, got, mine, to_sec, to_tile, to_both):
    sec = lax.div(lax.axis_index("sec"), lax.axis_size("sec") // 2)
    part = lax.rem(lax.div(lax.axis_index("tile"), 2), 2)
    size = rows // 2 * chan
    for dest, nest, half in (
        (to_sec, 1 - sec, part),
        (to_both, 1 - sec, 1 - part),
        (to_tile, sec, 1 - part),
        (mine, sec, part),
    ):
        at = pl.ds(aligned(half * size, 8), size)
        dest[pl.ds(0, size), :] = own[nest, at, :] + got[nest, at, :]
        at = pl.ds(rows * chan, chan)
        dest[pl.ds(size, chan), :] = own[nest, at, :] + got[nest, at, :]


def gathered(mine, from_sec, from_tile, from_both, out):
    out[0] = mine[...] + from_sec[...]
    out[1] = from_tile[...] + from_both[...]


def held_block(anchor, tile, rows, own_rows, group):
    first = lax.div(tile, group) * group
    low = jnp.maximum(anchor + (own_rows * first - 2), 0)
    base = lax.shift_right_arithmetic(low, rows.bit_length() - 1)
    return base + lax.bitwise_and(tile - base, group - 1)


def held(anchor, tile, rows, own_rows, group, tiles):
    if group == tiles:
        return jnp.full((8, LANES), tile, jnp.int32)
    return held_block(anchor, tile, rows, own_rows, group)


def choose(rows, own_rows, group, tiles, anchor, own, got, out):
    start = anchor[...]
    for k in range(2):
        tile = lax.bitwise_xor(lax.axis_index("tile"), 2 * k)
        keep = held(start, tile, rows, own_rows, 2 * group, tiles) == held_block(
            start, tile, rows, own_rows, group
        )
        for r in range(0, out.shape[1], 8):
            at = pl.ds(r, 8)
            out[k, at, :] = jnp.where(keep, own[k, at, :], got[k, at, :])


def wanted(anchor, row, tile, group, own_rows):
    first = lax.div(tile, group) * group
    low = anchor + (own_rows * first - 2)
    return (row >= low) & (row <= low + own_rows * group + 4)


def slot_rows(rows, own_rows, tiles, anchor):
    tile = lax.axis_index("tile")
    return [
        rows * held(anchor, lax.bitwise_xor(tile, 2 * k), rows, own_rows, 8, tiles) for k in range(2)
    ]


def select(rows, chan, own_rows, tiles, anchor, both, mine, sent):
    start = anchor[...]
    tile = lax.axis_index("tile")
    part = lax.rem(lax.div(tile, 2), 2)
    size = rows // 2 * chan
    base = slot_rows(rows, own_rows, tiles, start)
    lane_row = lax.div(lane_ids(), 2)
    for dest, owner in ((sent, lax.bitwise_xor(tile, 4)), (mine, tile)):
        for j in range(rows // 2 + 1):
            row = lane_row if j == rows // 2 else part * (rows // 2) + j
            second = wanted(start, base[1] + row, owner, 4, own_rows)
            for g in range(chan // 8):
                at = pl.ds(j * chan + 8 * g, 8)
                dest[at, :] = jnp.where(second, both[1, at, :], both[0, at, :])


def settle(rows, chan, own_rows, tiles, anchor, mine, got, near, nest, parent, out):
    start = anchor[...]
    tile = lax.axis_index("tile")
    part = lax.rem(lax.div(tile, 2), 2)
    base = slot_rows(rows, own_rows, tiles, start)
    lane_row = lax.div(lane_ids(), 2)
    for j in range(rows // 2 + 1):
        row = lane_row if j == rows // 2 else part * (rows // 2) + j
        keep = wanted(start, base[0] + row, tile, 4, own_rows)
        keep = keep | wanted(start, base[1] + row, tile, 4, own_rows)
        for g in range(chan // 8):
            at = pl.ds(j * chan + 8 * g, 8)
            out[at, :] = jnp.where(keep, mine[at, :], got[at, :])


def table_rows(chan, levels):
    return 4 * chan + 2 * levels + 6 * levels + 3


def make_table(diff, wind, conv, mix, table):
    chan, levels = diff.shape[0], conv.shape[1]

    def put(i, value):
        table[pl.ds(i, 1), :] = jnp.full((1, LANES), value, F32)

    for c in range(chan):
        d, wx, wy = diff[c], wind[0, c], wind[1, c]
        for k, value in enumerate((1.0 - 4.0 * d - wx - wy, d + wx, d + wy, d)):
            put(4 * c + k, value)
    base = 4 * chan
    for f in range(2):
        for l in range(levels):
            put(base + f * levels + l, conv[f, l])
    base += 2 * levels
    for f in range(3):
        m = jnp.full((1, LANES), mix[f], F32)
        ratio = None
        for l in range(levels):
            pivot = 1.0 + (1.0 if l in (0, levels - 1) else 2.0) * m
            if l:
                pivot = pivot - m * ratio
            inverse = 1.0 / pivot
            ratio = m * inverse
            table[pl.ds(base + 2 * (f * levels + l), 1), :] = inverse
            table[pl.ds(base + 2 * (f * levels + l) + 1, 1), :] = ratio
        put(base + 6 * levels + f, mix[f])


def rows_of(table):
    def coef(i):
        return jnp.broadcast_to(table[pl.ds(i, 1), :], (8, LANES))

    return coef


def step_blocks(chan, table, loads, stores):
    coef = rows_of(table)

    def horizontal(c):
        center, above, left, spread = (coef(4 * c + k) for k in range(4))
        out = []
        for load in loads:
            v, n, s, w, e = load(c)
            out.append(center * v + above * n + left * w + spread * (s + e))
        return out

    mix_blocks(chan, table, horizontal, stores)


def mix_blocks(chan, table, fields, stores):
    levels = chan // 3
    count = len(stores)
    coef = rows_of(table)
    conv = 4 * chan
    solve = conv + 2 * levels
    passed = None
    for f in range(3):
        ys, carry = [], []
        for l in range(levels):
            c = f * levels + l
            given = fields(c)
            rate = coef(conv + f * levels + l) if f < 2 else None
            ratio = coef(solve + 2 * (c - 1) + 1) if l else None
            row, moved = [], []
            for b in range(count):
                h = given[b]
                if passed is not None:
                    h = h + passed[l][b]
                if f < 2:
                    moved.append(rate * h)
                    h = h - moved[b]
                if l:
                    h = h + ratio * ys[-1][b]
                row.append(h)
            ys.append(row)
            carry.append(moved)
        passed = carry
        m = coef(solve + 6 * levels + f)
        x = [None] * count
        for l in range(levels - 1, -1, -1):
            c = f * levels + l
            inverse = coef(solve + 2 * c)
            for b in range(count):
                x[b] = inverse * (ys[l][b] if x[b] is None else ys[l][b] + m * x[b])
                stores[b](c, x[b])


def sides(lane, west, v, east):
    w = pltpu.roll(jnp.where(lane == LANES - 1, west, v), 1, axis=1)
    e = pltpu.roll(jnp.where(lane == 0, east, v), LANES - 1, axis=1)
    return w, e


def parent_step(rows, chan, table, parent, strip, out, edges, ext, done, sems):
    blocks = parent.shape[1] // LANES
    groups = chan // 8
    lane = lane_ids()
    packed_at = strip.shape[1] - chan

    def columns(j):
        return pl.ds(aligned(j * LANES, LANES), LANES)

    packed = [strip[0, pl.ds(packed_at + 8 * g, 8), :] for g in range(groups)]

    @pl.loop(0, rows)
    def _(row):
        for g in range(groups):
            at = pl.ds(aligned((row + 1) * chan + 8 * g, 8), 8)
            turn = LANES - 1 - 2 * rows - 2 * row
            turned = pltpu.roll(packed[g], turn, axis=1)
            ext[0, at, :] = turned
            ext[blocks + 1, at, :] = turned

    @pl.loop(0, blocks)
    def _(j):
        ext[j + 1, pl.ds(chan, rows * chan), :] = parent[:, columns(j)]
        ext[j + 1, pl.ds(0, chan), :] = jnp.zeros((chan, LANES), F32)
        ext[j + 1, pl.ds((rows + 1) * chan, chan), :] = jnp.zeros((chan, LANES), F32)

    @pl.loop(0, blocks)
    def _(j):
        def block(first):
            def loads(c):
                def at(r):
                    return pl.ds((first + r) * chan + c, 8, stride=chan)

                v = ext[j + 1, at(1), :]
                w, e = sides(lane, ext[j, at(1), :], v, ext[j + 2, at(1), :])
                return v, ext[j + 1, at(0), :], ext[j + 1, at(2), :], w, e

            def store(c, x):
                done[j, pl.ds(first * chan + c, 8, stride=chan), :] = x

            return loads, store

        loads, stores = zip(*(block(first) for first in range(0, rows, 8)))
        step_blocks(chan, table, loads, stores)
        at = pl.ds(aligned(j * chan, 8), chan)
        edges[0, at, :] = done[j, pl.ds(0, chan), :]
        edges[1, at, :] = done[j, pl.ds((rows - 1) * chan, chan), :]
        pltpu.make_async_copy(done.at[j], out.at[:, columns(j)], sems.at[j]).start()

    @pl.loop(0, blocks)
    def _(j):
        pltpu.make_async_copy(done.at[j], out.at[:, columns(j)], sems.at[j]).wait()


def parent_edges(rows, chan, deep, table, near, far, edges, given, out, beside, done, sems):
    blocks = edges.shape[1] // chan
    per = near.shape[1] // LANES
    odd = lax.rem(lax.axis_index("tile"), 2) == 1
    for j in range(blocks):
        for g in range(chan // 8):
            at = pl.ds((deep + j // per) * chan + 8 * g, 8)
            a, b = (ref[at, pl.ds(j % per * LANES, LANES)] for ref in (near, far))
            at = pl.ds(j * chan + 8 * g, 8)
            beside[0, at, :] = jnp.where(odd, a, b)
            beside[1, at, :] = jnp.where(odd, b, a)
    coef = rows_of(table)
    pieces = [(k, b) for k in range(2) for b in range(0, blocks, 8)]

    def at(b, c):
        return pl.ds(b * chan + c, 8, stride=chan)

    def fields(c):
        return [coef(4 * c + (1, 3)[k]) * beside[k, at(b, c), :] for k, b in pieces]

    def storing(k, b):
        def store(c, x):
            done[k, at(b, c), :] = edges[k, at(b, c), :] + x

        return store

    mix_blocks(chan, table, fields, [storing(k, b) for k, b in pieces])
    copies = []
    for k, row in enumerate((0, rows - 1)):
        for j in range(blocks):
            copies.append(
                pltpu.make_async_copy(
                    done.at[k, pl.ds(j * chan, chan), :],
                    out.at[pl.ds(row * chan, chan), pl.ds(j * LANES, LANES)],
                    sems.at[k * blocks + j],
                )
            )
    for copy in copies:
        copy.start()
    for copy in copies:
        copy.wait()


def dealing(cols, back):
    first = lax.broadcasted_iota(jnp.int32, (cols, cols), 0)
    second = lax.broadcasted_iota(jnp.int32, (cols, cols), 1)
    planes = cols // LANES
    natural, dealt = (second, first) if back else (first, second)
    hit = natural == planes * lax.bitwise_and(dealt, LANES - 1) + lax.shift_right_arithmetic(dealt, 7)
    return jnp.where(hit, 1.0, 0.0).astype(jnp.bfloat16)


def dealt(x, matrix):
    out = None
    for _ in range(3):
        part = x.astype(jnp.bfloat16)
        x = x - part.astype(F32)
        term = jnp.dot(part, matrix, preferred_element_type=F32)
        out = term if out is None else out + term
    return out


def plane_blocks(chan, table, planes, lane, load, store):
    cache = {}

    def center(k, c):
        if (k, c) not in cache:
            cache[k, c] = load(0, k, c)
        return cache[k, c]

    def block(k):
        def loads(c):
            if k == 0:
                w = jnp.where(lane == 0, 0.0, pltpu.roll(center(planes - 1, c), 1, axis=1))
            else:
                w = center(k - 1, c)
            if k == planes - 1:
                e = jnp.where(lane == LANES - 1, 0.0, pltpu.roll(center(0, c), LANES - 1, axis=1))
            else:
                e = center(k + 1, c)
            return center(k, c), load(-1, k, c), load(1, k, c), w, e

        def put(c, x):
            store(k, c, x)

        return loads, put

    loads, stores = zip(*(block(k) for k in range(planes)))
    step_blocks(chan, table, loads, stores)


def nest_first(chan, deep, box, table, nest, moved, nudge, back, matrix, ext):
    nest_rows = nest.shape[0] // chan
    planes = nest.shape[1] // LANES
    ext_rows = nest_rows + 2 * deep
    groups = chan // 8
    sec, tile = lax.axis_index("sec"), lax.axis_index("tile")
    extent_x, extent_y = box[sec, 2], box[sec, 3]
    lane, sub = lane_ids(), sublane_ids()
    first_row = nest_rows * tile - deep
    matrix[...] = dealing(nest.shape[1], False)
    back[...] = dealing(nest.shape[1], True)
    for k in range(planes):
        col = planes * lane + k
        for rb in range(0, ext_rows, 8):
            i = first_row + rb + sub
            live = one_if((i >= 0) & (i < extent_x) & (col < extent_y))
            dist = jnp.minimum(jnp.minimum(i, col), jnp.minimum(extent_x - 1 - i, extent_y - 1 - col))
            dist = jnp.maximum(dist, 0).astype(F32)
            rate = 0.1 + 0.4 * jnp.exp(-dist / 3.0)
            nudge[0, k, pl.ds(rb, 8), :] = live * (1.0 - rate)
            nudge[1, k, pl.ds(rb, 8), :] = live * rate
            nudge[2, k, pl.ds(rb, 8), :] = live

    together = 4

    @pl.loop(0, nest_rows // together)
    def _(step):
        size = together * chan
        x = dealt(nest[pl.ds(aligned(step * size, 8), size), :], matrix[...])
        for r in range(together):
            row = step * together + r
            for k in range(planes):
                live = jnp.broadcast_to(nudge[2, k, pl.ds(deep + row, 1), :], (8, LANES))
                for g in range(groups):
                    piece = x[r * chan + 8 * g : r * chan + 8 * g + 8, k * LANES : (k + 1) * LANES]
                    ext[k, pl.ds(aligned((row + 1) * chan + 8 * g, 8), 8), :] = piece * live

    for row in (0, nest_rows + 1):
        ext[:, pl.ds(row * chan, chan), :] = jnp.zeros((planes, chan, LANES), F32)
    for rb in range(0, nest_rows, 8):

        def load(shift, k, c):
            return ext[k, pl.ds((rb + 1 + shift) * chan + c, 8, stride=chan), :]

        def store(k, c, x):
            at = pl.ds(deep + rb, 8)
            moved[k, c, at, :] = x * nudge[0, k, at, :]

        plane_blocks(chan, table, planes, lane, load, store)


def nest_edges(chan, deep, table, nest, near, far, nudge, given, moved, matrix, natural, ext):
    nest_rows = nest.shape[0] // chan
    planes = nest.shape[1] // LANES
    ext_rows = nest_rows + 2 * deep
    size = deep * chan
    lane, sub = lane_ids(), sublane_ids()
    odd = lax.rem(lax.axis_index("tile"), 2) == 1
    matrix[...] = dealing(nest.shape[1], False)
    edge = (deep + 2) * chan
    a, b = near[pl.ds(0, size), :], far[pl.ds(0, size), :]
    natural[pl.ds(0, size), :] = jnp.where(odd, a, b)
    natural[pl.ds(size, 2 * chan), :] = nest[pl.ds(0, 2 * chan), :]
    natural[pl.ds(edge, 2 * chan), :] = nest[pl.ds((nest_rows - 2) * chan, 2 * chan), :]
    natural[pl.ds(edge + 2 * chan, size), :] = jnp.where(odd, b, a)
    for half in range(2):

        def rows_at(r):
            return r if half == 0 else ext_rows - deep - 2 + r

        x = dealt(natural[pl.ds(half * edge, edge), :], matrix[...])
        for r in range(deep + 2):
            for k in range(planes):
                live = jnp.broadcast_to(nudge[2, k, pl.ds(rows_at(r), 1), :], (8, LANES))
                for g in range(chan // 8):
                    piece = x[r * chan + 8 * g : r * chan + 8 * g + 8, k * LANES : (k + 1) * LANES]
                    ext[k, pl.ds(half * edge + r * chan + 8 * g, 8), :] = piece * live

    def load(shift, k, c):
        upper = ext[k, pl.ds((1 + shift) * chan + c, 8, stride=chan), :]
        lower = ext[k, pl.ds((3 + shift) * chan + c, 8, stride=chan), :]
        return jnp.where(sub < deep, upper, lower)

    def store(k, c, x):
        low, high = pl.ds(1, deep), pl.ds(ext_rows - 1 - deep, deep)
        moved[k, c, low, :] = x[:deep] * nudge[0, k, low, :]
        moved[k, c, high, :] = x[deep:] * nudge[0, k, high, :]

    plane_blocks(chan, table, planes, lane, load, store)


def nest_rest(
    rows, chan, deep, own_rows, tiles,
    anchor, table, own, got_a, got_b, got_c, moved, nudge, back, out,
    slots, foot, coarse, state, force, done, final, sems,
):
    planes, _, ext_rows, _ = moved.shape
    nest_rows = ext_rows - 2 * deep
    groups = chan // 8
    tile = lax.axis_index("tile")
    lane, sub = lane_ids(), sublane_ids()
    first_row = nest_rows * tile - deep
    start = jnp.max(anchor[...]) + own_rows * tile - 2
    span = foot.shape[1] // chan - 1
    size = rows // 2 * chan
    part = lax.rem(lax.div(tile, 2), 2)
    side = lax.rem(tile, 2)

    for k, ref in enumerate((own, got_a, got_b, got_c)):
        slots[k] = ref[...]

    for m in range(span):
        row = start + m
        local = lax.bitwise_and(row, rows - 1)
        upper = lax.div(local, rows // 2)
        other = lax.bitwise_and(lax.shift_right_arithmetic(row, rows.bit_length() - 1), 1)
        k = 2 * lax.bitwise_xor(upper, part) + lax.bitwise_xor(other, side)
        inside = one_if((row >= 0) & (row < rows * tiles))
        slot = (local - upper * (rows // 2)) * chan
        turn = LANES - 1 - 2 * local
        for g in range(groups):
            at = pl.ds(m * chan + 8 * g, 8)
            foot[0, at, :] = pltpu.roll(slots[k, pl.ds(size + 8 * g, 8), :] * inside, turn, axis=1)
            foot[1, at, :] = slots[k, pl.ds(aligned(slot + 8 * g, 8), 8), :] * inside

    for k in range(2):
        foot[k, pl.ds(span * chan, chan), :] = jnp.zeros((chan, LANES), F32)

    def foot_loads(c):
        def at(r):
            return pl.ds(r * chan + c, 8, stride=chan)

        v = foot[1, at(1), :]
        edge = foot[0, at(1), :]
        w, e = sides(lane, edge, v, edge)
        return v, foot[1, at(0), :], foot[1, at(2), :], w, e

    def foot_store(c, x):
        old = foot[1, pl.ds(chan + c, 8, stride=chan), :]
        coarse[0, c] = old
        coarse[1, c] = x - old

    step_blocks(chan, table, [foot_loads], [foot_store])

    share = []
    for rb in range(0, ext_rows, 8):
        p = lax.rem(sub, RATIO).astype(F32) / RATIO
        share.append(jnp.where(first_row + rb + sub >= RATIO * (own_rows * tiles - 1), 0.0, p))

    @pl.loop(0, chan)
    def _(c):
        for rb in range(0, ext_rows, 8):
            u = rb // RATIO
            at = pl.ds(rb, 8)
            lines = []
            for t in range(2):
                r0, r1, r2 = (
                    jnp.broadcast_to(coarse[t, c, pl.ds(u + i, 1), :], (8, LANES)) for i in range(3)
                )
                a0 = jnp.where(sub < RATIO, r0, r1)
                a1 = jnp.where(sub < RATIO, r1, r2)
                line = a0 + share[rb // 8] * (a1 - a0)
                beside = jnp.where(lane == LANES - 1, line, pltpu.roll(line, LANES - 1, axis=1))
                lines.append((line, (beside - line) * (1.0 / RATIO)))
            for k in range(planes):
                b = nudge[1, k, at, :]
                old, new = (b * (line + float(k) * slope if k else line) for line, slope in lines)
                force[0, k, c, at, :] = old
                force[1, k, c, at, :] = new
                state[0, k, c, pl.ds(8 + rb, 8), :] = moved[k, c, at, :] + (old + new * (1.0 / NSTEP))

    def advance(step, src, rb, put):
        weight = jnp.float32(step + 1) / NSTEP

        def load(shift, k, c):
            return state[src, k, c, pl.ds(8 + rb + shift, 8), :]

        def store(k, c, x):
            at = pl.ds(rb, 8)
            g = force[0, k, c, at, :] + weight * force[1, k, c, at, :]
            put(k, c, nudge[0, k, at, :] * x + g)

        plane_blocks(chan, table, planes, lane, load, store)

    @pl.loop(1, NSTEP - 1)
    def _(step):
        src = lax.rem(step + 1, 2)

        @pl.loop(0, ext_rows // 8)
        def _(block):
            rb = aligned(block * 8, 8)

            def put(k, c, x):
                state[1 - src, k, c, pl.ds(8 + rb, 8), :] = x

            advance(step, src, rb, put)

    copies = []
    for n, rb in enumerate(range(0, nest_rows, 8)):

        def put(k, c, x):
            done[n, k, pl.ds(c, 8, stride=chan), :] = x

        advance(NSTEP - 1, NSTEP % 2, deep + rb, put)
        whole = jnp.concatenate([done[n, k] for k in range(planes)], axis=1)
        final[n] = dealt(whole, back[...])
        copies.append(
            pltpu.make_async_copy(final.at[n], out.at[pl.ds(rb * chan, 8 * chan), :], sems.at[n])
        )
        copies[n].start()
    for copy in copies:
        copy.wait()


def bound(kernel, *static):
    def run(*refs):
        return kernel(*static, *refs)

    return run


def exchange(block, axis, bit):
    return lax.ppermute(block, axis, [(i, i ^ bit) for i in range(lax.axis_size(axis))])


def exchange_both(block, sec_bit, tile_bit):
    secs, tiles = lax.axis_size("sec"), lax.axis_size("tile")
    route = [
        (s * tiles + t, (s ^ sec_bit) * tiles + (t ^ tile_bit)) for s in range(secs) for t in range(tiles)
    ]
    return lax.ppermute(block, ("sec", "tile"), route)


def body(parent_old, nest_state, diffusion, wind_speed, conversion, vert_mix, nest_box):
    rows, chan, cols = parent_old.shape
    nest_rows, nest_cols = nest_state.shape[1], nest_state.shape[3]
    secs, tiles = lax.axis_size("sec"), lax.axis_size("tile")
    own_rows = nest_rows // RATIO
    levels = conversion.shape[1]
    deep = NSTEP
    ext_rows = nest_rows + 2 * deep
    col_blocks = nest_cols // LANES
    blocks = cols // LANES
    span = (ext_rows // RATIO + 1) + 2
    strip_rows = (rows + 1) * chan
    half_rows = (rows // 2 + 1) * chan
    parent = parent_old.reshape(rows * chan, cols)
    nest = nest_state.reshape(nest_rows * chan, nest_cols)
    half = shape(half_rows, LANES)

    halo = shape((deep + cols // nest_cols) * chan, nest_cols)
    near, far = call(
        bound(edge_rows, deep, chan), [halo] * 2, (nest, parent), (ANY, ANY),
        scratch=[pltpu.SemaphoreType.DMA((2 * (1 + cols // nest_cols),))], limit=4, cost=1 << 20,
    )
    near = exchange(near, "tile", 1)
    beside = [(i, i + 1) for i in range(1, tiles - 1, 2)]
    far = lax.ppermute(far, "tile", beside + [(j, i) for i, j in beside])

    (table,) = call(
        make_table, [shape(table_rows(chan, levels), LANES)],
        (diffusion, wind_speed, conversion, vert_mix), (SMEM,) * 4, limit=2, cost=1 << 20,
    )

    some = shape(secs // 2, strip_rows, LANES)
    keep, send, anchor = call(
        bound(extract, rows, chan), [some, some, shape(8, LANES, dtype=jnp.int32)],
        (nest_box, parent), (SMEM, VMEM), cost=4 << 20,
    )
    got = exchange(send, "sec", 1)
    bit = 2
    while bit < secs // 2:
        some = shape(secs // (2 * bit), strip_rows, LANES)
        keep, send = call(bound(combine, bit), [some, some], (keep, got), (VMEM, VMEM), cost=1 << 20)
        got = exchange(send, "sec", bit)
        bit *= 2
    mine, to_sec, to_tile, to_both = call(
        bound(split, rows, chan), [half] * 4, (keep, got), (VMEM, VMEM), cost=1 << 18,
    )
    from_sec = exchange_both(to_sec, secs // 2, 0)
    from_tile = exchange_both(to_tile, 0, 2)
    from_both = exchange_both(to_both, secs // 2, 2)
    two = shape(2, half_rows, LANES)
    (strip,) = call(
        gathered, [two], (mine, from_sec, from_tile, from_both), (VMEM,) * 4, cost=1 << 18,
    )
    pair = strip
    group = tiles // 2
    while group > 4:
        got = exchange(pair, "tile", group)
        (pair,) = call(
            bound(choose, rows, own_rows, group, tiles), [two], (anchor, pair, got), (VMEM,) * 3, cost=1 << 18,
        )
        group //= 2
    mine, sent = call(
        bound(select, rows, chan, own_rows, tiles), [half] * 2, (anchor, pair), (VMEM,) * 2, cost=1 << 18,
    )
    got = exchange(sent, "tile", 4)
    edge = shape(2, blocks * chan, LANES)
    parent_new, edges = call(
        bound(parent_step, rows, chan), [shape(rows * chan, cols), edge],
        (table, parent, strip), (VMEM,) * 3, cost=8 << 20, out_specs=[ANY, VMEM],
        scratch=[
            pltpu.VMEM((blocks + 2, (rows + 2) * chan, LANES), F32),
            pltpu.VMEM((blocks, rows * chan, LANES), F32),
            pltpu.SemaphoreType.DMA((blocks,)),
        ],
    )

    moved_shape = shape(col_blocks, chan, ext_rows, LANES)
    square = (nest_cols, nest_cols)
    moved, nudge, back = call(
        bound(nest_first, chan, deep),
        [moved_shape, shape(3, col_blocks, ext_rows, LANES), shape(*square, dtype=jnp.bfloat16)],
        (nest_box, table, nest), (SMEM, VMEM, VMEM), cost=6 << 20,
        scratch=[
            pltpu.VMEM(square, jnp.bfloat16),
            pltpu.VMEM((col_blocks, (nest_rows + 2) * chan, LANES), F32),
        ],
    )

    (own,) = call(
        bound(settle, rows, chan, own_rows, tiles), [half], (anchor, mine, got, near, moved, edges), (VMEM,) * 6, cost=1 << 18,
    )
    got_a, got_b, got_c = (exchange(own, "tile", k) for k in (1, 2, 3))

    (parent_new,) = call(
        bound(parent_edges, rows, chan, deep), [shape(rows * chan, cols)],
        (table, near, far, edges, parent_new), (VMEM,) * 4 + (ANY,), cost=1 << 20, out_specs=[ANY], same={4: 0},
        scratch=[
            pltpu.VMEM((2, blocks * chan, LANES), F32),
            pltpu.VMEM((2, blocks * chan, LANES), F32),
            pltpu.SemaphoreType.DMA((2 * blocks,)),
        ],
    )
    (moved,) = call(
        bound(nest_edges, chan, deep), [moved_shape],
        (table, nest, near, far, nudge, moved), (VMEM,) * 6, cost=3 << 20, same={5: 0},
        scratch=[
            pltpu.VMEM(square, jnp.bfloat16),
            pltpu.VMEM((2 * (deep + 2) * chan, nest_cols), F32),
            pltpu.VMEM((col_blocks, 2 * (deep + 2) * chan, LANES), F32),
        ],
    )

    (nest_new,) = call(
        bound(nest_rest, rows, chan, deep, own_rows, tiles), [shape(nest_rows * chan, nest_cols)],
        (anchor, table, own, got_a, got_b, got_c, moved, nudge, back), (VMEM,) * 9, cost=16 << 20, out_specs=[ANY],
        limit=32,
        scratch=[
            pltpu.VMEM((4, half_rows, LANES), F32),
            pltpu.VMEM((2, (span + 1) * chan, LANES), F32),
            pltpu.VMEM((2, chan, 8, LANES), F32),
            pltpu.VMEM((2, col_blocks, chan, ext_rows + 16, LANES), F32),
            pltpu.VMEM((2, col_blocks, chan, ext_rows, LANES), F32),
            pltpu.VMEM((nest_rows // 8, col_blocks, 8 * chan, LANES), F32),
            pltpu.VMEM((nest_rows // 8, 8 * chan, nest_cols), F32),
            pltpu.SemaphoreType.DMA((nest_rows // 8,)),
        ],
    )

    return parent_new.reshape(parent_old.shape), nest_new.reshape(nest_state.shape)


def solution(mesh):
    placed = (P("tile", None, "sec"), P("sec", "tile", None, None), P(), P(), P(), P(), P())
    return jax.shard_map(
        body,
        mesh=mesh,
        in_specs=placed,
        out_specs=(P("tile", None, "sec"), P("sec", "tile", None, None)),
        check_vma=False,
    )
```

```python
import jax
import jax.numpy as jnp
from jax import lax
from jax.experimental import pallas as pl
from jax.experimental.pallas import tpu as pltpu
from jax.sharding import PartitionSpec as P

NSTEP = 4
RATIO = 4
LANES = 128
F32 = jnp.float32
VMEM = pl.BlockSpec(memory_space=pltpu.VMEM)
SMEM = pl.BlockSpec(memory_space=pltpu.SMEM)
ANY = pl.BlockSpec(memory_space=pl.ANY)
HBM = pl.BlockSpec(memory_space=pltpu.HBM)
TOGETHER = 8


def call(kernel, outs, args, specs, scratch=(), limit=16, cost=0, out_specs=None, same=None):
    return pl.pallas_call(
        kernel,
        out_shape=list(outs),
        in_specs=list(specs),
        out_specs=[VMEM] * len(outs) if out_specs is None else out_specs,
        scratch_shapes=list(scratch),
        input_output_aliases=same or {},
        compiler_params=pltpu.CompilerParams(vmem_limit_bytes=limit << 20),
        cost_estimate=pl.CostEstimate(flops=0, bytes_accessed=cost, transcendentals=0),
    )(*args)


def shape(*dims, dtype=F32):
    return jax.ShapeDtypeStruct(dims, dtype)


def lane_ids():
    return lax.broadcasted_iota(jnp.int32, (8, LANES), 1)


def sublane_ids():
    return lax.broadcasted_iota(jnp.int32, (8, LANES), 0)


def one_if(condition):
    return jnp.where(condition, 1.0, 0.0).astype(F32)


def aligned(start, step):
    return pl.multiple_of(start, step)


def edge_rows(deep, chan, nest, parent, near, far, sems):
    odd = lax.rem(lax.axis_index("tile"), 2)
    cols = nest.shape[1]
    copies = []
    for k, (dest, last) in enumerate(((near, 1 - odd), (far, odd))):
        size = deep * chan
        at = aligned(last * (nest.shape[0] - size), 8)
        copies.append((nest.at[pl.ds(at, size), :], dest.at[pl.ds(0, size), :]))
        at = aligned(last * (parent.shape[0] - chan), 8)
        for part in range(parent.shape[1] // cols):
            source = parent.at[pl.ds(at, chan), pl.ds(part * cols, cols)]
            copies.append((source, dest.at[pl.ds(size + part * chan, chan), :]))
    made = [pltpu.make_async_copy(a, b, sems.at[i]) for i, (a, b) in enumerate(copies)]
    for copy in made:
        copy.start()
    for copy in made:
        copy.wait()


def extract(rows, chan, box_in, parent_in, keep, send, anchor, box, parent, sems):
    copies = [
        pltpu.make_async_copy(box_in, box, sems.at[0]),
        pltpu.make_async_copy(parent_in, parent, sems.at[1]),
    ]
    for copy in copies:
        copy.start()
    for copy in copies:
        copy.wait()
    cols = parent.shape[1]
    blocks = cols // LANES
    groups = chan // 8
    sec = lax.axis_index("sec")
    half = lax.rem(sec, 2)
    lane = lane_ids()
    anchor[...] = jnp.full((8, LANES), box[sec, 0], jnp.int32)

    def at(row, g):
        return pl.ds(aligned(row * chan + 8 * g, 8), 8)

    lane_row = lax.div(lane, 2)
    together = TOGETHER

    def outer(step, packed):
        packed = list(packed)
        for k in range(together):
            row = step * together + k
            for g in range(groups):
                ends = jnp.where(
                    lane < LANES // 2,
                    parent[at(row, g), pl.ds(0, LANES)],
                    parent[at(row, g), pl.ds(cols - LANES, LANES)],
                )
                ends = pltpu.roll(ends, 2 * rows + 2 * row + 1, axis=1)
                packed[g] = jnp.where(lane_row == rows + row, ends, packed[g])
        return tuple(packed)

    zeros = (jnp.zeros((8, LANES), F32),) * groups
    halo = lax.fori_loop(0, rows // together, outer, zeros)

    for which, dest in ((1 - half, send), (half, keep)):

        @pl.loop(0, dest.shape[0])
        def _(i):
            nest = 2 * i + which
            offset = box[nest, 1] - sec * cols
            shift = lax.bitwise_and(offset, LANES - 1)
            back = lax.bitwise_and(LANES - shift, LANES - 1)

            def place(k):
                start = aligned(jnp.clip(k, 0, blocks - 1) * LANES, LANES)
                return pl.ds(start, LANES), one_if((k >= 0) & (k < blocks))

            first = lax.shift_right_arithmetic(offset, 7)
            at_a, on_a = place(first)
            at_b, on_b = place(first + 1)
            at_c, on_c = place(lax.shift_right_arithmetic(offset - 1, 7))
            before = lax.bitwise_and(lane - shift, LANES - 1) >= LANES // 2
            sent = jnp.where(lax.rem(lane, 2) == 0, one_if(nest == sec + 1), one_if(nest == sec - 1))

            def inner(step, packed):
                packed = list(packed)
                shifted = []
                for k in range(together):
                    row = step * together + k
                    turn = lax.bitwise_and(back + 2 * row + 1, LANES - 1)
                    for g in range(groups):
                        a = parent[at(row, g), at_a] * on_a
                        b = parent[at(row, g), at_b] * on_b
                        c = parent[at(row, g), at_c] * on_c
                        main = pltpu.roll(jnp.where(lane < shift, b, a), back, axis=1)
                        shifted.append((at(row, g), main))
                        side = pltpu.roll(jnp.where(before, c, b), turn, axis=1)
                        packed[g] = jnp.where(lane_row == row, side, packed[g])
                for where, main in shifted:
                    dest[i, where, :] = main
                return tuple(packed)

            here = (offset >= -LANES) & (offset <= cols)

            @pl.when(here)
            def _():
                packed = lax.fori_loop(0, rows // together, inner, tuple(h * sent for h in halo))
                for g in range(groups):
                    dest[i, pl.ds(rows * chan + 8 * g, 8), :] = packed[g]

            @pl.when(jnp.logical_not(here))
            def _():
                dest[i, pl.ds(0, rows * chan), :] = jnp.zeros((rows * chan, LANES), F32)
                for g in range(groups):
                    dest[i, pl.ds(rows * chan + 8 * g, 8), :] = halo[g] * sent


def combine(bit, own, got, keep, send):
    mine = lax.rem(lax.axis_index("sec") // bit, 2)
    for i in range(keep.shape[0]):
        send[i] = own[2 * i + 1 - mine] + got[2 * i + 1 - mine]
        keep[i] = own[2 * i + mine] + got[2 * i + mine]


def split(rows, chan, own, got, mine, to_sec, to_tile, to_both):
    sec = lax.div(lax.axis_index("sec"), lax.axis_size("sec") // 2)
    part = lax.rem(lax.div(lax.axis_index("tile"), 2), 2)
    size = rows // 2 * chan
    for dest, nest, half in (
        (to_sec, 1 - sec, part),
        (to_both, 1 - sec, 1 - part),
        (to_tile, sec, 1 - part),
        (mine, sec, part),
    ):
        at = pl.ds(aligned(half * size, 8), size)
        dest[pl.ds(0, size), :] = own[nest, at, :] + got[nest, at, :]
        at = pl.ds(rows * chan, chan)
        dest[pl.ds(size, chan), :] = own[nest, at, :] + got[nest, at, :]


def gathered(mine, from_sec, from_tile, from_both, moved, out):
    out[0] = mine[...] + from_sec[...]
    out[1] = from_tile[...] + from_both[...]


def held_block(anchor, tile, rows, own_rows, group):
    first = lax.div(tile, group) * group
    low = jnp.maximum(anchor + (own_rows * first - 2), 0)
    base = lax.shift_right_arithmetic(low, rows.bit_length() - 1)
    return base + lax.bitwise_and(tile - base, group - 1)


def held(anchor, tile, rows, own_rows, group, tiles):
    if group == tiles:
        return jnp.full((8, LANES), tile, jnp.int32)
    return held_block(anchor, tile, rows, own_rows, group)


def choose(rows, own_rows, group, tiles, anchor, own, got, out):
    start = anchor[...]
    for k in range(2):
        tile = lax.bitwise_xor(lax.axis_index("tile"), 2 * k)
        keep = held(start, tile, rows, own_rows, 2 * group, tiles) == held_block(
            start, tile, rows, own_rows, group
        )
        for r in range(0, out.shape[1], 8):
            at = pl.ds(r, 8)
            out[k, at, :] = jnp.where(keep, own[k, at, :], got[k, at, :])


def wanted(anchor, row, tile, group, own_rows):
    first = lax.div(tile, group) * group
    low = anchor + (own_rows * first - 2)
    return (row >= low) & (row <= low + own_rows * group + 4)


def slot_rows(rows, own_rows, tiles, anchor):
    tile = lax.axis_index("tile")
    return [
        rows * held(anchor, lax.bitwise_xor(tile, 2 * k), rows, own_rows, 8, tiles) for k in range(2)
    ]


def select(rows, chan, own_rows, tiles, anchor, both, mine, sent):
    start = anchor[...]
    tile = lax.axis_index("tile")
    part = lax.rem(lax.div(tile, 2), 2)
    size = rows // 2 * chan
    base = slot_rows(rows, own_rows, tiles, start)
    lane_row = lax.div(lane_ids(), 2)
    for dest, owner in ((sent, lax.bitwise_xor(tile, 4)), (mine, tile)):
        for j in range(rows // 2 + 1):
            row = lane_row if j == rows // 2 else part * (rows // 2) + j
            second = wanted(start, base[1] + row, owner, 4, own_rows)
            for g in range(chan // 8):
                at = pl.ds(j * chan + 8 * g, 8)
                dest[at, :] = jnp.where(second, both[1, at, :], both[0, at, :])


def settle(rows, chan, own_rows, tiles, anchor, mine, got, near, parent, out):
    start = anchor[...]
    tile = lax.axis_index("tile")
    part = lax.rem(lax.div(tile, 2), 2)
    base = slot_rows(rows, own_rows, tiles, start)
    lane_row = lax.div(lane_ids(), 2)
    for j in range(rows // 2 + 1):
        row = lane_row if j == rows // 2 else part * (rows // 2) + j
        keep = wanted(start, base[0] + row, tile, 4, own_rows)
        keep = keep | wanted(start, base[1] + row, tile, 4, own_rows)
        for g in range(chan // 8):
            at = pl.ds(j * chan + 8 * g, 8)
            out[at, :] = jnp.where(keep, mine[at, :], got[at, :])


def table_rows(chan, levels):
    return 4 * chan + 2 * levels + chan


def make_table(diff, wind, conv, mix, table):
    chan, levels = diff.shape[0], conv.shape[1]

    def line(value):
        return jnp.full((1, LANES), value, F32)

    def put(i, value):
        table[pl.ds(i, 1), :] = value

    scale = {}
    for f in range(3):
        m = line(mix[f])
        ratio = None
        for l in range(levels):
            c = f * levels + l
            pivot = 1.0 + (1.0 if l in (0, levels - 1) else 2.0) * m
            if l:
                pivot = pivot - m * ratio
            inverse = 1.0 / pivot
            ratio = m * inverse
            put(4 * chan + 2 * levels + c, ratio)
            scale[c] = inverse * (1.0 - line(conv[f, l])) if f < 2 else inverse
            d, wx, wy = diff[c], wind[0, c], wind[1, c]
            for k, value in enumerate((1.0 - 4.0 * d - wx - wy, d + wx, d + wy, d)):
                put(4 * c + k, scale[c] * line(value))
            if f:
                before = c - levels
                put(4 * chan + before, scale[c] * line(conv[f - 1, l]) / scale[before])


def rows_of(table):
    def coef(i):
        return jnp.broadcast_to(table[pl.ds(i, 1), :], (8, LANES))

    return coef


def step_blocks(chan, table, loads, stores):
    coef = rows_of(table)

    def horizontal(c):
        center, above, left, spread = (coef(4 * c + k) for k in range(4))
        out = []
        for load in loads:
            v, n, s, w, e = load(c)
            out.append(center * v + above * n + left * w + spread * (s + e))
        return out

    mix_blocks(chan, table, horizontal, stores)


def mix_blocks(chan, table, fields, stores):
    levels = chan // 3
    blocks = range(len(stores))
    coef = rows_of(table)
    ys = {}
    for l in range(levels):
        for f in range(3):
            c = f * levels + l
            row = fields(c)
            if f:
                rate = coef(4 * chan + c - levels)
                row = [row[b] + rate * given[b] for b in blocks]
            given = row
            if l:
                ratio = coef(4 * chan + 2 * levels + c)
                row = [row[b] + ratio * ys[c - 1][b] for b in blocks]
            ys[c] = row
    xs = {}
    for l in range(levels - 1, -1, -1):
        for f in range(3):
            c = f * levels + l
            xs[f] = ys[c] if l == levels - 1 else [
                ys[c][b] + coef(4 * chan + 2 * levels + c) * xs[f][b] for b in blocks
            ]
            for b in blocks:
                stores[b](c, xs[f][b])


def sides(lane, west, v, east):
    w = pltpu.roll(jnp.where(lane == LANES - 1, west, v), 1, axis=1)
    e = pltpu.roll(jnp.where(lane == 0, east, v), LANES - 1, axis=1)
    return w, e


def parent_step(rows, chan, table, parent, strip, out, edges, ext, done, sems):
    blocks = parent.shape[1] // LANES
    groups = chan // 8
    lane = lane_ids()
    packed_at = strip.shape[1] - chan

    def columns(j):
        return pl.ds(aligned(j * LANES, LANES), LANES)

    packed = [strip[0, pl.ds(packed_at + 8 * g, 8), :] for g in range(groups)]

    @pl.loop(0, rows)
    def _(row):
        for g in range(groups):
            at = pl.ds(aligned((row + 1) * chan + 8 * g, 8), 8)
            turn = LANES - 1 - 2 * rows - 2 * row
            turned = pltpu.roll(packed[g], turn, axis=1)
            ext[0, at, :] = turned
            ext[blocks + 1, at, :] = turned

    @pl.loop(0, blocks)
    def _(j):
        ext[j + 1, pl.ds(chan, rows * chan), :] = parent[:, columns(j)]
        ext[j + 1, pl.ds(0, chan), :] = jnp.zeros((chan, LANES), F32)
        ext[j + 1, pl.ds((rows + 1) * chan, chan), :] = jnp.zeros((chan, LANES), F32)

    @pl.loop(0, blocks)
    def _(j):
        def block(first):
            def loads(c):
                def at(r):
                    return pl.ds((first + r) * chan + c, 8, stride=chan)

                v = ext[j + 1, at(1), :]
                w, e = sides(lane, ext[j, at(1), :], v, ext[j + 2, at(1), :])
                return v, ext[j + 1, at(0), :], ext[j + 1, at(2), :], w, e

            def store(c, x):
                done[j, pl.ds(first * chan + c, 8, stride=chan), :] = x

            return loads, store

        loads, stores = zip(*(block(first) for first in range(0, rows, 8)))
        step_blocks(chan, table, loads, stores)
        at = pl.ds(aligned(j * chan, 8), chan)
        edges[0, at, :] = done[j, pl.ds(0, chan), :]
        edges[1, at, :] = done[j, pl.ds((rows - 1) * chan, chan), :]
        pltpu.make_async_copy(done.at[j], out.at[:, columns(j)], sems.at[j]).start()

    @pl.loop(0, blocks)
    def _(j):
        pltpu.make_async_copy(done.at[j], out.at[:, columns(j)], sems.at[j]).wait()


def parent_edges(rows, chan, deep, table, near, far, edges, given, out, beside, done, sems):
    blocks = edges.shape[1] // chan
    per = near.shape[1] // LANES
    odd = lax.rem(lax.axis_index("tile"), 2) == 1
    for j in range(blocks):
        for g in range(chan // 8):
            at = pl.ds((deep + j // per) * chan + 8 * g, 8)
            a, b = (ref[at, pl.ds(j % per * LANES, LANES)] for ref in (near, far))
            at = pl.ds(j * chan + 8 * g, 8)
            beside[0, at, :] = jnp.where(odd, a, b)
            beside[1, at, :] = jnp.where(odd, b, a)
    coef = rows_of(table)
    pieces = [(k, b) for k in range(2) for b in range(0, blocks, 8)]

    def at(b, c):
        return pl.ds(b * chan + c, 8, stride=chan)

    def fields(c):
        return [coef(4 * c + (1, 3)[k]) * beside[k, at(b, c), :] for k, b in pieces]

    def storing(k, b):
        def store(c, x):
            done[k, at(b, c), :] = edges[k, at(b, c), :] + x

        return store

    mix_blocks(chan, table, fields, [storing(k, b) for k, b in pieces])
    copies = []
    for k, row in enumerate((0, rows - 1)):
        for j in range(blocks):
            copies.append(
                pltpu.make_async_copy(
                    done.at[k, pl.ds(j * chan, chan), :],
                    out.at[pl.ds(row * chan, chan), pl.ds(j * LANES, LANES)],
                    sems.at[k * blocks + j],
                )
            )
    for copy in copies:
        copy.start()
    for copy in copies:
        copy.wait()


def dealing(cols, back):
    first = lax.broadcasted_iota(jnp.int32, (cols, cols), 0)
    second = lax.broadcasted_iota(jnp.int32, (cols, cols), 1)
    planes = cols // LANES
    natural, dealt = (second, first) if back else (first, second)
    hit = natural == planes * lax.bitwise_and(dealt, LANES - 1) + lax.shift_right_arithmetic(dealt, 7)
    return jnp.where(hit, 1.0, 0.0).astype(jnp.bfloat16)


def dealt(x, matrix):
    out = None
    for _ in range(3):
        part = x.astype(jnp.bfloat16)
        x = x - part.astype(F32)
        term = jnp.dot(part, matrix, preferred_element_type=F32)
        out = term if out is None else out + term
    return out


def plane_blocks(chan, table, planes, lane, load, store):
    cache = {}

    def center(k, c):
        if (k, c) not in cache:
            cache[k, c] = load(0, k, c)
        return cache[k, c]

    def block(k):
        def loads(c):
            if k == 0:
                w = jnp.where(lane == 0, 0.0, pltpu.roll(center(planes - 1, c), 1, axis=1))
            else:
                w = center(k - 1, c)
            if k == planes - 1:
                e = jnp.where(lane == LANES - 1, 0.0, pltpu.roll(center(0, c), LANES - 1, axis=1))
            else:
                e = center(k + 1, c)
            return center(k, c), load(-1, k, c), load(1, k, c), w, e

        def put(c, x):
            store(k, c, x)

        return loads, put

    loads, stores = zip(*(block(k) for k in range(planes)))
    step_blocks(chan, table, loads, stores)


def nest_first(chan, deep, box, diff, wind, conv, mix, nest, moved, nudge, back, table, matrix, ext):
    make_table(diff, wind, conv, mix, table)
    nest_rows = nest.shape[0] // chan
    planes = nest.shape[1] // LANES
    ext_rows = nest_rows + 2 * deep
    groups = chan // 8
    sec, tile = lax.axis_index("sec"), lax.axis_index("tile")
    extent_x, extent_y = box[sec, 2], box[sec, 3]
    lane, sub = lane_ids(), sublane_ids()
    first_row = nest_rows * tile - deep
    matrix[...] = dealing(nest.shape[1], False)
    back[...] = dealing(nest.shape[1], True)
    for k in range(planes):
        col = planes * lane + k
        for rb in range(0, ext_rows, 8):
            i = first_row + rb + sub
            live = one_if((i >= 0) & (i < extent_x) & (col < extent_y))
            dist = jnp.minimum(jnp.minimum(i, col), jnp.minimum(extent_x - 1 - i, extent_y - 1 - col))
            dist = jnp.maximum(dist, 0).astype(F32)
            rate = 0.1 + 0.4 * jnp.exp(-dist / 3.0)
            nudge[0, k, pl.ds(rb, 8), :] = live * (1.0 - rate)
            nudge[1, k, pl.ds(rb, 8), :] = live * rate
            nudge[2, k, pl.ds(rb, 8), :] = live

    together = 4

    @pl.loop(0, nest_rows // together)
    def _(step):
        size = together * chan
        x = dealt(nest[pl.ds(aligned(step * size, 8), size), :], matrix[...])
        for r in range(together):
            row = step * together + r
            for k in range(planes):
                live = jnp.broadcast_to(nudge[2, k, pl.ds(deep + row, 1), :], (8, LANES))
                for g in range(groups):
                    piece = x[r * chan + 8 * g : r * chan + 8 * g + 8, k * LANES : (k + 1) * LANES]
                    ext[k, pl.ds(aligned((row + 1) * chan + 8 * g, 8), 8), :] = piece * live

    for row in (0, nest_rows + 1):
        ext[:, pl.ds(row * chan, chan), :] = jnp.zeros((planes, chan, LANES), F32)
    for rb in range(0, nest_rows, 8):

        def load(shift, k, c):
            return ext[k, pl.ds((rb + 1 + shift) * chan + c, 8, stride=chan), :]

        def store(k, c, x):
            at = pl.ds(deep + rb, 8)
            moved[k, c, at, :] = x * nudge[0, k, at, :]

        plane_blocks(chan, table, planes, lane, load, store)


def nest_edges(chan, deep, table, nest, near, far, nudge, given, moved, matrix, natural, ext):
    nest_rows = nest.shape[0] // chan
    planes = nest.shape[1] // LANES
    ext_rows = nest_rows + 2 * deep
    size = deep * chan
    lane, sub = lane_ids(), sublane_ids()
    odd = lax.rem(lax.axis_index("tile"), 2) == 1
    matrix[...] = dealing(nest.shape[1], False)
    edge = (deep + 2) * chan
    a, b = near[pl.ds(0, size), :], far[pl.ds(0, size), :]
    natural[pl.ds(0, size), :] = jnp.where(odd, a, b)
    natural[pl.ds(size, 2 * chan), :] = nest[pl.ds(0, 2 * chan), :]
    natural[pl.ds(edge, 2 * chan), :] = nest[pl.ds((nest_rows - 2) * chan, 2 * chan), :]
    natural[pl.ds(edge + 2 * chan, size), :] = jnp.where(odd, b, a)
    for half in range(2):

        def rows_at(r):
            return r if half == 0 else ext_rows - deep - 2 + r

        x = dealt(natural[pl.ds(half * edge, edge), :], matrix[...])
        for r in range(deep + 2):
            for k in range(planes):
                live = jnp.broadcast_to(nudge[2, k, pl.ds(rows_at(r), 1), :], (8, LANES))
                for g in range(chan // 8):
                    piece = x[r * chan + 8 * g : r * chan + 8 * g + 8, k * LANES : (k + 1) * LANES]
                    ext[k, pl.ds(half * edge + r * chan + 8 * g, 8), :] = piece * live

    def load(shift, k, c):
        upper = ext[k, pl.ds((1 + shift) * chan + c, 8, stride=chan), :]
        lower = ext[k, pl.ds((3 + shift) * chan + c, 8, stride=chan), :]
        return jnp.where(sub < deep, upper, lower)

    def store(k, c, x):
        low, high = pl.ds(1, deep), pl.ds(ext_rows - 1 - deep, deep)
        moved[k, c, low, :] = x[:deep] * nudge[0, k, low, :]
        moved[k, c, high, :] = x[deep:] * nudge[0, k, high, :]

    plane_blocks(chan, table, planes, lane, load, store)


def nest_rest(
    rows, chan, deep, own_rows, tiles,
    anchor, table, own, got_a, got_b, got_c, moved, nudge, back, out,
    slots, foot, coarse, state, force, done, final, sems,
):
    planes, _, ext_rows, _ = moved.shape
    nest_rows = ext_rows - 2 * deep
    groups = chan // 8
    tile = lax.axis_index("tile")
    lane, sub = lane_ids(), sublane_ids()
    first_row = nest_rows * tile - deep
    start = jnp.max(anchor[...]) + own_rows * tile - 2
    span = foot.shape[1] // chan - 1
    size = rows // 2 * chan
    part = lax.rem(lax.div(tile, 2), 2)
    side = lax.rem(tile, 2)

    for k, ref in enumerate((own, got_a, got_b, got_c)):
        slots[k] = ref[...]

    for m in range(span):
        row = start + m
        local = lax.bitwise_and(row, rows - 1)
        upper = lax.div(local, rows // 2)
        other = lax.bitwise_and(lax.shift_right_arithmetic(row, rows.bit_length() - 1), 1)
        k = 2 * lax.bitwise_xor(upper, part) + lax.bitwise_xor(other, side)
        inside = one_if((row >= 0) & (row < rows * tiles))
        slot = (local - upper * (rows // 2)) * chan
        turn = LANES - 1 - 2 * local
        for g in range(groups):
            at = pl.ds(m * chan + 8 * g, 8)
            foot[0, at, :] = pltpu.roll(slots[k, pl.ds(size + 8 * g, 8), :] * inside, turn, axis=1)
            foot[1, at, :] = slots[k, pl.ds(aligned(slot + 8 * g, 8), 8), :] * inside

    for k in range(2):
        foot[k, pl.ds(span * chan, chan), :] = jnp.zeros((chan, LANES), F32)

    def foot_loads(c):
        def at(r):
            return pl.ds(r * chan + c, 8, stride=chan)

        v = foot[1, at(1), :]
        edge = foot[0, at(1), :]
        w, e = sides(lane, edge, v, edge)
        return v, foot[1, at(0), :], foot[1, at(2), :], w, e

    def foot_store(c, x):
        old = foot[1, pl.ds(chan + c, 8, stride=chan), :]
        coarse[0, c] = old
        coarse[1, c] = x - old

    step_blocks(chan, table, [foot_loads], [foot_store])

    share = []
    for rb in range(0, ext_rows, 8):
        p = lax.rem(sub, RATIO).astype(F32) / RATIO
        share.append(jnp.where(first_row + rb + sub >= RATIO * (own_rows * tiles - 1), 0.0, p))

    together = 3

    @pl.loop(0, chan // together)
    def _(i):
        for c in (together * i + t for t in range(together)):
            for rb in range(0, ext_rows, 8):
                u = rb // RATIO
                at = pl.ds(rb, 8)
                lines = []
                for t in range(2):
                    r0, r1, r2 = (
                        jnp.broadcast_to(coarse[t, c, pl.ds(u + n, 1), :], (8, LANES)) for n in range(3)
                    )
                    a0 = jnp.where(sub < RATIO, r0, r1)
                    a1 = jnp.where(sub < RATIO, r1, r2)
                    level = a0 + share[rb // 8] * (a1 - a0)
                    beside = jnp.where(lane == LANES - 1, level, pltpu.roll(level, LANES - 1, axis=1))
                    slope = (beside - level) * (1.0 / RATIO)
                    force[t, c, at, :] = level
                    force[2 + t, c, at, :] = slope
                    lines.append((level, slope))
                level, slope = (old + new * (1.0 / NSTEP) for old, new in zip(*lines))
                for k in range(planes):
                    g = level + float(k) * slope if k else level
                    state[0, k, c, pl.ds(8 + rb, 8), :] = moved[k, c, at, :] + nudge[1, k, at, :] * g

    def advance(step, src, rb, put):
        weight = jnp.float32(step + 1) / NSTEP
        at = pl.ds(rb, 8)
        lines = {}

        def load(shift, k, c):
            return state[src, k, c, pl.ds(8 + rb + shift, 8), :]

        def store(k, c, x):
            if c not in lines:
                lines[c] = [force[t, c, at, :] + weight * force[t + 1, c, at, :] for t in (0, 2)]
            level, slope = lines[c]
            g = level + float(k) * slope if k else level
            put(k, c, nudge[0, k, at, :] * x + nudge[1, k, at, :] * g)

        plane_blocks(chan, table, planes, lane, load, store)

    @pl.loop(1, NSTEP - 1)
    def _(step):
        src = lax.rem(step + 1, 2)

        @pl.loop(0, ext_rows // 8)
        def _(block):
            rb = aligned(block * 8, 8)

            def put(k, c, x):
                state[1 - src, k, c, pl.ds(8 + rb, 8), :] = x

            advance(step, src, rb, put)

    copies = []
    for n, rb in enumerate(range(0, nest_rows, 8)):

        def put(k, c, x):
            done[n, k, pl.ds(c, 8, stride=chan), :] = x

        advance(NSTEP - 1, NSTEP % 2, deep + rb, put)
        whole = jnp.concatenate([done[n, k] for k in range(planes)], axis=1)
        final[n] = dealt(whole, back[...])
        copies.append(
            pltpu.make_async_copy(final.at[n], out.at[pl.ds(rb * chan, 8 * chan), :], sems.at[n])
        )
        copies[n].start()
    for copy in copies:
        copy.wait()


def bound(kernel, *static):
    def run(*refs):
        return kernel(*static, *refs)

    return run


def exchange(block, axis, bit):
    return lax.ppermute(block, axis, [(i, i ^ bit) for i in range(lax.axis_size(axis))])


def exchange_both(block, sec_bit, tile_bit):
    secs, tiles = lax.axis_size("sec"), lax.axis_size("tile")
    route = [
        (s * tiles + t, (s ^ sec_bit) * tiles + (t ^ tile_bit)) for s in range(secs) for t in range(tiles)
    ]
    return lax.ppermute(block, ("sec", "tile"), route)


def body(parent_old, nest_state, diffusion, wind_speed, conversion, vert_mix, nest_box):
    rows, chan, cols = parent_old.shape
    nest_rows, nest_cols = nest_state.shape[1], nest_state.shape[3]
    secs, tiles = lax.axis_size("sec"), lax.axis_size("tile")
    own_rows = nest_rows // RATIO
    levels = conversion.shape[1]
    deep = NSTEP
    ext_rows = nest_rows + 2 * deep
    col_blocks = nest_cols // LANES
    blocks = cols // LANES
    span = (ext_rows // RATIO + 1) + 2
    strip_rows = (rows + 1) * chan
    half_rows = (rows // 2 + 1) * chan
    parent = parent_old.reshape(rows * chan, cols)
    nest = nest_state.reshape(nest_rows * chan, nest_cols)
    half = shape(half_rows, LANES)

    halo = shape((deep + cols // nest_cols) * chan, nest_cols)
    near, far = call(
        bound(edge_rows, deep, chan), [halo] * 2, (nest, parent), (ANY, ANY),
        scratch=[pltpu.SemaphoreType.DMA((2 * (1 + cols // nest_cols),))], limit=4, cost=1 << 20,
    )
    near = exchange(near, "tile", 1)
    beside = [(i, i + 1) for i in range(1, tiles - 1, 2)]
    far = lax.ppermute(far, "tile", beside + [(j, i) for i, j in beside])

    some = shape(secs // 2, strip_rows, LANES)
    keep, send, anchor = call(
        bound(extract, rows, chan), [some, some, shape(8, LANES, dtype=jnp.int32)],
        (nest_box, parent), (HBM, HBM), cost=4 << 20,
        scratch=[
            pltpu.SMEM(nest_box.shape, jnp.int32),
            pltpu.VMEM(parent.shape, F32),
            pltpu.SemaphoreType.DMA((2,)),
        ],
    )
    got = exchange(send, "sec", 1)
    bit = 2
    while bit < secs // 2:
        some = shape(secs // (2 * bit), strip_rows, LANES)
        keep, send = call(bound(combine, bit), [some, some], (keep, got), (VMEM, VMEM), cost=1 << 20)
        got = exchange(send, "sec", bit)
        bit *= 2
    mine, to_sec, to_tile, to_both = call(
        bound(split, rows, chan), [half] * 4, (keep, got), (VMEM, VMEM), cost=1 << 18,
    )
    from_sec = exchange_both(to_sec, secs // 2, 0)
    from_tile = exchange_both(to_tile, 0, 2)
    from_both = exchange_both(to_both, secs // 2, 2)
    moved_shape = shape(col_blocks, chan, ext_rows, LANES)
    square = (nest_cols, nest_cols)
    moved, nudge, back, table = call(
        bound(nest_first, chan, deep),
        [moved_shape, shape(3, col_blocks, ext_rows, LANES), shape(*square, dtype=jnp.bfloat16),
         shape(table_rows(chan, levels), LANES)],
        (nest_box, diffusion, wind_speed, conversion, vert_mix, nest), (SMEM,) * 5 + (VMEM,), cost=6 << 20,
        scratch=[
            pltpu.VMEM(square, jnp.bfloat16),
            pltpu.VMEM((col_blocks, (nest_rows + 2) * chan, LANES), F32),
        ],
    )

    two = shape(2, half_rows, LANES)
    (strip,) = call(
        gathered, [two], (mine, from_sec, from_tile, from_both, moved), (VMEM,) * 5, cost=1 << 18,
    )
    pair = strip
    group = tiles // 2
    while group > 4:
        got = exchange(pair, "tile", group)
        (pair,) = call(
            bound(choose, rows, own_rows, group, tiles), [two], (anchor, pair, got), (VMEM,) * 3, cost=1 << 18,
        )
        group //= 2
    mine, sent = call(
        bound(select, rows, chan, own_rows, tiles), [half] * 2, (anchor, pair), (VMEM,) * 2, cost=1 << 18,
    )
    got = exchange(sent, "tile", 4)
    edge = shape(2, blocks * chan, LANES)
    parent_new, edges = call(
        bound(parent_step, rows, chan), [shape(rows * chan, cols), edge],
        (table, parent, strip), (VMEM,) * 3, cost=8 << 20, out_specs=[ANY, VMEM],
        scratch=[
            pltpu.VMEM((blocks + 2, (rows + 2) * chan, LANES), F32),
            pltpu.VMEM((blocks, rows * chan, LANES), F32),
            pltpu.SemaphoreType.DMA((blocks,)),
        ],
    )

    (own,) = call(
        bound(settle, rows, chan, own_rows, tiles), [half], (anchor, mine, got, near, edges), (VMEM,) * 5, cost=1 << 18,
    )
    got_a, got_b, got_c = (exchange(own, "tile", k) for k in (1, 2, 3))

    (parent_new,) = call(
        bound(parent_edges, rows, chan, deep), [shape(rows * chan, cols)],
        (table, near, far, edges, parent_new), (VMEM,) * 4 + (ANY,), cost=1 << 20, out_specs=[ANY], same={4: 0},
        scratch=[
            pltpu.VMEM((2, blocks * chan, LANES), F32),
            pltpu.VMEM((2, blocks * chan, LANES), F32),
            pltpu.SemaphoreType.DMA((2 * blocks,)),
        ],
    )
    (moved,) = call(
        bound(nest_edges, chan, deep), [moved_shape],
        (table, nest, near, far, nudge, moved), (VMEM,) * 6, cost=3 << 20, same={5: 0},
        scratch=[
            pltpu.VMEM(square, jnp.bfloat16),
            pltpu.VMEM((2 * (deep + 2) * chan, nest_cols), F32),
            pltpu.VMEM((col_blocks, 2 * (deep + 2) * chan, LANES), F32),
        ],
    )

    (nest_new,) = call(
        bound(nest_rest, rows, chan, deep, own_rows, tiles), [shape(nest_rows * chan, nest_cols)],
        (anchor, table, own, got_a, got_b, got_c, moved, nudge, back), (VMEM,) * 9, cost=16 << 20, out_specs=[ANY],
        limit=32,
        scratch=[
            pltpu.VMEM((4, half_rows, LANES), F32),
            pltpu.VMEM((2, (span + 1) * chan, LANES), F32),
            pltpu.VMEM((2, chan, 8, LANES), F32),
            pltpu.VMEM((2, col_blocks, chan, ext_rows + 16, LANES), F32),
            pltpu.VMEM((4, chan, ext_rows, LANES), F32),
            pltpu.VMEM((nest_rows // 8, col_blocks, 8 * chan, LANES), F32),
            pltpu.VMEM((nest_rows // 8, 8 * chan, nest_cols), F32),
            pltpu.SemaphoreType.DMA((nest_rows // 8,)),
        ],
    )

    return parent_new.reshape(parent_old.shape), nest_new.reshape(nest_state.shape)


def solution(mesh):
    placed = (P("tile", None, "sec"), P("sec", "tile", None, None), P(), P(), P(), P(), P())
    return jax.shard_map(
        body,
        mesh=mesh,
        in_specs=placed,
        out_specs=(P("tile", None, "sec"), P("sec", "tile", None, None)),
        check_vma=False,
    )
```

```python
import jax
import jax.numpy as jnp
from jax import lax
from jax.experimental import pallas as pl
from jax.experimental.pallas import tpu as pltpu
from jax.sharding import PartitionSpec as P

NSTEP = 4
RATIO = 4
LANES = 128
F32 = jnp.float32
VMEM = pl.BlockSpec(memory_space=pltpu.VMEM)
SMEM = pl.BlockSpec(memory_space=pltpu.SMEM)
ANY = pl.BlockSpec(memory_space=pl.ANY)
HBM = pl.BlockSpec(memory_space=pltpu.HBM)
TOGETHER = 8


def call(kernel, outs, args, specs, scratch=(), limit=16, cost=0, out_specs=None, same=None):
    return pl.pallas_call(
        kernel,
        out_shape=list(outs),
        in_specs=list(specs),
        out_specs=[VMEM] * len(outs) if out_specs is None else out_specs,
        scratch_shapes=list(scratch),
        input_output_aliases=same or {},
        compiler_params=pltpu.CompilerParams(vmem_limit_bytes=limit << 20),
        cost_estimate=pl.CostEstimate(flops=0, bytes_accessed=cost, transcendentals=0),
    )(*args)


def shape(*dims, dtype=F32):
    return jax.ShapeDtypeStruct(dims, dtype)


def lane_ids():
    return lax.broadcasted_iota(jnp.int32, (8, LANES), 1)


def sublane_ids():
    return lax.broadcasted_iota(jnp.int32, (8, LANES), 0)


def one_if(condition):
    return jnp.where(condition, 1.0, 0.0).astype(F32)


def aligned(start, step):
    return pl.multiple_of(start, step)


def edge_rows(deep, chan, nest, parent, near, far, sems):
    odd = lax.rem(lax.axis_index("tile"), 2)
    cols = nest.shape[1]
    copies = []
    for k, (dest, last) in enumerate(((near, 1 - odd), (far, odd))):
        size = deep * chan
        at = aligned(last * (nest.shape[0] - size), 8)
        copies.append((nest.at[pl.ds(at, size), :], dest.at[pl.ds(0, size), :]))
        at = aligned(last * (parent.shape[0] - chan), 8)
        for part in range(parent.shape[1] // cols):
            source = parent.at[pl.ds(at, chan), pl.ds(part * cols, cols)]
            copies.append((source, dest.at[pl.ds(size + part * chan, chan), :]))
    made = [pltpu.make_async_copy(a, b, sems.at[i]) for i, (a, b) in enumerate(copies)]
    for copy in made:
        copy.start()
    for copy in made:
        copy.wait()


def extract(rows, chan, box_in, parent_in, keep, send, anchor, box, parent, sems):
    copies = [
        pltpu.make_async_copy(box_in, box, sems.at[0]),
        pltpu.make_async_copy(parent_in, parent, sems.at[1]),
    ]
    for copy in copies:
        copy.start()
    for copy in copies:
        copy.wait()
    cols = parent.shape[1]
    blocks = cols // LANES
    groups = chan // 8
    sec = lax.axis_index("sec")
    half = lax.rem(sec, 2)
    lane = lane_ids()
    anchor[...] = jnp.full((8, LANES), box[sec, 0], jnp.int32)

    def at(row, g):
        return pl.ds(aligned(row * chan + 8 * g, 8), 8)

    lane_row = lax.div(lane, 2)
    together = TOGETHER

    def outer(step, packed):
        packed = list(packed)
        for k in range(together):
            row = step * together + k
            for g in range(groups):
                ends = jnp.where(
                    lane < LANES // 2,
                    parent[at(row, g), pl.ds(0, LANES)],
                    parent[at(row, g), pl.ds(cols - LANES, LANES)],
                )
                ends = pltpu.roll(ends, 2 * rows + 2 * row + 1, axis=1)
                packed[g] = jnp.where(lane_row == rows + row, ends, packed[g])
        return tuple(packed)

    zeros = (jnp.zeros((8, LANES), F32),) * groups
    halo = lax.fori_loop(0, rows // together, outer, zeros)

    for which, dest in ((1 - half, send), (half, keep)):

        @pl.loop(0, dest.shape[0])
        def _(i):
            nest = 2 * i + which
            offset = box[nest, 1] - sec * cols
            shift = lax.bitwise_and(offset, LANES - 1)
            back = lax.bitwise_and(LANES - shift, LANES - 1)

            def place(k):
                start = aligned(jnp.clip(k, 0, blocks - 1) * LANES, LANES)
                return pl.ds(start, LANES), one_if((k >= 0) & (k < blocks))

            first = lax.shift_right_arithmetic(offset, 7)
            at_a, on_a = place(first)
            at_b, on_b = place(first + 1)
            at_c, on_c = place(lax.shift_right_arithmetic(offset - 1, 7))
            before = lax.bitwise_and(lane - shift, LANES - 1) >= LANES // 2
            sent = jnp.where(lax.rem(lane, 2) == 0, one_if(nest == sec + 1), one_if(nest == sec - 1))

            def inner(step, packed):
                packed = list(packed)
                shifted = []
                for k in range(together):
                    row = step * together + k
                    turn = lax.bitwise_and(back + 2 * row + 1, LANES - 1)
                    for g in range(groups):
                        a = parent[at(row, g), at_a] * on_a
                        b = parent[at(row, g), at_b] * on_b
                        c = parent[at(row, g), at_c] * on_c
                        main = pltpu.roll(jnp.where(lane < shift, b, a), back, axis=1)
                        shifted.append((at(row, g), main))
                        side = pltpu.roll(jnp.where(before, c, b), turn, axis=1)
                        packed[g] = jnp.where(lane_row == row, side, packed[g])
                for where, main in shifted:
                    dest[i, where, :] = main
                return tuple(packed)

            here = (offset >= -LANES) & (offset <= cols)

            @pl.when(here)
            def _():
                packed = lax.fori_loop(0, rows // together, inner, tuple(h * sent for h in halo))
                for g in range(groups):
                    dest[i, pl.ds(rows * chan + 8 * g, 8), :] = packed[g]

            @pl.when(jnp.logical_not(here))
            def _():
                dest[i, pl.ds(0, rows * chan), :] = jnp.zeros((rows * chan, LANES), F32)
                for g in range(groups):
                    dest[i, pl.ds(rows * chan + 8 * g, 8), :] = halo[g] * sent


def combine(bit, own, got, keep, send):
    mine = lax.rem(lax.axis_index("sec") // bit, 2)
    for i in range(keep.shape[0]):
        send[i] = own[2 * i + 1 - mine] + got[2 * i + 1 - mine]
        keep[i] = own[2 * i + mine] + got[2 * i + mine]


def split(rows, chan, own, got, mine, to_sec, to_tile, to_both):
    sec = lax.div(lax.axis_index("sec"), lax.axis_size("sec") // 2)
    part = lax.rem(lax.div(lax.axis_index("tile"), 2), 2)
    size = rows // 2 * chan
    for dest, nest, half in (
        (to_sec, 1 - sec, part),
        (to_both, 1 - sec, 1 - part),
        (to_tile, sec, 1 - part),
        (mine, sec, part),
    ):
        for j in range(rows // 2):
            at = pl.ds(aligned((2 * j + half) * chan, 8), chan)
            dest[pl.ds(j * chan, chan), :] = own[nest, at, :] + got[nest, at, :]
        at = pl.ds(rows * chan, chan)
        dest[pl.ds(size, chan), :] = own[nest, at, :] + got[nest, at, :]


def gathered(mine, from_sec, from_tile, from_both, moved, out):
    out[0] = mine[...] + from_sec[...]
    out[1] = from_tile[...] + from_both[...]


def held_block(anchor, tile, rows, own_rows, group):
    first = lax.div(tile, group) * group
    low = jnp.maximum(anchor + (own_rows * first - 2), 0)
    base = lax.shift_right_arithmetic(low, rows.bit_length() - 1)
    return base + lax.bitwise_and(tile - base, group - 1)


def held(anchor, tile, rows, own_rows, group, tiles):
    if group == tiles:
        return jnp.full((8, LANES), tile, jnp.int32)
    return held_block(anchor, tile, rows, own_rows, group)


def choose(rows, own_rows, group, tiles, anchor, own, got, out):
    start = anchor[...]
    for k in range(2):
        tile = lax.bitwise_xor(lax.axis_index("tile"), 2 * k)
        keep = held(start, tile, rows, own_rows, 2 * group, tiles) == held_block(
            start, tile, rows, own_rows, group
        )
        for r in range(0, out.shape[1], 8):
            at = pl.ds(r, 8)
            out[k, at, :] = jnp.where(keep, own[k, at, :], got[k, at, :])


def wanted(anchor, row, tile, group, own_rows):
    first = lax.div(tile, group) * group
    low = anchor + (own_rows * first - 2)
    return (row >= low) & (row <= low + own_rows * group + 4)


def slot_rows(rows, own_rows, tiles, anchor):
    tile = lax.axis_index("tile")
    return [
        rows * held(anchor, lax.bitwise_xor(tile, 2 * k), rows, own_rows, 8, tiles) for k in range(2)
    ]


def select(rows, chan, own_rows, tiles, anchor, both, mine, sent):
    start = anchor[...]
    tile = lax.axis_index("tile")
    part = lax.rem(lax.div(tile, 2), 2)
    size = rows // 2 * chan
    base = slot_rows(rows, own_rows, tiles, start)
    lane_row = lax.div(lane_ids(), 2)
    for dest, owner in ((sent, lax.bitwise_xor(tile, 4)), (mine, tile)):
        for j in range(rows // 2 + 1):
            row = lane_row if j == rows // 2 else 2 * j + part
            second = wanted(start, base[1] + row, owner, 4, own_rows)
            for g in range(chan // 8):
                at = pl.ds(j * chan + 8 * g, 8)
                dest[at, :] = jnp.where(second, both[1, at, :], both[0, at, :])


def settle(rows, chan, own_rows, tiles, anchor, mine, got, near, parent, out, *sent):
    start = anchor[...]
    tile = lax.axis_index("tile")
    part = lax.rem(lax.div(tile, 2), 2)
    base = slot_rows(rows, own_rows, tiles, start)
    lane_row = lax.div(lane_ids(), 2)
    groups = range(chan // 8)
    slots = rows // 2
    held_rows = {}
    for j in range(slots + 1):
        row = lane_row if j == slots else 2 * j + part
        keep = wanted(start, base[0] + row, tile, 4, own_rows)
        keep = keep | wanted(start, base[1] + row, tile, 4, own_rows)
        for g in groups:
            at = pl.ds(j * chan + 8 * g, 8)
            held_rows[j, g] = jnp.where(keep, mine[at, :], got[at, :])
            out[at, :] = held_rows[j, g]
    for k, dest in enumerate(sent):
        count = dest.shape[0] // chan - 1
        first = start + (own_rows * lax.bitwise_xor(tile, k + 1) - 2)
        first = lax.shift_right_arithmetic(first + lax.bitwise_and(lax.bitwise_xor(first, part), 1), 1)
        for i in range(count):
            slot = lax.bitwise_and(first + i, slots - 1)
            row = [held_rows[0, g] for g in groups]
            for j in range(1, slots):
                row = [jnp.where(slot == j, held_rows[j, g], row[g]) for g in groups]
            for g in groups:
                dest[pl.ds(i * chan + 8 * g, 8), :] = row[g]
        for g in groups:
            dest[pl.ds(count * chan + 8 * g, 8), :] = held_rows[slots, g]


def table_rows(chan, levels):
    return 4 * chan + 2 * levels + chan


def make_table(diff, wind, conv, mix, table):
    chan, levels = diff.shape[0], conv.shape[1]

    def line(value):
        return jnp.full((1, LANES), value, F32)

    def put(i, value):
        table[pl.ds(i, 1), :] = value

    scale = {}
    for f in range(3):
        m = line(mix[f])
        ratio = None
        for l in range(levels):
            c = f * levels + l
            pivot = 1.0 + (1.0 if l in (0, levels - 1) else 2.0) * m
            if l:
                pivot = pivot - m * ratio
            inverse = 1.0 / pivot
            ratio = m * inverse
            put(4 * chan + 2 * levels + c, ratio)
            scale[c] = inverse * (1.0 - line(conv[f, l])) if f < 2 else inverse
            d, wx, wy = diff[c], wind[0, c], wind[1, c]
            for k, value in enumerate((1.0 - 4.0 * d - wx - wy, d + wx, d + wy, d)):
                put(4 * c + k, scale[c] * line(value))
            if f:
                before = c - levels
                put(4 * chan + before, scale[c] * line(conv[f - 1, l]) / scale[before])


def rows_of(table):
    def coef(i):
        return jnp.broadcast_to(table[pl.ds(i, 1), :], (8, LANES))

    return coef


def step_blocks(chan, table, loads, stores):
    coef = rows_of(table)

    def horizontal(c):
        center, above, left, spread = (coef(4 * c + k) for k in range(4))
        out = []
        for load in loads:
            v, n, s, w, e = load(c)
            out.append(center * v + above * n + left * w + spread * (s + e))
        return out

    mix_blocks(chan, table, horizontal, stores)


def mix_blocks(chan, table, fields, stores):
    levels = chan // 3
    blocks = range(len(stores))
    coef = rows_of(table)
    ys = {}
    for l in range(levels):
        for f in range(3):
            c = f * levels + l
            row = fields(c)
            if f:
                rate = coef(4 * chan + c - levels)
                row = [row[b] + rate * given[b] for b in blocks]
            given = row
            if l:
                ratio = coef(4 * chan + 2 * levels + c)
                row = [row[b] + ratio * ys[c - 1][b] for b in blocks]
            ys[c] = row
    xs = {}
    for l in range(levels - 1, -1, -1):
        for f in range(3):
            c = f * levels + l
            xs[f] = ys[c] if l == levels - 1 else [
                ys[c][b] + coef(4 * chan + 2 * levels + c) * xs[f][b] for b in blocks
            ]
            for b in blocks:
                stores[b](c, xs[f][b])


def sides(lane, west, v, east):
    w = pltpu.roll(jnp.where(lane == LANES - 1, west, v), 1, axis=1)
    e = pltpu.roll(jnp.where(lane == 0, east, v), LANES - 1, axis=1)
    return w, e


def parent_step(rows, chan, table, parent, strip, out, edges, ext, done, sems):
    blocks = parent.shape[1] // LANES
    groups = chan // 8
    lane = lane_ids()
    packed_at = strip.shape[1] - chan

    def columns(j):
        return pl.ds(aligned(j * LANES, LANES), LANES)

    packed = [strip[0, pl.ds(packed_at + 8 * g, 8), :] for g in range(groups)]

    @pl.loop(0, rows)
    def _(row):
        for g in range(groups):
            at = pl.ds(aligned((row + 1) * chan + 8 * g, 8), 8)
            turn = LANES - 1 - 2 * rows - 2 * row
            turned = pltpu.roll(packed[g], turn, axis=1)
            ext[0, at, :] = turned
            ext[blocks + 1, at, :] = turned

    @pl.loop(0, blocks)
    def _(j):
        ext[j + 1, pl.ds(chan, rows * chan), :] = parent[:, columns(j)]
        ext[j + 1, pl.ds(0, chan), :] = jnp.zeros((chan, LANES), F32)
        ext[j + 1, pl.ds((rows + 1) * chan, chan), :] = jnp.zeros((chan, LANES), F32)

    @pl.loop(0, blocks)
    def _(j):
        def block(first):
            def loads(c):
                def at(r):
                    return pl.ds((first + r) * chan + c, 8, stride=chan)

                v = ext[j + 1, at(1), :]
                w, e = sides(lane, ext[j, at(1), :], v, ext[j + 2, at(1), :])
                return v, ext[j + 1, at(0), :], ext[j + 1, at(2), :], w, e

            def store(c, x):
                done[j, pl.ds(first * chan + c, 8, stride=chan), :] = x

            return loads, store

        loads, stores = zip(*(block(first) for first in range(0, rows, 8)))
        step_blocks(chan, table, loads, stores)
        at = pl.ds(aligned(j * chan, 8), chan)
        edges[0, at, :] = done[j, pl.ds(0, chan), :]
        edges[1, at, :] = done[j, pl.ds((rows - 1) * chan, chan), :]
        pltpu.make_async_copy(done.at[j], out.at[:, columns(j)], sems.at[j]).start()

    @pl.loop(0, blocks)
    def _(j):
        pltpu.make_async_copy(done.at[j], out.at[:, columns(j)], sems.at[j]).wait()


def parent_edges(rows, chan, deep, table, near, far, edges, given, out, beside, done, sems):
    blocks = edges.shape[1] // chan
    per = near.shape[1] // LANES
    odd = lax.rem(lax.axis_index("tile"), 2) == 1
    for j in range(blocks):
        for g in range(chan // 8):
            at = pl.ds((deep + j // per) * chan + 8 * g, 8)
            a, b = (ref[at, pl.ds(j % per * LANES, LANES)] for ref in (near, far))
            at = pl.ds(j * chan + 8 * g, 8)
            beside[0, at, :] = jnp.where(odd, a, b)
            beside[1, at, :] = jnp.where(odd, b, a)
    coef = rows_of(table)
    pieces = [(k, b) for k in range(2) for b in range(0, blocks, 8)]

    def at(b, c):
        return pl.ds(b * chan + c, 8, stride=chan)

    def fields(c):
        return [coef(4 * c + (1, 3)[k]) * beside[k, at(b, c), :] for k, b in pieces]

    def storing(k, b):
        def store(c, x):
            done[k, at(b, c), :] = edges[k, at(b, c), :] + x

        return store

    mix_blocks(chan, table, fields, [storing(k, b) for k, b in pieces])
    copies = []
    for k, row in enumerate((0, rows - 1)):
        for j in range(blocks):
            copies.append(
                pltpu.make_async_copy(
                    done.at[k, pl.ds(j * chan, chan), :],
                    out.at[pl.ds(row * chan, chan), pl.ds(j * LANES, LANES)],
                    sems.at[k * blocks + j],
                )
            )
    for copy in copies:
        copy.start()
    for copy in copies:
        copy.wait()


def dealing(cols, back):
    first = lax.broadcasted_iota(jnp.int32, (cols, cols), 0)
    second = lax.broadcasted_iota(jnp.int32, (cols, cols), 1)
    planes = cols // LANES
    natural, dealt = (second, first) if back else (first, second)
    hit = natural == planes * lax.bitwise_and(dealt, LANES - 1) + lax.shift_right_arithmetic(dealt, 7)
    return jnp.where(hit, 1.0, 0.0).astype(jnp.bfloat16)


def dealt(x, matrix):
    out = None
    for _ in range(3):
        part = x.astype(jnp.bfloat16)
        x = x - part.astype(F32)
        term = jnp.dot(part, matrix, preferred_element_type=F32)
        out = term if out is None else out + term
    return out


def plane_blocks(chan, table, planes, lane, load, store):
    cache = {}

    def center(k, c):
        if (k, c) not in cache:
            cache[k, c] = load(0, k, c)
        return cache[k, c]

    def block(k):
        def loads(c):
            if k == 0:
                w = jnp.where(lane == 0, 0.0, pltpu.roll(center(planes - 1, c), 1, axis=1))
            else:
                w = center(k - 1, c)
            if k == planes - 1:
                e = jnp.where(lane == LANES - 1, 0.0, pltpu.roll(center(0, c), LANES - 1, axis=1))
            else:
                e = center(k + 1, c)
            return center(k, c), load(-1, k, c), load(1, k, c), w, e

        def put(c, x):
            store(k, c, x)

        return loads, put

    loads, stores = zip(*(block(k) for k in range(planes)))
    step_blocks(chan, table, loads, stores)


def nest_first(chan, deep, box, diff, wind, conv, mix, nest, moved, nudge, back, matrix, table, ext):
    make_table(diff, wind, conv, mix, table)
    nest_rows = nest.shape[0] // chan
    planes = nest.shape[1] // LANES
    ext_rows = nest_rows + 2 * deep
    groups = chan // 8
    sec, tile = lax.axis_index("sec"), lax.axis_index("tile")
    extent_x, extent_y = box[sec, 2], box[sec, 3]
    lane, sub = lane_ids(), sublane_ids()
    first_row = nest_rows * tile - deep
    matrix[...] = dealing(nest.shape[1], False)
    back[...] = dealing(nest.shape[1], True)
    for k in range(planes):
        col = planes * lane + k
        for rb in range(0, ext_rows, 8):
            i = first_row + rb + sub
            live = one_if((i >= 0) & (i < extent_x) & (col < extent_y))
            dist = jnp.minimum(jnp.minimum(i, col), jnp.minimum(extent_x - 1 - i, extent_y - 1 - col))
            dist = jnp.maximum(dist, 0).astype(F32)
            rate = 0.1 + 0.4 * jnp.exp(-dist / 3.0)
            nudge[0, k, pl.ds(rb, 8), :] = live * (1.0 - rate)
            nudge[1, k, pl.ds(rb, 8), :] = live * rate
            nudge[2, k, pl.ds(rb, 8), :] = live

    together = 4

    @pl.loop(0, nest_rows // together)
    def _(step):
        size = together * chan
        x = dealt(nest[pl.ds(aligned(step * size, 8), size), :], matrix[...])
        for r in range(together):
            row = step * together + r
            for k in range(planes):
                live = jnp.broadcast_to(nudge[2, k, pl.ds(deep + row, 1), :], (8, LANES))
                for g in range(groups):
                    piece = x[r * chan + 8 * g : r * chan + 8 * g + 8, k * LANES : (k + 1) * LANES]
                    ext[k, pl.ds(aligned((row + 1) * chan + 8 * g, 8), 8), :] = piece * live

    for row in (0, nest_rows + 1):
        ext[:, pl.ds(row * chan, chan), :] = jnp.zeros((planes, chan, LANES), F32)
    for rb in range(0, nest_rows, 8):

        def load(shift, k, c):
            return ext[k, pl.ds((rb + 1 + shift) * chan + c, 8, stride=chan), :]

        def store(k, c, x):
            at = pl.ds(deep + rb, 8)
            moved[k, c, at, :] = x * nudge[0, k, at, :]

        plane_blocks(chan, table, planes, lane, load, store)


def nest_edges(chan, deep, table, nest, near, far, nudge, matrix, given, moved, natural, ext):
    nest_rows = nest.shape[0] // chan
    planes = nest.shape[1] // LANES
    ext_rows = nest_rows + 2 * deep
    size = deep * chan
    lane, sub = lane_ids(), sublane_ids()
    odd = lax.rem(lax.axis_index("tile"), 2) == 1
    edge = (deep + 2) * chan
    a, b = near[pl.ds(0, size), :], far[pl.ds(0, size), :]
    natural[pl.ds(0, size), :] = jnp.where(odd, a, b)
    natural[pl.ds(size, 2 * chan), :] = nest[pl.ds(0, 2 * chan), :]
    natural[pl.ds(edge, 2 * chan), :] = nest[pl.ds((nest_rows - 2) * chan, 2 * chan), :]
    natural[pl.ds(edge + 2 * chan, size), :] = jnp.where(odd, b, a)
    for half in range(2):

        def rows_at(r):
            return r if half == 0 else ext_rows - deep - 2 + r

        x = dealt(natural[pl.ds(half * edge, edge), :], matrix[...])
        for r in range(deep + 2):
            for k in range(planes):
                live = jnp.broadcast_to(nudge[2, k, pl.ds(rows_at(r), 1), :], (8, LANES))
                for g in range(chan // 8):
                    piece = x[r * chan + 8 * g : r * chan + 8 * g + 8, k * LANES : (k + 1) * LANES]
                    ext[k, pl.ds(half * edge + r * chan + 8 * g, 8), :] = piece * live

    def load(shift, k, c):
        upper = ext[k, pl.ds((1 + shift) * chan + c, 8, stride=chan), :]
        lower = ext[k, pl.ds((3 + shift) * chan + c, 8, stride=chan), :]
        return jnp.where(sub < deep, upper, lower)

    def store(k, c, x):
        low, high = pl.ds(1, deep), pl.ds(ext_rows - 1 - deep, deep)
        moved[k, c, low, :] = x[:deep] * nudge[0, k, low, :]
        moved[k, c, high, :] = x[deep:] * nudge[0, k, high, :]

    plane_blocks(chan, table, planes, lane, load, store)


def nest_rest(
    rows, chan, deep, own_rows, tiles,
    anchor, table, own, got_a, got_b, got_c, moved, nudge, back, out,
    slots, foot, coarse, state, force, done, final, sems,
):
    planes, _, ext_rows, _ = moved.shape
    nest_rows = ext_rows - 2 * deep
    groups = chan // 8
    tile = lax.axis_index("tile")
    lane, sub = lane_ids(), sublane_ids()
    first_row = nest_rows * tile - deep
    start = jnp.max(anchor[...]) + own_rows * tile - 2
    span = foot.shape[1] // chan - 1
    size = rows // 2 * chan
    part = lax.rem(lax.div(tile, 2), 2)
    side = lax.rem(tile, 2)

    slots[0] = own[...]
    for k, ref in enumerate((got_a, got_b, got_c)):
        count = ref.shape[0] - chan
        slots[k + 1, pl.ds(0, count), :] = ref[pl.ds(0, count), :]
        slots[k + 1, pl.ds(size, chan), :] = ref[pl.ds(count, chan), :]

    for m in range(span):
        row = start + m
        local = lax.bitwise_and(row, rows - 1)
        other = lax.bitwise_and(lax.shift_right_arithmetic(row, rows.bit_length() - 1), 1)
        k = 2 * lax.bitwise_xor(lax.bitwise_and(row, 1), part) + lax.bitwise_xor(other, side)
        inside = one_if((row >= 0) & (row < rows * tiles))
        slot = jnp.where(k == 0, lax.shift_right_arithmetic(local, 1), m // 2) * chan
        turn = LANES - 1 - 2 * local
        for g in range(groups):
            at = pl.ds(m * chan + 8 * g, 8)
            foot[0, at, :] = pltpu.roll(slots[k, pl.ds(size + 8 * g, 8), :] * inside, turn, axis=1)
            foot[1, at, :] = slots[k, pl.ds(aligned(slot + 8 * g, 8), 8), :] * inside

    for k in range(2):
        foot[k, pl.ds(span * chan, chan), :] = jnp.zeros((chan, LANES), F32)

    def foot_loads(c):
        def at(r):
            return pl.ds(r * chan + c, 8, stride=chan)

        v = foot[1, at(1), :]
        edge = foot[0, at(1), :]
        w, e = sides(lane, edge, v, edge)
        return v, foot[1, at(0), :], foot[1, at(2), :], w, e

    def foot_store(c, x):
        old = foot[1, pl.ds(chan + c, 8, stride=chan), :]
        coarse[0, c] = old
        coarse[1, c] = x - old

    step_blocks(chan, table, [foot_loads], [foot_store])

    share = []
    for rb in range(0, ext_rows, 8):
        p = lax.rem(sub, RATIO).astype(F32) / RATIO
        share.append(jnp.where(first_row + rb + sub >= RATIO * (own_rows * tiles - 1), 0.0, p))

    together = 6

    @pl.loop(0, chan // together)
    def _(i):
        for c in (together * i + t for t in range(together)):
            for rb in range(0, ext_rows, 8):
                u = rb // RATIO
                at = pl.ds(rb, 8)
                lines = []
                for t in range(2):
                    r0, r1, r2 = (
                        jnp.broadcast_to(coarse[t, c, pl.ds(u + n, 1), :], (8, LANES)) for n in range(3)
                    )
                    a0 = jnp.where(sub < RATIO, r0, r1)
                    a1 = jnp.where(sub < RATIO, r1, r2)
                    level = a0 + share[rb // 8] * (a1 - a0)
                    beside = jnp.where(lane == LANES - 1, level, pltpu.roll(level, LANES - 1, axis=1))
                    slope = (beside - level) * (1.0 / RATIO)
                    force[t, c, at, :] = level
                    force[2 + t, c, at, :] = slope
                    lines.append((level, slope))
                level, slope = (old + new * (1.0 / NSTEP) for old, new in zip(*lines))
                for k in range(planes):
                    g = level + float(k) * slope if k else level
                    state[0, k, c, pl.ds(8 + rb, 8), :] = moved[k, c, at, :] + nudge[1, k, at, :] * g

    def advance(step, src, rb, put):
        weight = jnp.float32(step + 1) / NSTEP
        at = pl.ds(rb, 8)
        lines = {}

        def load(shift, k, c):
            return state[src, k, c, pl.ds(8 + rb + shift, 8), :]

        def store(k, c, x):
            if c not in lines:
                lines[c] = [force[t, c, at, :] + weight * force[t + 1, c, at, :] for t in (0, 2)]
            level, slope = lines[c]
            g = level + float(k) * slope if k else level
            put(k, c, nudge[0, k, at, :] * x + nudge[1, k, at, :] * g)

        plane_blocks(chan, table, planes, lane, load, store)

    @pl.loop(1, NSTEP - 1)
    def _(step):
        src = lax.rem(step + 1, 2)

        @pl.loop(0, ext_rows // 8)
        def _(block):
            rb = aligned(block * 8, 8)

            def put(k, c, x):
                state[1 - src, k, c, pl.ds(8 + rb, 8), :] = x

            advance(step, src, rb, put)

    copies = []
    for n, rb in enumerate(range(0, nest_rows, 8)):

        def put(k, c, x):
            done[n, k, pl.ds(c, 8, stride=chan), :] = x

        advance(NSTEP - 1, NSTEP % 2, deep + rb, put)
        whole = jnp.concatenate([done[n, k] for k in range(planes)], axis=1)
        final[n] = dealt(whole, back[...])
        copies.append(
            pltpu.make_async_copy(final.at[n], out.at[pl.ds(rb * chan, 8 * chan), :], sems.at[n])
        )
        copies[n].start()
    for copy in copies:
        copy.wait()


def bound(kernel, *static):
    def run(*refs):
        return kernel(*static, *refs)

    return run


def exchange(block, axis, bit):
    return lax.ppermute(block, axis, [(i, i ^ bit) for i in range(lax.axis_size(axis))])


def exchange_both(block, sec_bit, tile_bit):
    secs, tiles = lax.axis_size("sec"), lax.axis_size("tile")
    route = [
        (s * tiles + t, (s ^ sec_bit) * tiles + (t ^ tile_bit)) for s in range(secs) for t in range(tiles)
    ]
    return lax.ppermute(block, ("sec", "tile"), route)


def body(parent_old, nest_state, diffusion, wind_speed, conversion, vert_mix, nest_box):
    rows, chan, cols = parent_old.shape
    nest_rows, nest_cols = nest_state.shape[1], nest_state.shape[3]
    secs, tiles = lax.axis_size("sec"), lax.axis_size("tile")
    own_rows = nest_rows // RATIO
    levels = conversion.shape[1]
    deep = NSTEP
    ext_rows = nest_rows + 2 * deep
    col_blocks = nest_cols // LANES
    blocks = cols // LANES
    span = (ext_rows // RATIO + 1) + 2
    strip_rows = (rows + 1) * chan
    half_rows = (rows // 2 + 1) * chan
    parent = parent_old.reshape(rows * chan, cols)
    nest = nest_state.reshape(nest_rows * chan, nest_cols)
    half = shape(half_rows, LANES)

    halo = shape((deep + cols // nest_cols) * chan, nest_cols)
    near, far = call(
        bound(edge_rows, deep, chan), [halo] * 2, (nest, parent), (ANY, ANY),
        scratch=[pltpu.SemaphoreType.DMA((2 * (1 + cols // nest_cols),))], limit=4, cost=1 << 20,
    )
    near = exchange(near, "tile", 1)
    beside = [(i, i + 1) for i in range(1, tiles - 1, 2)]
    far = lax.ppermute(far, "tile", beside + [(j, i) for i, j in beside])

    some = shape(secs // 2, strip_rows, LANES)
    keep, send, anchor = call(
        bound(extract, rows, chan), [some, some, shape(8, LANES, dtype=jnp.int32)],
        (nest_box, parent), (HBM, HBM), cost=4 << 20,
        scratch=[
            pltpu.SMEM(nest_box.shape, jnp.int32),
            pltpu.VMEM(parent.shape, F32),
            pltpu.SemaphoreType.DMA((2,)),
        ],
    )
    got = exchange(send, "sec", 1)
    bit = 2
    while bit < secs // 2:
        some = shape(secs // (2 * bit), strip_rows, LANES)
        keep, send = call(bound(combine, bit), [some, some], (keep, got), (VMEM, VMEM), cost=1 << 20)
        got = exchange(send, "sec", bit)
        bit *= 2
    mine, to_sec, to_tile, to_both = call(
        bound(split, rows, chan), [half] * 4, (keep, got), (VMEM, VMEM), cost=1 << 18,
    )
    from_sec = exchange_both(to_sec, secs // 2, 0)
    from_tile = exchange_both(to_tile, 0, 2)
    from_both = exchange_both(to_both, secs // 2, 2)
    moved_shape = shape(col_blocks, chan, ext_rows, LANES)
    square = (nest_cols, nest_cols)
    moved, nudge, back, matrix, table = call(
        bound(nest_first, chan, deep),
        [moved_shape, shape(3, col_blocks, ext_rows, LANES), shape(*square, dtype=jnp.bfloat16),
         shape(*square, dtype=jnp.bfloat16), shape(table_rows(chan, levels), LANES)],
        (nest_box, diffusion, wind_speed, conversion, vert_mix, nest), (SMEM,) * 5 + (VMEM,), cost=6 << 20,
        scratch=[
            pltpu.VMEM((col_blocks, (nest_rows + 2) * chan, LANES), F32),
        ],
    )

    two = shape(2, half_rows, LANES)
    (strip,) = call(
        gathered, [two], (mine, from_sec, from_tile, from_both, moved), (VMEM,) * 5, cost=1 << 18,
    )
    pair = strip
    group = tiles // 2
    while group > 4:
        got = exchange(pair, "tile", group)
        (pair,) = call(
            bound(choose, rows, own_rows, group, tiles), [two], (anchor, pair, got), (VMEM,) * 3, cost=1 << 18,
        )
        group //= 2
    mine, sent = call(
        bound(select, rows, chan, own_rows, tiles), [half] * 2, (anchor, pair), (VMEM,) * 2, cost=1 << 18,
    )
    got = exchange(sent, "tile", 4)
    edge = shape(2, blocks * chan, LANES)
    parent_new, edges = call(
        bound(parent_step, rows, chan), [shape(rows * chan, cols), edge],
        (table, parent, strip), (VMEM,) * 3, cost=8 << 20, out_specs=[ANY, VMEM],
        scratch=[
            pltpu.VMEM((blocks + 2, (rows + 2) * chan, LANES), F32),
            pltpu.VMEM((blocks, rows * chan, LANES), F32),
            pltpu.SemaphoreType.DMA((blocks,)),
        ],
    )

    message = shape(((span + 1) // 2 + 1) * chan, LANES)
    own, *sent = call(
        bound(settle, rows, chan, own_rows, tiles), [half] + [message] * 3,
        (anchor, mine, got, near, edges), (VMEM,) * 5, cost=1 << 18,
    )
    got_a, got_b, got_c = (exchange(block, "tile", k + 1) for k, block in enumerate(sent))

    (parent_new,) = call(
        bound(parent_edges, rows, chan, deep), [shape(rows * chan, cols)],
        (table, near, far, edges, parent_new), (VMEM,) * 4 + (ANY,), cost=1 << 20, out_specs=[ANY], same={4: 0},
        scratch=[
            pltpu.VMEM((2, blocks * chan, LANES), F32),
            pltpu.VMEM((2, blocks * chan, LANES), F32),
            pltpu.SemaphoreType.DMA((2 * blocks,)),
        ],
    )
    (moved,) = call(
        bound(nest_edges, chan, deep), [moved_shape],
        (table, nest, near, far, nudge, matrix, moved), (VMEM,) * 7, cost=3 << 20, same={6: 0},
        scratch=[
            pltpu.VMEM((2 * (deep + 2) * chan, nest_cols), F32),
            pltpu.VMEM((col_blocks, 2 * (deep + 2) * chan, LANES), F32),
        ],
    )

    (nest_new,) = call(
        bound(nest_rest, rows, chan, deep, own_rows, tiles), [shape(nest_rows * chan, nest_cols)],
        (anchor, table, own, got_a, got_b, got_c, moved, nudge, back), (VMEM,) * 9, cost=16 << 20, out_specs=[ANY],
        limit=32,
        scratch=[
            pltpu.VMEM((4, half_rows, LANES), F32),
            pltpu.VMEM((2, (span + 1) * chan, LANES), F32),
            pltpu.VMEM((2, chan, 8, LANES), F32),
            pltpu.VMEM((2, col_blocks, chan, ext_rows + 16, LANES), F32),
            pltpu.VMEM((4, chan, ext_rows, LANES), F32),
            pltpu.VMEM((nest_rows // 8, col_blocks, 8 * chan, LANES), F32),
            pltpu.VMEM((nest_rows // 8, 8 * chan, nest_cols), F32),
            pltpu.SemaphoreType.DMA((nest_rows // 8,)),
        ],
    )

    return parent_new.reshape(parent_old.shape), nest_new.reshape(nest_state.shape)


def solution(mesh):
    placed = (P("tile", None, "sec"), P("sec", "tile", None, None), P(), P(), P(), P(), P())
    return jax.shard_map(
        body,
        mesh=mesh,
        in_specs=placed,
        out_specs=(P("tile", None, "sec"), P("sec", "tile", None, None)),
        check_vma=False,
    )
```

```python
import jax
import jax.numpy as jnp
from jax import lax
from jax.experimental import pallas as pl
from jax.experimental.pallas import tpu as pltpu
from jax.sharding import PartitionSpec as P

NSTEP = 4
RATIO = 4
LANES = 128
F32 = jnp.float32
VMEM = pl.BlockSpec(memory_space=pltpu.VMEM)
SMEM = pl.BlockSpec(memory_space=pltpu.SMEM)
ANY = pl.BlockSpec(memory_space=pl.ANY)
HBM = pl.BlockSpec(memory_space=pltpu.HBM)
TOGETHER = 8


def call(kernel, outs, args, specs, scratch=(), limit=16, cost=0, out_specs=None, same=None):
    return pl.pallas_call(
        kernel,
        out_shape=list(outs),
        in_specs=list(specs),
        out_specs=[VMEM] * len(outs) if out_specs is None else out_specs,
        scratch_shapes=list(scratch),
        input_output_aliases=same or {},
        compiler_params=pltpu.CompilerParams(vmem_limit_bytes=limit << 20),
        cost_estimate=pl.CostEstimate(flops=0, bytes_accessed=cost, transcendentals=0),
    )(*args)


def shape(*dims, dtype=F32):
    return jax.ShapeDtypeStruct(dims, dtype)


def lane_ids():
    return lax.broadcasted_iota(jnp.int32, (8, LANES), 1)


def sublane_ids():
    return lax.broadcasted_iota(jnp.int32, (8, LANES), 0)


def one_if(condition):
    return jnp.where(condition, 1.0, 0.0).astype(F32)


def aligned(start, step):
    return pl.multiple_of(start, step)


def edge_rows(deep, chan, nest, parent, near, far, sems):
    odd = lax.rem(lax.axis_index("tile"), 2)
    cols = nest.shape[1]
    copies = []
    for k, (dest, last) in enumerate(((near, 1 - odd), (far, odd))):
        size = deep * chan
        at = aligned(last * (nest.shape[0] - size), 8)
        copies.append((nest.at[pl.ds(at, size), :], dest.at[pl.ds(0, size), :]))
        at = aligned(last * (parent.shape[0] - chan), 8)
        for part in range(parent.shape[1] // cols):
            source = parent.at[pl.ds(at, chan), pl.ds(part * cols, cols)]
            copies.append((source, dest.at[pl.ds(size + part * chan, chan), :]))
    made = [pltpu.make_async_copy(a, b, sems.at[i]) for i, (a, b) in enumerate(copies)]
    for copy in made:
        copy.start()
    for copy in made:
        copy.wait()


def extract(rows, chan, box_in, parent_in, keep, send, anchor, box, parent, sems):
    copies = [
        pltpu.make_async_copy(box_in, box, sems.at[0]),
        pltpu.make_async_copy(parent_in, parent, sems.at[1]),
    ]
    for copy in copies:
        copy.start()
    for copy in copies:
        copy.wait()
    cols = parent.shape[1]
    blocks = cols // LANES
    groups = chan // 8
    sec = lax.axis_index("sec")
    half = lax.rem(sec, 2)
    lane = lane_ids()
    anchor[...] = jnp.full((8, LANES), box[sec, 0], jnp.int32)

    def at(row, g):
        return pl.ds(aligned(row * chan + 8 * g, 8), 8)

    lane_row = lax.div(lane, 2)
    together = TOGETHER

    def outer(step, packed):
        packed = list(packed)
        for k in range(together):
            row = step * together + k
            for g in range(groups):
                ends = jnp.where(
                    lane < LANES // 2,
                    parent[at(row, g), pl.ds(0, LANES)],
                    parent[at(row, g), pl.ds(cols - LANES, LANES)],
                )
                ends = pltpu.roll(ends, 2 * rows + 2 * row + 1, axis=1)
                packed[g] = jnp.where(lane_row == rows + row, ends, packed[g])
        return tuple(packed)

    zeros = (jnp.zeros((8, LANES), F32),) * groups
    halo = lax.fori_loop(0, rows // together, outer, zeros)

    for which, dest in ((1 - half, send), (half, keep)):

        @pl.loop(0, dest.shape[0])
        def _(i):
            nest = 2 * i + which
            offset = box[nest, 1] - sec * cols
            shift = lax.bitwise_and(offset, LANES - 1)
            back = lax.bitwise_and(LANES - shift, LANES - 1)

            def place(k):
                start = aligned(jnp.clip(k, 0, blocks - 1) * LANES, LANES)
                return pl.ds(start, LANES), one_if((k >= 0) & (k < blocks))

            first = lax.shift_right_arithmetic(offset, 7)
            at_a, on_a = place(first)
            at_b, on_b = place(first + 1)
            at_c, on_c = place(lax.shift_right_arithmetic(offset - 1, 7))
            before = lax.bitwise_and(lane - shift, LANES - 1) >= LANES // 2
            sent = jnp.where(lax.rem(lane, 2) == 0, one_if(nest == sec + 1), one_if(nest == sec - 1))

            def inner(step, packed):
                packed = list(packed)
                shifted = []
                for k in range(together):
                    row = step * together + k
                    turn = lax.bitwise_and(back + 2 * row + 1, LANES - 1)
                    for g in range(groups):
                        a = parent[at(row, g), at_a] * on_a
                        b = parent[at(row, g), at_b] * on_b
                        c = parent[at(row, g), at_c] * on_c
                        main = pltpu.roll(jnp.where(lane < shift, b, a), back, axis=1)
                        shifted.append((at(row, g), main))
                        side = pltpu.roll(jnp.where(before, c, b), turn, axis=1)
                        packed[g] = jnp.where(lane_row == row, side, packed[g])
                for where, main in shifted:
                    dest[i, where, :] = main
                return tuple(packed)

            here = (offset >= -LANES) & (offset <= cols)

            @pl.when(here)
            def _():
                packed = lax.fori_loop(0, rows // together, inner, tuple(h * sent for h in halo))
                for g in range(groups):
                    dest[i, pl.ds(rows * chan + 8 * g, 8), :] = packed[g]

            @pl.when(jnp.logical_not(here))
            def _():
                dest[i, pl.ds(0, rows * chan), :] = jnp.zeros((rows * chan, LANES), F32)
                for g in range(groups):
                    dest[i, pl.ds(rows * chan + 8 * g, 8), :] = halo[g] * sent


def combine(bit, own, got, keep, send):
    mine = lax.rem(lax.axis_index("sec") // bit, 2)
    for i in range(keep.shape[0]):
        send[i] = own[2 * i + 1 - mine] + got[2 * i + 1 - mine]
        keep[i] = own[2 * i + mine] + got[2 * i + mine]


def split(rows, chan, own, got, mine, to_sec, to_tile, to_both):
    sec = lax.div(lax.axis_index("sec"), lax.axis_size("sec") // 2)
    part = lax.rem(lax.div(lax.axis_index("tile"), 2), 2)
    size = rows // 2 * chan
    for dest, nest, half in (
        (to_sec, 1 - sec, part),
        (to_both, 1 - sec, 1 - part),
        (to_tile, sec, 1 - part),
        (mine, sec, part),
    ):
        for j in range(rows // 2):
            at = pl.ds(aligned((2 * j + half) * chan, 8), chan)
            dest[pl.ds(j * chan, chan), :] = own[nest, at, :] + got[nest, at, :]
        at = pl.ds(rows * chan, chan)
        dest[pl.ds(size, chan), :] = own[nest, at, :] + got[nest, at, :]


def gathered(mine, from_sec, from_tile, from_both, moved, out):
    out[0] = mine[...] + from_sec[...]
    out[1] = from_tile[...] + from_both[...]


def held_block(anchor, tile, rows, own_rows, group):
    first = lax.div(tile, group) * group
    low = jnp.maximum(anchor + (own_rows * first - 2), 0)
    base = lax.shift_right_arithmetic(low, rows.bit_length() - 1)
    return base + lax.bitwise_and(tile - base, group - 1)


def held(anchor, tile, rows, own_rows, group, tiles):
    if group == tiles:
        return jnp.full((8, LANES), tile, jnp.int32)
    return held_block(anchor, tile, rows, own_rows, group)


def choose(rows, own_rows, group, tiles, anchor, own, got, out):
    start = anchor[...]
    for k in range(2):
        tile = lax.bitwise_xor(lax.axis_index("tile"), 2 * k)
        keep = held(start, tile, rows, own_rows, 2 * group, tiles) == held_block(
            start, tile, rows, own_rows, group
        )
        for r in range(0, out.shape[1], 8):
            at = pl.ds(r, 8)
            out[k, at, :] = jnp.where(keep, own[k, at, :], got[k, at, :])


def wanted(anchor, row, tile, group, own_rows):
    first = lax.div(tile, group) * group
    low = anchor + (own_rows * first - 2)
    return (row >= low) & (row <= low + own_rows * group + 4)


def slot_rows(rows, own_rows, tiles, anchor):
    tile = lax.axis_index("tile")
    return [
        rows * held(anchor, lax.bitwise_xor(tile, 2 * k), rows, own_rows, 8, tiles) for k in range(2)
    ]


def select(rows, chan, own_rows, tiles, anchor, both, mine, sent):
    start = anchor[...]
    tile = lax.axis_index("tile")
    part = lax.rem(lax.div(tile, 2), 2)
    size = rows // 2 * chan
    base = slot_rows(rows, own_rows, tiles, start)
    lane_row = lax.div(lane_ids(), 2)
    for dest, owner in ((sent, lax.bitwise_xor(tile, 4)), (mine, tile)):
        for j in range(rows // 2 + 1):
            row = lane_row if j == rows // 2 else 2 * j + part
            second = wanted(start, base[1] + row, owner, 4, own_rows)
            for g in range(chan // 8):
                at = pl.ds(j * chan + 8 * g, 8)
                dest[at, :] = jnp.where(second, both[1, at, :], both[0, at, :])


def settle(rows, chan, own_rows, tiles, anchor, mine, got, near, parent, out, *sent):
    start = anchor[...]
    tile = lax.axis_index("tile")
    part = lax.rem(lax.div(tile, 2), 2)
    base = slot_rows(rows, own_rows, tiles, start)
    lane_row = lax.div(lane_ids(), 2)
    groups = range(chan // 8)
    slots = rows // 2
    held_rows = {}
    for j in range(slots + 1):
        row = lane_row if j == slots else 2 * j + part
        keep = wanted(start, base[0] + row, tile, 4, own_rows)
        keep = keep | wanted(start, base[1] + row, tile, 4, own_rows)
        for g in groups:
            at = pl.ds(j * chan + 8 * g, 8)
            held_rows[j, g] = jnp.where(keep, mine[at, :], got[at, :])
            out[at, :] = held_rows[j, g]
    for k, dest in enumerate(sent):
        count = dest.shape[0] // chan - 1
        first = start + (own_rows * lax.bitwise_xor(tile, k + 1) - 2)
        first = lax.shift_right_arithmetic(first + lax.bitwise_and(lax.bitwise_xor(first, part), 1), 1)
        for i in range(count):
            slot = lax.bitwise_and(first + i, slots - 1)
            row = [held_rows[0, g] for g in groups]
            for j in range(1, slots):
                row = [jnp.where(slot == j, held_rows[j, g], row[g]) for g in groups]
            for g in groups:
                dest[pl.ds(i * chan + 8 * g, 8), :] = row[g]
        for g in groups:
            dest[pl.ds(count * chan + 8 * g, 8), :] = held_rows[slots, g]


def table_rows(chan, levels):
    return 4 * chan + 2 * levels + chan


def make_table(diff, wind, conv, mix, table):
    chan, levels = diff.shape[0], conv.shape[1]

    def line(value):
        return jnp.full((1, LANES), value, F32)

    def put(i, value):
        table[pl.ds(i, 1), :] = value

    scale = {}
    for f in range(3):
        m = line(mix[f])
        ratio = None
        for l in range(levels):
            c = f * levels + l
            pivot = 1.0 + (1.0 if l in (0, levels - 1) else 2.0) * m
            if l:
                pivot = pivot - m * ratio
            inverse = 1.0 / pivot
            ratio = m * inverse
            put(4 * chan + 2 * levels + c, ratio)
            scale[c] = inverse * (1.0 - line(conv[f, l])) if f < 2 else inverse
            d, wx, wy = diff[c], wind[0, c], wind[1, c]
            for k, value in enumerate((1.0 - 4.0 * d - wx - wy, d + wx, d + wy, d)):
                put(4 * c + k, scale[c] * line(value))
            if f:
                before = c - levels
                put(4 * chan + before, scale[c] * line(conv[f - 1, l]) / scale[before])


def rows_of(table):
    def coef(i):
        return jnp.broadcast_to(table[pl.ds(i, 1), :], (8, LANES))

    return coef


def step_blocks(chan, table, loads, stores):
    coef = rows_of(table)

    def horizontal(c):
        center, above, left, spread = (coef(4 * c + k) for k in range(4))
        out = []
        for load in loads:
            v, n, s, w, e = load(c)
            out.append(center * v + above * n + left * w + spread * (s + e))
        return out

    mix_blocks(chan, table, horizontal, stores)


def mix_blocks(chan, table, fields, stores):
    levels = chan // 3
    blocks = range(len(stores))
    coef = rows_of(table)
    ys = {}
    for l in range(levels):
        for f in range(3):
            c = f * levels + l
            row = fields(c)
            if f:
                rate = coef(4 * chan + c - levels)
                row = [row[b] + rate * given[b] for b in blocks]
            given = row
            if l:
                ratio = coef(4 * chan + 2 * levels + c)
                row = [row[b] + ratio * ys[c - 1][b] for b in blocks]
            ys[c] = row
    xs = {}
    for l in range(levels - 1, -1, -1):
        for f in range(3):
            c = f * levels + l
            xs[f] = ys[c] if l == levels - 1 else [
                ys[c][b] + coef(4 * chan + 2 * levels + c) * xs[f][b] for b in blocks
            ]
            for b in blocks:
                stores[b](c, xs[f][b])


def sides(lane, west, v, east):
    w = pltpu.roll(jnp.where(lane == LANES - 1, west, v), 1, axis=1)
    e = pltpu.roll(jnp.where(lane == 0, east, v), LANES - 1, axis=1)
    return w, e


def parent_step(rows, chan, table, parent, strip, out, edges, ext, done, sems):
    blocks = parent.shape[1] // LANES
    groups = chan // 8
    lane = lane_ids()
    packed_at = strip.shape[1] - chan

    def columns(j):
        return pl.ds(aligned(j * LANES, LANES), LANES)

    packed = [strip[0, pl.ds(packed_at + 8 * g, 8), :] for g in range(groups)]

    @pl.loop(0, rows)
    def _(row):
        for g in range(groups):
            at = pl.ds(aligned((row + 1) * chan + 8 * g, 8), 8)
            turn = LANES - 1 - 2 * rows - 2 * row
            turned = pltpu.roll(packed[g], turn, axis=1)
            ext[0, at, :] = turned
            ext[blocks + 1, at, :] = turned

    @pl.loop(0, blocks)
    def _(j):
        ext[j + 1, pl.ds(chan, rows * chan), :] = parent[:, columns(j)]
        ext[j + 1, pl.ds(0, chan), :] = jnp.zeros((chan, LANES), F32)
        ext[j + 1, pl.ds((rows + 1) * chan, chan), :] = jnp.zeros((chan, LANES), F32)

    @pl.loop(0, blocks)
    def _(j):
        def block(first):
            def loads(c):
                def at(r):
                    return pl.ds((first + r) * chan + c, 8, stride=chan)

                v = ext[j + 1, at(1), :]
                w, e = sides(lane, ext[j, at(1), :], v, ext[j + 2, at(1), :])
                return v, ext[j + 1, at(0), :], ext[j + 1, at(2), :], w, e

            def store(c, x):
                done[j, pl.ds(first * chan + c, 8, stride=chan), :] = x

            return loads, store

        loads, stores = zip(*(block(first) for first in range(0, rows, 8)))
        step_blocks(chan, table, loads, stores)
        at = pl.ds(aligned(j * chan, 8), chan)
        edges[0, at, :] = done[j, pl.ds(0, chan), :]
        edges[1, at, :] = done[j, pl.ds((rows - 1) * chan, chan), :]
        pltpu.make_async_copy(done.at[j], out.at[:, columns(j)], sems.at[j]).start()

    @pl.loop(0, blocks)
    def _(j):
        pltpu.make_async_copy(done.at[j], out.at[:, columns(j)], sems.at[j]).wait()


def parent_edges(rows, chan, deep, table, near, far, edges, given, out, beside, done, sems):
    blocks = edges.shape[1] // chan
    per = near.shape[1] // LANES
    odd = lax.rem(lax.axis_index("tile"), 2) == 1
    for j in range(blocks):
        for g in range(chan // 8):
            at = pl.ds((deep + j // per) * chan + 8 * g, 8)
            a, b = (ref[at, pl.ds(j % per * LANES, LANES)] for ref in (near, far))
            at = pl.ds(j * chan + 8 * g, 8)
            beside[0, at, :] = jnp.where(odd, a, b)
            beside[1, at, :] = jnp.where(odd, b, a)
    coef = rows_of(table)
    pieces = [(k, b) for k in range(2) for b in range(0, blocks, 8)]

    def at(b, c):
        return pl.ds(b * chan + c, 8, stride=chan)

    def fields(c):
        return [coef(4 * c + (1, 3)[k]) * beside[k, at(b, c), :] for k, b in pieces]

    def storing(k, b):
        def store(c, x):
            done[k, at(b, c), :] = edges[k, at(b, c), :] + x

        return store

    mix_blocks(chan, table, fields, [storing(k, b) for k, b in pieces])
    copies = []
    for k, row in enumerate((0, rows - 1)):
        for j in range(blocks):
            copies.append(
                pltpu.make_async_copy(
                    done.at[k, pl.ds(j * chan, chan), :],
                    out.at[pl.ds(row * chan, chan), pl.ds(j * LANES, LANES)],
                    sems.at[k * blocks + j],
                )
            )
    for copy in copies:
        copy.start()
    for copy in copies:
        copy.wait()


def dealing(cols, back):
    first = lax.broadcasted_iota(jnp.int32, (cols, cols), 0)
    second = lax.broadcasted_iota(jnp.int32, (cols, cols), 1)
    planes = cols // LANES
    natural, dealt = (second, first) if back else (first, second)
    hit = natural == planes * lax.bitwise_and(dealt, LANES - 1) + lax.shift_right_arithmetic(dealt, 7)
    return jnp.where(hit, 1.0, 0.0).astype(jnp.bfloat16)


def dealt(x, matrix):
    out = None
    for _ in range(3):
        part = x.astype(jnp.bfloat16)
        x = x - part.astype(F32)
        term = jnp.dot(part, matrix, preferred_element_type=F32)
        out = term if out is None else out + term
    return out


def plane_blocks(chan, table, planes, lane, load, store):
    cache = {}

    def center(k, c):
        if (k, c) not in cache:
            cache[k, c] = load(0, k, c)
        return cache[k, c]

    def block(k):
        def loads(c):
            if k == 0:
                w = jnp.where(lane == 0, 0.0, pltpu.roll(center(planes - 1, c), 1, axis=1))
            else:
                w = center(k - 1, c)
            if k == planes - 1:
                e = jnp.where(lane == LANES - 1, 0.0, pltpu.roll(center(0, c), LANES - 1, axis=1))
            else:
                e = center(k + 1, c)
            return center(k, c), load(-1, k, c), load(1, k, c), w, e

        def put(c, x):
            store(k, c, x)

        return loads, put

    loads, stores = zip(*(block(k) for k in range(planes)))
    step_blocks(chan, table, loads, stores)


def nest_first(chan, deep, box, diff, wind, conv, mix, nest, moved, nudge, back, matrix, table, ext):
    make_table(diff, wind, conv, mix, table)
    nest_rows = nest.shape[0] // chan
    planes = nest.shape[1] // LANES
    ext_rows = nest_rows + 2 * deep
    groups = chan // 8
    sec, tile = lax.axis_index("sec"), lax.axis_index("tile")
    extent_x, extent_y = box[sec, 2], box[sec, 3]
    lane, sub = lane_ids(), sublane_ids()
    first_row = nest_rows * tile - deep
    matrix[...] = dealing(nest.shape[1], False)
    back[...] = dealing(nest.shape[1], True)
    for k in range(planes):
        col = planes * lane + k
        for rb in range(0, ext_rows, 8):
            i = first_row + rb + sub
            live = one_if((i >= 0) & (i < extent_x) & (col < extent_y))
            dist = jnp.minimum(jnp.minimum(i, col), jnp.minimum(extent_x - 1 - i, extent_y - 1 - col))
            dist = jnp.maximum(dist, 0).astype(F32)
            rate = 0.1 + 0.4 * jnp.exp(-dist / 3.0)
            nudge[0, k, pl.ds(rb, 8), :] = live * (1.0 - rate)
            nudge[1, k, pl.ds(rb, 8), :] = live * rate
            nudge[2, k, pl.ds(rb, 8), :] = live

    together = nest_rows

    @pl.loop(0, nest_rows // together)
    def _(step):
        size = together * chan
        x = dealt(nest[pl.ds(aligned(step * size, 8), size), :], matrix[...])
        for r in range(together):
            row = step * together + r
            for k in range(planes):
                live = jnp.broadcast_to(nudge[2, k, pl.ds(deep + row, 1), :], (8, LANES))
                for g in range(groups):
                    piece = x[r * chan + 8 * g : r * chan + 8 * g + 8, k * LANES : (k + 1) * LANES]
                    ext[k, pl.ds(aligned((row + 1) * chan + 8 * g, 8), 8), :] = piece * live

    for row in (0, nest_rows + 1):
        ext[:, pl.ds(row * chan, chan), :] = jnp.zeros((planes, chan, LANES), F32)
    for rb in range(0, nest_rows, 8):

        def load(shift, k, c):
            return ext[k, pl.ds((rb + 1 + shift) * chan + c, 8, stride=chan), :]

        def store(k, c, x):
            at = pl.ds(deep + rb, 8)
            moved[k, c, at, :] = x * nudge[0, k, at, :]

        plane_blocks(chan, table, planes, lane, load, store)


def nest_edges(chan, deep, table, nest, near, far, nudge, matrix, given, moved, natural, ext):
    nest_rows = nest.shape[0] // chan
    planes = nest.shape[1] // LANES
    ext_rows = nest_rows + 2 * deep
    size = deep * chan
    lane, sub = lane_ids(), sublane_ids()
    odd = lax.rem(lax.axis_index("tile"), 2) == 1
    edge = (deep + 2) * chan
    a, b = near[pl.ds(0, size), :], far[pl.ds(0, size), :]
    natural[pl.ds(0, size), :] = jnp.where(odd, a, b)
    natural[pl.ds(size, 2 * chan), :] = nest[pl.ds(0, 2 * chan), :]
    natural[pl.ds(edge, 2 * chan), :] = nest[pl.ds((nest_rows - 2) * chan, 2 * chan), :]
    natural[pl.ds(edge + 2 * chan, size), :] = jnp.where(odd, b, a)
    for half in range(2):

        def rows_at(r):
            return r if half == 0 else ext_rows - deep - 2 + r

        x = dealt(natural[pl.ds(half * edge, edge), :], matrix[...])
        for r in range(deep + 2):
            for k in range(planes):
                live = jnp.broadcast_to(nudge[2, k, pl.ds(rows_at(r), 1), :], (8, LANES))
                for g in range(chan // 8):
                    piece = x[r * chan + 8 * g : r * chan + 8 * g + 8, k * LANES : (k + 1) * LANES]
                    ext[k, pl.ds(half * edge + r * chan + 8 * g, 8), :] = piece * live

    def load(shift, k, c):
        upper = ext[k, pl.ds((1 + shift) * chan + c, 8, stride=chan), :]
        lower = ext[k, pl.ds((3 + shift) * chan + c, 8, stride=chan), :]
        return jnp.where(sub < deep, upper, lower)

    def store(k, c, x):
        low, high = pl.ds(1, deep), pl.ds(ext_rows - 1 - deep, deep)
        moved[k, c, low, :] = x[:deep] * nudge[0, k, low, :]
        moved[k, c, high, :] = x[deep:] * nudge[0, k, high, :]

    plane_blocks(chan, table, planes, lane, load, store)


def nest_rest(
    rows, chan, deep, own_rows, tiles,
    anchor, table, own, got_a, got_b, got_c, moved, nudge, back, out,
    slots, foot, coarse, state, force, done, final, sems,
):
    planes, _, ext_rows, _ = moved.shape
    nest_rows = ext_rows - 2 * deep
    groups = chan // 8
    tile = lax.axis_index("tile")
    lane, sub = lane_ids(), sublane_ids()
    first_row = nest_rows * tile - deep
    start = jnp.max(anchor[...]) + own_rows * tile - 2
    span = foot.shape[1] // chan - 1
    size = rows // 2 * chan
    part = lax.rem(lax.div(tile, 2), 2)
    side = lax.rem(tile, 2)

    slots[0] = own[...]
    for k, ref in enumerate((got_a, got_b, got_c)):
        count = ref.shape[0] - chan
        slots[k + 1, pl.ds(0, count), :] = ref[pl.ds(0, count), :]
        slots[k + 1, pl.ds(size, chan), :] = ref[pl.ds(count, chan), :]

    for m in range(span):
        row = start + m
        local = lax.bitwise_and(row, rows - 1)
        other = lax.bitwise_and(lax.shift_right_arithmetic(row, rows.bit_length() - 1), 1)
        k = 2 * lax.bitwise_xor(lax.bitwise_and(row, 1), part) + lax.bitwise_xor(other, side)
        inside = one_if((row >= 0) & (row < rows * tiles))
        slot = jnp.where(k == 0, lax.shift_right_arithmetic(local, 1), m // 2) * chan
        turn = LANES - 1 - 2 * local
        for g in range(groups):
            at = pl.ds(m * chan + 8 * g, 8)
            foot[0, at, :] = pltpu.roll(slots[k, pl.ds(size + 8 * g, 8), :] * inside, turn, axis=1)
            foot[1, at, :] = slots[k, pl.ds(aligned(slot + 8 * g, 8), 8), :] * inside

    for k in range(2):
        foot[k, pl.ds(span * chan, chan), :] = jnp.zeros((chan, LANES), F32)

    def foot_loads(c):
        def at(r):
            return pl.ds(r * chan + c, 8, stride=chan)

        v = foot[1, at(1), :]
        edge = foot[0, at(1), :]
        w, e = sides(lane, edge, v, edge)
        return v, foot[1, at(0), :], foot[1, at(2), :], w, e

    def foot_store(c, x):
        old = foot[1, pl.ds(chan + c, 8, stride=chan), :]
        coarse[0, c] = old
        coarse[1, c] = x - old

    step_blocks(chan, table, [foot_loads], [foot_store])

    share = []
    for rb in range(0, ext_rows, 8):
        p = lax.rem(sub, RATIO).astype(F32) / RATIO
        share.append(jnp.where(first_row + rb + sub >= RATIO * (own_rows * tiles - 1), 0.0, p))

    together = 12

    @pl.loop(0, chan // together)
    def _(i):
        for c in (together * i + t for t in range(together)):
            for rb in range(0, ext_rows, 8):
                u = rb // RATIO
                at = pl.ds(rb, 8)
                lines = []
                for t in range(2):
                    r0, r1, r2 = (
                        jnp.broadcast_to(coarse[t, c, pl.ds(u + n, 1), :], (8, LANES)) for n in range(3)
                    )
                    a0 = jnp.where(sub < RATIO, r0, r1)
                    a1 = jnp.where(sub < RATIO, r1, r2)
                    level = a0 + share[rb // 8] * (a1 - a0)
                    beside = jnp.where(lane == LANES - 1, level, pltpu.roll(level, LANES - 1, axis=1))
                    slope = (beside - level) * (1.0 / RATIO)
                    force[t, c, at, :] = level
                    force[2 + t, c, at, :] = slope
                    lines.append((level, slope))
                level, slope = (old + new * (1.0 / NSTEP) for old, new in zip(*lines))
                for k in range(planes):
                    g = level + float(k) * slope if k else level
                    state[0, k, c, pl.ds(8 + rb, 8), :] = moved[k, c, at, :] + nudge[1, k, at, :] * g

    def advance(step, src, rb, put):
        weight = jnp.float32(step + 1) / NSTEP
        at = pl.ds(rb, 8)
        lines = {}

        def load(shift, k, c):
            return state[src, k, c, pl.ds(8 + rb + shift, 8), :]

        def store(k, c, x):
            if c not in lines:
                lines[c] = [force[t, c, at, :] + weight * force[t + 1, c, at, :] for t in (0, 2)]
            level, slope = lines[c]
            g = level + float(k) * slope if k else level
            put(k, c, nudge[0, k, at, :] * x + nudge[1, k, at, :] * g)

        plane_blocks(chan, table, planes, lane, load, store)

    @pl.loop(1, NSTEP - 1)
    def _(step):
        src = lax.rem(step + 1, 2)

        @pl.loop(0, ext_rows // 8)
        def _(block):
            rb = aligned(block * 8, 8)

            def put(k, c, x):
                state[1 - src, k, c, pl.ds(8 + rb, 8), :] = x

            advance(step, src, rb, put)

    copies = []
    for n, rb in enumerate(range(0, nest_rows, 8)):

        def put(k, c, x):
            done[n, k, pl.ds(c, 8, stride=chan), :] = x

        advance(NSTEP - 1, NSTEP % 2, deep + rb, put)
        whole = jnp.concatenate([done[n, k] for k in range(planes)], axis=1)
        final[n] = dealt(whole, back[...])
        copies.append(
            pltpu.make_async_copy(final.at[n], out.at[pl.ds(rb * chan, 8 * chan), :], sems.at[n])
        )
        copies[n].start()
    for copy in copies:
        copy.wait()


def bound(kernel, *static):
    def run(*refs):
        return kernel(*static, *refs)

    return run


def exchange(block, axis, bit):
    return lax.ppermute(block, axis, [(i, i ^ bit) for i in range(lax.axis_size(axis))])


def exchange_both(block, sec_bit, tile_bit):
    secs, tiles = lax.axis_size("sec"), lax.axis_size("tile")
    route = [
        (s * tiles + t, (s ^ sec_bit) * tiles + (t ^ tile_bit)) for s in range(secs) for t in range(tiles)
    ]
    return lax.ppermute(block, ("sec", "tile"), route)


def body(parent_old, nest_state, diffusion, wind_speed, conversion, vert_mix, nest_box):
    rows, chan, cols = parent_old.shape
    nest_rows, nest_cols = nest_state.shape[1], nest_state.shape[3]
    secs, tiles = lax.axis_size("sec"), lax.axis_size("tile")
    own_rows = nest_rows // RATIO
    levels = conversion.shape[1]
    deep = NSTEP
    ext_rows = nest_rows + 2 * deep
    col_blocks = nest_cols // LANES
    blocks = cols // LANES
    span = (ext_rows // RATIO + 1) + 2
    strip_rows = (rows + 1) * chan
    half_rows = (rows // 2 + 1) * chan
    parent = parent_old.reshape(rows * chan, cols)
    nest = nest_state.reshape(nest_rows * chan, nest_cols)
    half = shape(half_rows, LANES)

    halo = shape((deep + cols // nest_cols) * chan, nest_cols)
    near, far = call(
        bound(edge_rows, deep, chan), [halo] * 2, (nest, parent), (ANY, ANY),
        scratch=[pltpu.SemaphoreType.DMA((2 * (1 + cols // nest_cols),))], limit=4, cost=1 << 20,
    )
    near = exchange(near, "tile", 1)
    beside = [(i, i + 1) for i in range(1, tiles - 1, 2)]
    far = lax.ppermute(far, "tile", beside + [(j, i) for i, j in beside])

    some = shape(secs // 2, strip_rows, LANES)
    keep, send, anchor = call(
        bound(extract, rows, chan), [some, some, shape(8, LANES, dtype=jnp.int32)],
        (nest_box, parent), (HBM, HBM), cost=4 << 20,
        scratch=[
            pltpu.SMEM(nest_box.shape, jnp.int32),
            pltpu.VMEM(parent.shape, F32),
            pltpu.SemaphoreType.DMA((2,)),
        ],
    )
    got = exchange(send, "sec", 1)
    bit = 2
    while bit < secs // 2:
        some = shape(secs // (2 * bit), strip_rows, LANES)
        keep, send = call(bound(combine, bit), [some, some], (keep, got), (VMEM, VMEM), cost=1 << 20)
        got = exchange(send, "sec", bit)
        bit *= 2
    mine, to_sec, to_tile, to_both = call(
        bound(split, rows, chan), [half] * 4, (keep, got), (VMEM, VMEM), cost=1 << 18,
    )
    from_sec = exchange_both(to_sec, secs // 2, 0)
    from_tile = exchange_both(to_tile, 0, 2)
    from_both = exchange_both(to_both, secs // 2, 2)
    moved_shape = shape(col_blocks, chan, ext_rows, LANES)
    square = (nest_cols, nest_cols)
    moved, nudge, back, matrix, table = call(
        bound(nest_first, chan, deep),
        [moved_shape, shape(3, col_blocks, ext_rows, LANES), shape(*square, dtype=jnp.bfloat16),
         shape(*square, dtype=jnp.bfloat16), shape(table_rows(chan, levels), LANES)],
        (nest_box, diffusion, wind_speed, conversion, vert_mix, nest), (SMEM,) * 5 + (VMEM,), cost=6 << 20,
        scratch=[
            pltpu.VMEM((col_blocks, (nest_rows + 2) * chan, LANES), F32),
        ],
    )

    two = shape(2, half_rows, LANES)
    (strip,) = call(
        gathered, [two], (mine, from_sec, from_tile, from_both, moved), (VMEM,) * 5, cost=1 << 18,
    )
    pair = strip
    group = tiles // 2
    while group > 4:
        got = exchange(pair, "tile", group)
        (pair,) = call(
            bound(choose, rows, own_rows, group, tiles), [two], (anchor, pair, got), (VMEM,) * 3, cost=1 << 18,
        )
        group //= 2
    mine, sent = call(
        bound(select, rows, chan, own_rows, tiles), [half] * 2, (anchor, pair), (VMEM,) * 2, cost=1 << 18,
    )
    got = exchange(sent, "tile", 4)
    edge = shape(2, blocks * chan, LANES)
    parent_new, edges = call(
        bound(parent_step, rows, chan), [shape(rows * chan, cols), edge],
        (table, parent, strip), (VMEM,) * 3, cost=8 << 20, out_specs=[ANY, VMEM],
        scratch=[
            pltpu.VMEM((blocks + 2, (rows + 2) * chan, LANES), F32),
            pltpu.VMEM((blocks, rows * chan, LANES), F32),
            pltpu.SemaphoreType.DMA((blocks,)),
        ],
    )

    message = shape(((span + 1) // 2 + 1) * chan, LANES)
    own, *sent = call(
        bound(settle, rows, chan, own_rows, tiles), [half] + [message] * 3,
        (anchor, mine, got, near, edges), (VMEM,) * 5, cost=1 << 18,
    )
    got_a, got_b, got_c = (exchange(block, "tile", k + 1) for k, block in enumerate(sent))

    (parent_new,) = call(
        bound(parent_edges, rows, chan, deep), [shape(rows * chan, cols)],
        (table, near, far, edges, parent_new), (VMEM,) * 4 + (ANY,), cost=1 << 20, out_specs=[ANY], same={4: 0},
        scratch=[
            pltpu.VMEM((2, blocks * chan, LANES), F32),
            pltpu.VMEM((2, blocks * chan, LANES), F32),
            pltpu.SemaphoreType.DMA((2 * blocks,)),
        ],
    )
    (moved,) = call(
        bound(nest_edges, chan, deep), [moved_shape],
        (table, nest, near, far, nudge, matrix, moved), (VMEM,) * 7, cost=3 << 20, same={6: 0},
        scratch=[
            pltpu.VMEM((2 * (deep + 2) * chan, nest_cols), F32),
            pltpu.VMEM((col_blocks, 2 * (deep + 2) * chan, LANES), F32),
        ],
    )

    (nest_new,) = call(
        bound(nest_rest, rows, chan, deep, own_rows, tiles), [shape(nest_rows * chan, nest_cols)],
        (anchor, table, own, got_a, got_b, got_c, moved, nudge, back), (VMEM,) * 9, cost=16 << 20, out_specs=[ANY],
        limit=32,
        scratch=[
            pltpu.VMEM((4, half_rows, LANES), F32),
            pltpu.VMEM((2, (span + 1) * chan, LANES), F32),
            pltpu.VMEM((2, chan, 8, LANES), F32),
            pltpu.VMEM((2, col_blocks, chan, ext_rows + 16, LANES), F32),
            pltpu.VMEM((4, chan, ext_rows, LANES), F32),
            pltpu.VMEM((nest_rows // 8, col_blocks, 8 * chan, LANES), F32),
            pltpu.VMEM((nest_rows // 8, 8 * chan, nest_cols), F32),
            pltpu.SemaphoreType.DMA((nest_rows // 8,)),
        ],
    )

    return parent_new.reshape(parent_old.shape), nest_new.reshape(nest_state.shape)


def solution(mesh):
    placed = (P("tile", None, "sec"), P("sec", "tile", None, None), P(), P(), P(), P(), P())
    return jax.shard_map(
        body,
        mesh=mesh,
        in_specs=placed,
        out_specs=(P("tile", None, "sec"), P("sec", "tile", None, None)),
        check_vma=False,
    )
```

```python
import jax
import jax.numpy as jnp
from jax import lax
from jax.experimental import pallas as pl
from jax.experimental.pallas import tpu as pltpu
from jax.sharding import PartitionSpec as P

NSTEP = 4
RATIO = 4
LANES = 128
F32 = jnp.float32
VMEM = pl.BlockSpec(memory_space=pltpu.VMEM)
SMEM = pl.BlockSpec(memory_space=pltpu.SMEM)
ANY = pl.BlockSpec(memory_space=pl.ANY)
HBM = pl.BlockSpec(memory_space=pltpu.HBM)
TOGETHER = 16


def call(kernel, outs, args, specs, scratch=(), limit=16, cost=0, out_specs=None, same=None):
    return pl.pallas_call(
        kernel,
        out_shape=list(outs),
        in_specs=list(specs),
        out_specs=[VMEM] * len(outs) if out_specs is None else out_specs,
        scratch_shapes=list(scratch),
        input_output_aliases=same or {},
        compiler_params=pltpu.CompilerParams(vmem_limit_bytes=limit << 20),
        cost_estimate=pl.CostEstimate(flops=0, bytes_accessed=cost, transcendentals=0),
    )(*args)


def shape(*dims, dtype=F32):
    return jax.ShapeDtypeStruct(dims, dtype)


def lane_ids():
    return lax.broadcasted_iota(jnp.int32, (8, LANES), 1)


def sublane_ids():
    return lax.broadcasted_iota(jnp.int32, (8, LANES), 0)


def one_if(condition):
    return jnp.where(condition, 1.0, 0.0).astype(F32)


def aligned(start, step):
    return pl.multiple_of(start, step)


def edge_rows(deep, chan, nest, parent, near, far, sems):
    odd = lax.rem(lax.axis_index("tile"), 2)
    cols = nest.shape[1]
    copies = []
    for k, (dest, last) in enumerate(((near, 1 - odd), (far, odd))):
        size = deep * chan
        at = aligned(last * (nest.shape[0] - size), 8)
        copies.append((nest.at[pl.ds(at, size), :], dest.at[pl.ds(0, size), :]))
        at = aligned(last * (parent.shape[0] - chan), 8)
        for part in range(parent.shape[1] // cols):
            source = parent.at[pl.ds(at, chan), pl.ds(part * cols, cols)]
            copies.append((source, dest.at[pl.ds(size + part * chan, chan), :]))
    made = [pltpu.make_async_copy(a, b, sems.at[i]) for i, (a, b) in enumerate(copies)]
    for copy in made:
        copy.start()
    for copy in made:
        copy.wait()


def extract(rows, chan, box_in, parent_in, keep, send, anchor, box, parent, sems):
    copies = [
        pltpu.make_async_copy(box_in, box, sems.at[0]),
        pltpu.make_async_copy(parent_in, parent, sems.at[1]),
    ]
    for copy in copies:
        copy.start()
    for copy in copies:
        copy.wait()
    cols = parent.shape[1]
    blocks = cols // LANES
    groups = chan // 8
    sec = lax.axis_index("sec")
    half = lax.rem(sec, 2)
    lane = lane_ids()
    anchor[...] = jnp.full((8, LANES), box[sec, 0], jnp.int32)

    def at(row, g):
        return pl.ds(aligned(row * chan + 8 * g, 8), 8)

    lane_row = lax.div(lane, 2)
    together = TOGETHER

    def outer(step, packed):
        packed = list(packed)
        for k in range(together):
            row = step * together + k
            for g in range(groups):
                ends = jnp.where(
                    lane < LANES // 2,
                    parent[at(row, g), pl.ds(0, LANES)],
                    parent[at(row, g), pl.ds(cols - LANES, LANES)],
                )
                ends = pltpu.roll(ends, 2 * rows + 2 * row + 1, axis=1)
                packed[g] = jnp.where(lane_row == rows + row, ends, packed[g])
        return tuple(packed)

    zeros = (jnp.zeros((8, LANES), F32),) * groups
    halo = lax.fori_loop(0, rows // together, outer, zeros)

    for which, dest in ((1 - half, send), (half, keep)):

        @pl.loop(0, dest.shape[0])
        def _(i):
            nest = 2 * i + which
            offset = box[nest, 1] - sec * cols
            shift = lax.bitwise_and(offset, LANES - 1)
            back = lax.bitwise_and(LANES - shift, LANES - 1)

            def place(k):
                start = aligned(jnp.clip(k, 0, blocks - 1) * LANES, LANES)
                return pl.ds(start, LANES), one_if((k >= 0) & (k < blocks))

            first = lax.shift_right_arithmetic(offset, 7)
            at_a, on_a = place(first)
            at_b, on_b = place(first + 1)
            at_c, on_c = place(lax.shift_right_arithmetic(offset - 1, 7))
            before = lax.bitwise_and(lane - shift, LANES - 1) >= LANES // 2
            sent = jnp.where(lax.rem(lane, 2) == 0, one_if(nest == sec + 1), one_if(nest == sec - 1))

            def inner(step, packed):
                packed = list(packed)
                shifted = []
                for k in range(together):
                    row = step * together + k
                    turn = lax.bitwise_and(back + 2 * row + 1, LANES - 1)
                    for g in range(groups):
                        a = parent[at(row, g), at_a] * on_a
                        b = parent[at(row, g), at_b] * on_b
                        c = parent[at(row, g), at_c] * on_c
                        main = pltpu.roll(jnp.where(lane < shift, b, a), back, axis=1)
                        shifted.append((at(row, g), main))
                        side = pltpu.roll(jnp.where(before, c, b), turn, axis=1)
                        packed[g] = jnp.where(lane_row == row, side, packed[g])
                for where, main in shifted:
                    dest[i, where, :] = main
                return tuple(packed)

            here = (offset >= -LANES) & (offset <= cols)

            @pl.when(here)
            def _():
                packed = lax.fori_loop(0, rows // together, inner, tuple(h * sent for h in halo))
                for g in range(groups):
                    dest[i, pl.ds(rows * chan + 8 * g, 8), :] = packed[g]

            @pl.when(jnp.logical_not(here))
            def _():
                dest[i, pl.ds(0, rows * chan), :] = jnp.zeros((rows * chan, LANES), F32)
                for g in range(groups):
                    dest[i, pl.ds(rows * chan + 8 * g, 8), :] = halo[g] * sent


def combine(bit, own, got, keep, send):
    mine = lax.rem(lax.axis_index("sec") // bit, 2)
    for i in range(keep.shape[0]):
        send[i] = own[2 * i + 1 - mine] + got[2 * i + 1 - mine]
        keep[i] = own[2 * i + mine] + got[2 * i + mine]


def split(rows, chan, own, got, mine, to_sec, to_tile, to_both):
    sec = lax.div(lax.axis_index("sec"), lax.axis_size("sec") // 2)
    part = lax.rem(lax.div(lax.axis_index("tile"), 2), 2)
    size = rows // 2 * chan
    for dest, nest, half in (
        (to_sec, 1 - sec, part),
        (to_both, 1 - sec, 1 - part),
        (to_tile, sec, 1 - part),
        (mine, sec, part),
    ):
        for j in range(rows // 2):
            at = pl.ds(aligned((2 * j + half) * chan, 8), chan)
            dest[pl.ds(j * chan, chan), :] = own[nest, at, :] + got[nest, at, :]
        at = pl.ds(rows * chan, chan)
        dest[pl.ds(size, chan), :] = own[nest, at, :] + got[nest, at, :]


def gathered(mine, from_sec, from_tile, from_both, moved, out):
    out[0] = mine[...] + from_sec[...]
    out[1] = from_tile[...] + from_both[...]


def held_block(anchor, tile, rows, own_rows, group):
    first = lax.div(tile, group) * group
    low = jnp.maximum(anchor + (own_rows * first - 2), 0)
    base = lax.shift_right_arithmetic(low, rows.bit_length() - 1)
    return base + lax.bitwise_and(tile - base, group - 1)


def held(anchor, tile, rows, own_rows, group, tiles):
    if group == tiles:
        return jnp.full((8, LANES), tile, jnp.int32)
    return held_block(anchor, tile, rows, own_rows, group)


def choose(rows, own_rows, group, tiles, anchor, own, got, out):
    start = anchor[...]
    for k in range(2):
        tile = lax.bitwise_xor(lax.axis_index("tile"), 2 * k)
        keep = held(start, tile, rows, own_rows, 2 * group, tiles) == held_block(
            start, tile, rows, own_rows, group
        )
        for r in range(0, out.shape[1], 8):
            at = pl.ds(r, 8)
            out[k, at, :] = jnp.where(keep, own[k, at, :], got[k, at, :])


def wanted(anchor, row, tile, group, own_rows):
    first = lax.div(tile, group) * group
    low = anchor + (own_rows * first - 2)
    return (row >= low) & (row <= low + own_rows * group + 4)


def slot_rows(rows, own_rows, tiles, anchor):
    tile = lax.axis_index("tile")
    return [
        rows * held(anchor, lax.bitwise_xor(tile, 2 * k), rows, own_rows, 8, tiles) for k in range(2)
    ]


def select(rows, chan, own_rows, tiles, anchor, both, mine, sent):
    start = anchor[...]
    tile = lax.axis_index("tile")
    part = lax.rem(lax.div(tile, 2), 2)
    size = rows // 2 * chan
    base = slot_rows(rows, own_rows, tiles, start)
    lane_row = lax.div(lane_ids(), 2)
    for dest, owner in ((sent, lax.bitwise_xor(tile, 4)), (mine, tile)):
        for j in range(rows // 2 + 1):
            row = lane_row if j == rows // 2 else 2 * j + part
            second = wanted(start, base[1] + row, owner, 4, own_rows)
            for g in range(chan // 8):
                at = pl.ds(j * chan + 8 * g, 8)
                dest[at, :] = jnp.where(second, both[1, at, :], both[0, at, :])


def settle(rows, chan, own_rows, tiles, anchor, mine, got, near, parent, out, *sent):
    start = anchor[...]
    tile = lax.axis_index("tile")
    part = lax.rem(lax.div(tile, 2), 2)
    base = slot_rows(rows, own_rows, tiles, start)
    lane_row = lax.div(lane_ids(), 2)
    groups = range(chan // 8)
    slots = rows // 2
    held_rows = {}
    for j in range(slots + 1):
        row = lane_row if j == slots else 2 * j + part
        keep = wanted(start, base[0] + row, tile, 4, own_rows)
        keep = keep | wanted(start, base[1] + row, tile, 4, own_rows)
        for g in groups:
            at = pl.ds(j * chan + 8 * g, 8)
            held_rows[j, g] = jnp.where(keep, mine[at, :], got[at, :])
            out[at, :] = held_rows[j, g]
    for k, dest in enumerate(sent):
        count = dest.shape[0] // chan - 1
        first = start + (own_rows * lax.bitwise_xor(tile, k + 1) - 2)
        first = lax.shift_right_arithmetic(first + lax.bitwise_and(lax.bitwise_xor(first, part), 1), 1)
        for i in range(count):
            slot = lax.bitwise_and(first + i, slots - 1)
            row = [held_rows[0, g] for g in groups]
            for j in range(1, slots):
                row = [jnp.where(slot == j, held_rows[j, g], row[g]) for g in groups]
            for g in groups:
                dest[pl.ds(i * chan + 8 * g, 8), :] = row[g]
        for g in groups:
            dest[pl.ds(count * chan + 8 * g, 8), :] = held_rows[slots, g]


def table_rows(chan, levels):
    return 4 * chan + 2 * levels + chan


def make_table(diff, wind, conv, mix, table):
    chan, levels = diff.shape[0], conv.shape[1]

    def line(value):
        return jnp.full((1, LANES), value, F32)

    def put(i, value):
        table[pl.ds(i, 1), :] = value

    scale = {}
    for f in range(3):
        m = line(mix[f])
        ratio = None
        for l in range(levels):
            c = f * levels + l
            pivot = 1.0 + (1.0 if l in (0, levels - 1) else 2.0) * m
            if l:
                pivot = pivot - m * ratio
            inverse = 1.0 / pivot
            ratio = m * inverse
            put(4 * chan + 2 * levels + c, ratio)
            scale[c] = inverse * (1.0 - line(conv[f, l])) if f < 2 else inverse
            d, wx, wy = diff[c], wind[0, c], wind[1, c]
            for k, value in enumerate((1.0 - 4.0 * d - wx - wy, d + wx, d + wy, d)):
                put(4 * c + k, scale[c] * line(value))
            if f:
                before = c - levels
                put(4 * chan + before, scale[c] * line(conv[f - 1, l]) / scale[before])


def rows_of(table):
    def coef(i):
        return jnp.broadcast_to(table[pl.ds(i, 1), :], (8, LANES))

    return coef


def step_blocks(chan, table, loads, stores):
    coef = rows_of(table)

    def horizontal(c):
        center, above, left, spread = (coef(4 * c + k) for k in range(4))
        out = []
        for load in loads:
            v, n, s, w, e = load(c)
            out.append(center * v + above * n + left * w + spread * (s + e))
        return out

    mix_blocks(chan, table, horizontal, stores)


def mix_blocks(chan, table, fields, stores):
    levels = chan // 3
    blocks = range(len(stores))
    coef = rows_of(table)
    ys = {}
    for l in range(levels):
        for f in range(3):
            c = f * levels + l
            row = fields(c)
            if f:
                rate = coef(4 * chan + c - levels)
                row = [row[b] + rate * given[b] for b in blocks]
            given = row
            if l:
                ratio = coef(4 * chan + 2 * levels + c)
                row = [row[b] + ratio * ys[c - 1][b] for b in blocks]
            ys[c] = row
    xs = {}
    for l in range(levels - 1, -1, -1):
        for f in range(3):
            c = f * levels + l
            xs[f] = ys[c] if l == levels - 1 else [
                ys[c][b] + coef(4 * chan + 2 * levels + c) * xs[f][b] for b in blocks
            ]
            for b in blocks:
                stores[b](c, xs[f][b])


def sides(lane, west, v, east):
    w = pltpu.roll(jnp.where(lane == LANES - 1, west, v), 1, axis=1)
    e = pltpu.roll(jnp.where(lane == 0, east, v), LANES - 1, axis=1)
    return w, e


def parent_step(rows, chan, table, parent, strip, out, edges, ext, done, sems):
    blocks = parent.shape[1] // LANES
    groups = chan // 8
    lane = lane_ids()
    packed_at = strip.shape[1] - chan

    def columns(j):
        return pl.ds(aligned(j * LANES, LANES), LANES)

    packed = [strip[0, pl.ds(packed_at + 8 * g, 8), :] for g in range(groups)]

    @pl.loop(0, rows)
    def _(row):
        for g in range(groups):
            at = pl.ds(aligned((row + 1) * chan + 8 * g, 8), 8)
            turn = LANES - 1 - 2 * rows - 2 * row
            turned = pltpu.roll(packed[g], turn, axis=1)
            ext[0, at, :] = turned
            ext[blocks + 1, at, :] = turned

    @pl.loop(0, blocks)
    def _(j):
        ext[j + 1, pl.ds(chan, rows * chan), :] = parent[:, columns(j)]
        ext[j + 1, pl.ds(0, chan), :] = jnp.zeros((chan, LANES), F32)
        ext[j + 1, pl.ds((rows + 1) * chan, chan), :] = jnp.zeros((chan, LANES), F32)

    @pl.loop(0, blocks)
    def _(j):
        def block(first):
            def loads(c):
                def at(r):
                    return pl.ds((first + r) * chan + c, 8, stride=chan)

                v = ext[j + 1, at(1), :]
                w, e = sides(lane, ext[j, at(1), :], v, ext[j + 2, at(1), :])
                return v, ext[j + 1, at(0), :], ext[j + 1, at(2), :], w, e

            def store(c, x):
                done[j, pl.ds(first * chan + c, 8, stride=chan), :] = x

            return loads, store

        loads, stores = zip(*(block(first) for first in range(0, rows, 8)))
        step_blocks(chan, table, loads, stores)
        at = pl.ds(aligned(j * chan, 8), chan)
        edges[0, at, :] = done[j, pl.ds(0, chan), :]
        edges[1, at, :] = done[j, pl.ds((rows - 1) * chan, chan), :]
        pltpu.make_async_copy(done.at[j], out.at[:, columns(j)], sems.at[j]).start()

    @pl.loop(0, blocks)
    def _(j):
        pltpu.make_async_copy(done.at[j], out.at[:, columns(j)], sems.at[j]).wait()


def parent_edges(rows, chan, deep, table, near, far, edges, given, out, beside, done, sems):
    blocks = edges.shape[1] // chan
    per = near.shape[1] // LANES
    odd = lax.rem(lax.axis_index("tile"), 2) == 1
    for j in range(blocks):
        for g in range(chan // 8):
            at = pl.ds((deep + j // per) * chan + 8 * g, 8)
            a, b = (ref[at, pl.ds(j % per * LANES, LANES)] for ref in (near, far))
            at = pl.ds(j * chan + 8 * g, 8)
            beside[0, at, :] = jnp.where(odd, a, b)
            beside[1, at, :] = jnp.where(odd, b, a)
    coef = rows_of(table)
    pieces = [(k, b) for k in range(2) for b in range(0, blocks, 8)]

    def at(b, c):
        return pl.ds(b * chan + c, 8, stride=chan)

    def fields(c):
        return [coef(4 * c + (1, 3)[k]) * beside[k, at(b, c), :] for k, b in pieces]

    def storing(k, b):
        def store(c, x):
            done[k, at(b, c), :] = edges[k, at(b, c), :] + x

        return store

    mix_blocks(chan, table, fields, [storing(k, b) for k, b in pieces])
    copies = []
    for k, row in enumerate((0, rows - 1)):
        for j in range(blocks):
            copies.append(
                pltpu.make_async_copy(
                    done.at[k, pl.ds(j * chan, chan), :],
                    out.at[pl.ds(row * chan, chan), pl.ds(j * LANES, LANES)],
                    sems.at[k * blocks + j],
                )
            )
    for copy in copies:
        copy.start()
    for copy in copies:
        copy.wait()


def dealing(cols, back):
    first = lax.broadcasted_iota(jnp.int32, (cols, cols), 0)
    second = lax.broadcasted_iota(jnp.int32, (cols, cols), 1)
    planes = cols // LANES
    natural, dealt = (second, first) if back else (first, second)
    hit = natural == planes * lax.bitwise_and(dealt, LANES - 1) + lax.shift_right_arithmetic(dealt, 7)
    return jnp.where(hit, 1.0, 0.0).astype(jnp.bfloat16)


def dealt(x, matrix):
    out = None
    for _ in range(3):
        part = x.astype(jnp.bfloat16)
        x = x - part.astype(F32)
        term = jnp.dot(part, matrix, preferred_element_type=F32)
        out = term if out is None else out + term
    return out


def plane_blocks(chan, table, planes, lane, load, store):
    cache = {}

    def center(k, c):
        if (k, c) not in cache:
            cache[k, c] = load(0, k, c)
        return cache[k, c]

    def block(k):
        def loads(c):
            if k == 0:
                w = jnp.where(lane == 0, 0.0, pltpu.roll(center(planes - 1, c), 1, axis=1))
            else:
                w = center(k - 1, c)
            if k == planes - 1:
                e = jnp.where(lane == LANES - 1, 0.0, pltpu.roll(center(0, c), LANES - 1, axis=1))
            else:
                e = center(k + 1, c)
            return center(k, c), load(-1, k, c), load(1, k, c), w, e

        def put(c, x):
            store(k, c, x)

        return loads, put

    loads, stores = zip(*(block(k) for k in range(planes)))
    step_blocks(chan, table, loads, stores)


def nest_first(chan, deep, box, diff, wind, conv, mix, nest, moved, nudge, back, matrix, table, ext):
    make_table(diff, wind, conv, mix, table)
    nest_rows = nest.shape[0] // chan
    planes = nest.shape[1] // LANES
    ext_rows = nest_rows + 2 * deep
    groups = chan // 8
    sec, tile = lax.axis_index("sec"), lax.axis_index("tile")
    extent_x, extent_y = box[sec, 2], box[sec, 3]
    lane, sub = lane_ids(), sublane_ids()
    first_row = nest_rows * tile - deep
    matrix[...] = dealing(nest.shape[1], False)
    back[...] = dealing(nest.shape[1], True)
    for k in range(planes):
        col = planes * lane + k
        for rb in range(0, ext_rows, 8):
            i = first_row + rb + sub
            live = one_if((i >= 0) & (i < extent_x) & (col < extent_y))
            dist = jnp.minimum(jnp.minimum(i, col), jnp.minimum(extent_x - 1 - i, extent_y - 1 - col))
            dist = jnp.maximum(dist, 0).astype(F32)
            rate = 0.1 + 0.4 * jnp.exp(-dist / 3.0)
            nudge[0, k, pl.ds(rb, 8), :] = live * (1.0 - rate)
            nudge[1, k, pl.ds(rb, 8), :] = live * rate
            nudge[2, k, pl.ds(rb, 8), :] = live

    together = nest_rows

    @pl.loop(0, nest_rows // together)
    def _(step):
        size = together * chan
        x = dealt(nest[pl.ds(aligned(step * size, 8), size), :], matrix[...])
        for r in range(together):
            row = step * together + r
            for k in range(planes):
                live = jnp.broadcast_to(nudge[2, k, pl.ds(deep + row, 1), :], (8, LANES))
                for g in range(groups):
                    piece = x[r * chan + 8 * g : r * chan + 8 * g + 8, k * LANES : (k + 1) * LANES]
                    ext[k, pl.ds(aligned((row + 1) * chan + 8 * g, 8), 8), :] = piece * live

    for row in (0, nest_rows + 1):
        ext[:, pl.ds(row * chan, chan), :] = jnp.zeros((planes, chan, LANES), F32)
    for rb in range(0, nest_rows, 8):

        def load(shift, k, c):
            return ext[k, pl.ds((rb + 1 + shift) * chan + c, 8, stride=chan), :]

        def store(k, c, x):
            at = pl.ds(deep + rb, 8)
            moved[k, c, at, :] = x * nudge[0, k, at, :]

        plane_blocks(chan, table, planes, lane, load, store)


def nest_edges(chan, deep, table, nest, near, far, nudge, matrix, given, moved, natural, ext):
    nest_rows = nest.shape[0] // chan
    planes = nest.shape[1] // LANES
    ext_rows = nest_rows + 2 * deep
    size = deep * chan
    lane, sub = lane_ids(), sublane_ids()
    odd = lax.rem(lax.axis_index("tile"), 2) == 1
    edge = (deep + 2) * chan
    a, b = near[pl.ds(0, size), :], far[pl.ds(0, size), :]
    natural[pl.ds(0, size), :] = jnp.where(odd, a, b)
    natural[pl.ds(size, 2 * chan), :] = nest[pl.ds(0, 2 * chan), :]
    natural[pl.ds(edge, 2 * chan), :] = nest[pl.ds((nest_rows - 2) * chan, 2 * chan), :]
    natural[pl.ds(edge + 2 * chan, size), :] = jnp.where(odd, b, a)
    for half in range(2):

        def rows_at(r):
            return r if half == 0 else ext_rows - deep - 2 + r

        x = dealt(natural[pl.ds(half * edge, edge), :], matrix[...])
        for r in range(deep + 2):
            for k in range(planes):
                live = jnp.broadcast_to(nudge[2, k, pl.ds(rows_at(r), 1), :], (8, LANES))
                for g in range(chan // 8):
                    piece = x[r * chan + 8 * g : r * chan + 8 * g + 8, k * LANES : (k + 1) * LANES]
                    ext[k, pl.ds(half * edge + r * chan + 8 * g, 8), :] = piece * live

    def load(shift, k, c):
        upper = ext[k, pl.ds((1 + shift) * chan + c, 8, stride=chan), :]
        lower = ext[k, pl.ds((3 + shift) * chan + c, 8, stride=chan), :]
        return jnp.where(sub < deep, upper, lower)

    def store(k, c, x):
        low, high = pl.ds(1, deep), pl.ds(ext_rows - 1 - deep, deep)
        moved[k, c, low, :] = x[:deep] * nudge[0, k, low, :]
        moved[k, c, high, :] = x[deep:] * nudge[0, k, high, :]

    plane_blocks(chan, table, planes, lane, load, store)


def nest_rest(
    rows, chan, deep, own_rows, tiles,
    anchor, table, own, got_a, got_b, got_c, moved, nudge, back, out,
    slots, foot, coarse, state, force, done, final, sems,
):
    planes, _, ext_rows, _ = moved.shape
    nest_rows = ext_rows - 2 * deep
    groups = chan // 8
    tile = lax.axis_index("tile")
    lane, sub = lane_ids(), sublane_ids()
    first_row = nest_rows * tile - deep
    start = jnp.max(anchor[...]) + own_rows * tile - 2
    span = foot.shape[1] // chan - 1
    size = rows // 2 * chan
    part = lax.rem(lax.div(tile, 2), 2)
    side = lax.rem(tile, 2)

    slots[0] = own[...]
    for k, ref in enumerate((got_a, got_b, got_c)):
        count = ref.shape[0] - chan
        slots[k + 1, pl.ds(0, count), :] = ref[pl.ds(0, count), :]
        slots[k + 1, pl.ds(size, chan), :] = ref[pl.ds(count, chan), :]

    for m in range(span):
        row = start + m
        local = lax.bitwise_and(row, rows - 1)
        other = lax.bitwise_and(lax.shift_right_arithmetic(row, rows.bit_length() - 1), 1)
        k = 2 * lax.bitwise_xor(lax.bitwise_and(row, 1), part) + lax.bitwise_xor(other, side)
        inside = one_if((row >= 0) & (row < rows * tiles))
        slot = jnp.where(k == 0, lax.shift_right_arithmetic(local, 1), m // 2) * chan
        turn = LANES - 1 - 2 * local
        for g in range(groups):
            at = pl.ds(m * chan + 8 * g, 8)
            foot[0, at, :] = pltpu.roll(slots[k, pl.ds(size + 8 * g, 8), :] * inside, turn, axis=1)
            foot[1, at, :] = slots[k, pl.ds(aligned(slot + 8 * g, 8), 8), :] * inside

    for k in range(2):
        foot[k, pl.ds(span * chan, chan), :] = jnp.zeros((chan, LANES), F32)

    def foot_loads(c):
        def at(r):
            return pl.ds(r * chan + c, 8, stride=chan)

        v = foot[1, at(1), :]
        edge = foot[0, at(1), :]
        w, e = sides(lane, edge, v, edge)
        return v, foot[1, at(0), :], foot[1, at(2), :], w, e

    def foot_store(c, x):
        old = foot[1, pl.ds(chan + c, 8, stride=chan), :]
        coarse[0, c] = old
        coarse[1, c] = x - old

    step_blocks(chan, table, [foot_loads], [foot_store])

    share = []
    for rb in range(0, ext_rows, 8):
        p = lax.rem(sub, RATIO).astype(F32) / RATIO
        share.append(jnp.where(first_row + rb + sub >= RATIO * (own_rows * tiles - 1), 0.0, p))

    together = 12

    @pl.loop(0, chan // together)
    def _(i):
        for c in (together * i + t for t in range(together)):
            for rb in range(0, ext_rows, 8):
                u = rb // RATIO
                at = pl.ds(rb, 8)
                lines = []
                for t in range(2):
                    r0, r1, r2 = (
                        jnp.broadcast_to(coarse[t, c, pl.ds(u + n, 1), :], (8, LANES)) for n in range(3)
                    )
                    a0 = jnp.where(sub < RATIO, r0, r1)
                    a1 = jnp.where(sub < RATIO, r1, r2)
                    level = a0 + share[rb // 8] * (a1 - a0)
                    beside = jnp.where(lane == LANES - 1, level, pltpu.roll(level, LANES - 1, axis=1))
                    slope = (beside - level) * (1.0 / RATIO)
                    force[t, c, at, :] = level
                    force[2 + t, c, at, :] = slope
                    lines.append((level, slope))
                level, slope = (old + new * (1.0 / NSTEP) for old, new in zip(*lines))
                for k in range(planes):
                    g = level + float(k) * slope if k else level
                    state[0, k, c, pl.ds(8 + rb, 8), :] = moved[k, c, at, :] + nudge[1, k, at, :] * g

    def advance(step, src, rb, put):
        weight = jnp.float32(step + 1) / NSTEP
        at = pl.ds(rb, 8)
        lines = {}

        def load(shift, k, c):
            return state[src, k, c, pl.ds(8 + rb + shift, 8), :]

        def store(k, c, x):
            if c not in lines:
                lines[c] = [force[t, c, at, :] + weight * force[t + 1, c, at, :] for t in (0, 2)]
            level, slope = lines[c]
            g = level + float(k) * slope if k else level
            put(k, c, nudge[0, k, at, :] * x + nudge[1, k, at, :] * g)

        plane_blocks(chan, table, planes, lane, load, store)

    @pl.loop(1, NSTEP - 1)
    def _(step):
        src = lax.rem(step + 1, 2)

        @pl.loop(0, ext_rows // 8)
        def _(block):
            rb = aligned(block * 8, 8)

            def put(k, c, x):
                state[1 - src, k, c, pl.ds(8 + rb, 8), :] = x

            advance(step, src, rb, put)

    copies = []
    for n, rb in enumerate(range(0, nest_rows, 8)):

        def put(k, c, x):
            done[n, k, pl.ds(c, 8, stride=chan), :] = x

        advance(NSTEP - 1, NSTEP % 2, deep + rb, put)
        whole = jnp.concatenate([done[n, k] for k in range(planes)], axis=1)
        final[n] = dealt(whole, back[...])
        copies.append(
            pltpu.make_async_copy(final.at[n], out.at[pl.ds(rb * chan, 8 * chan), :], sems.at[n])
        )
        copies[n].start()
    for copy in copies:
        copy.wait()


def bound(kernel, *static):
    def run(*refs):
        return kernel(*static, *refs)

    return run


def exchange(block, axis, bit):
    return lax.ppermute(block, axis, [(i, i ^ bit) for i in range(lax.axis_size(axis))])


def exchange_both(block, sec_bit, tile_bit):
    secs, tiles = lax.axis_size("sec"), lax.axis_size("tile")
    route = [
        (s * tiles + t, (s ^ sec_bit) * tiles + (t ^ tile_bit)) for s in range(secs) for t in range(tiles)
    ]
    return lax.ppermute(block, ("sec", "tile"), route)


def body(parent_old, nest_state, diffusion, wind_speed, conversion, vert_mix, nest_box):
    rows, chan, cols = parent_old.shape
    nest_rows, nest_cols = nest_state.shape[1], nest_state.shape[3]
    secs, tiles = lax.axis_size("sec"), lax.axis_size("tile")
    own_rows = nest_rows // RATIO
    levels = conversion.shape[1]
    deep = NSTEP
    ext_rows = nest_rows + 2 * deep
    col_blocks = nest_cols // LANES
    blocks = cols // LANES
    span = (ext_rows // RATIO + 1) + 2
    strip_rows = (rows + 1) * chan
    half_rows = (rows // 2 + 1) * chan
    parent = parent_old.reshape(rows * chan, cols)
    nest = nest_state.reshape(nest_rows * chan, nest_cols)
    half = shape(half_rows, LANES)

    halo = shape((deep + cols // nest_cols) * chan, nest_cols)
    near, far = call(
        bound(edge_rows, deep, chan), [halo] * 2, (nest, parent), (ANY, ANY),
        scratch=[pltpu.SemaphoreType.DMA((2 * (1 + cols // nest_cols),))], limit=4, cost=1 << 20,
    )
    near = exchange(near, "tile", 1)
    beside = [(i, i + 1) for i in range(1, tiles - 1, 2)]
    far = lax.ppermute(far, "tile", beside + [(j, i) for i, j in beside])

    some = shape(secs // 2, strip_rows, LANES)
    keep, send, anchor = call(
        bound(extract, rows, chan), [some, some, shape(8, LANES, dtype=jnp.int32)],
        (nest_box, parent), (HBM, HBM), cost=4 << 20,
        scratch=[
            pltpu.SMEM(nest_box.shape, jnp.int32),
            pltpu.VMEM(parent.shape, F32),
            pltpu.SemaphoreType.DMA((2,)),
        ],
    )
    got = exchange(send, "sec", 1)
    bit = 2
    while bit < secs // 2:
        some = shape(secs // (2 * bit), strip_rows, LANES)
        keep, send = call(bound(combine, bit), [some, some], (keep, got), (VMEM, VMEM), cost=1 << 20)
        got = exchange(send, "sec", bit)
        bit *= 2
    mine, to_sec, to_tile, to_both = call(
        bound(split, rows, chan), [half] * 4, (keep, got), (VMEM, VMEM), cost=1 << 18,
    )
    from_sec = exchange_both(to_sec, secs // 2, 0)
    from_tile = exchange_both(to_tile, 0, 2)
    from_both = exchange_both(to_both, secs // 2, 2)
    moved_shape = shape(col_blocks, chan, ext_rows, LANES)
    square = (nest_cols, nest_cols)
    moved, nudge, back, matrix, table = call(
        bound(nest_first, chan, deep),
        [moved_shape, shape(3, col_blocks, ext_rows, LANES), shape(*square, dtype=jnp.bfloat16),
         shape(*square, dtype=jnp.bfloat16), shape(table_rows(chan, levels), LANES)],
        (nest_box, diffusion, wind_speed, conversion, vert_mix, nest), (SMEM,) * 5 + (VMEM,), cost=6 << 20,
        scratch=[
            pltpu.VMEM((col_blocks, (nest_rows + 2) * chan, LANES), F32),
        ],
    )

    two = shape(2, half_rows, LANES)
    (strip,) = call(
        gathered, [two], (mine, from_sec, from_tile, from_both, moved), (VMEM,) * 5, cost=1 << 18,
    )
    pair = strip
    group = tiles // 2
    while group > 4:
        got = exchange(pair, "tile", group)
        (pair,) = call(
            bound(choose, rows, own_rows, group, tiles), [two], (anchor, pair, got), (VMEM,) * 3, cost=1 << 18,
        )
        group //= 2
    mine, sent = call(
        bound(select, rows, chan, own_rows, tiles), [half] * 2, (anchor, pair), (VMEM,) * 2, cost=1 << 18,
    )
    got = exchange(sent, "tile", 4)
    edge = shape(2, blocks * chan, LANES)
    parent_new, edges = call(
        bound(parent_step, rows, chan), [shape(rows * chan, cols), edge],
        (table, parent, strip), (VMEM,) * 3, cost=8 << 20, out_specs=[ANY, VMEM],
        scratch=[
            pltpu.VMEM((blocks + 2, (rows + 2) * chan, LANES), F32),
            pltpu.VMEM((blocks, rows * chan, LANES), F32),
            pltpu.SemaphoreType.DMA((blocks,)),
        ],
    )

    message = shape(((span + 1) // 2 + 1) * chan, LANES)
    own, *sent = call(
        bound(settle, rows, chan, own_rows, tiles), [half] + [message] * 3,
        (anchor, mine, got, near, edges), (VMEM,) * 5, cost=1 << 18,
    )
    got_a, got_b, got_c = (exchange(block, "tile", k + 1) for k, block in enumerate(sent))

    (parent_new,) = call(
        bound(parent_edges, rows, chan, deep), [shape(rows * chan, cols)],
        (table, near, far, edges, parent_new), (VMEM,) * 4 + (ANY,), cost=1 << 20, out_specs=[ANY], same={4: 0},
        scratch=[
            pltpu.VMEM((2, blocks * chan, LANES), F32),
            pltpu.VMEM((2, blocks * chan, LANES), F32),
            pltpu.SemaphoreType.DMA((2 * blocks,)),
        ],
    )
    (moved,) = call(
        bound(nest_edges, chan, deep), [moved_shape],
        (table, nest, near, far, nudge, matrix, moved), (VMEM,) * 7, cost=3 << 20, same={6: 0},
        scratch=[
            pltpu.VMEM((2 * (deep + 2) * chan, nest_cols), F32),
            pltpu.VMEM((col_blocks, 2 * (deep + 2) * chan, LANES), F32),
        ],
    )

    (nest_new,) = call(
        bound(nest_rest, rows, chan, deep, own_rows, tiles), [shape(nest_rows * chan, nest_cols)],
        (anchor, table, own, got_a, got_b, got_c, moved, nudge, back), (VMEM,) * 9, cost=16 << 20, out_specs=[ANY],
        limit=32,
        scratch=[
            pltpu.VMEM((4, half_rows, LANES), F32),
            pltpu.VMEM((2, (span + 1) * chan, LANES), F32),
            pltpu.VMEM((2, chan, 8, LANES), F32),
            pltpu.VMEM((2, col_blocks, chan, ext_rows + 16, LANES), F32),
            pltpu.VMEM((4, chan, ext_rows, LANES), F32),
            pltpu.VMEM((nest_rows // 8, col_blocks, 8 * chan, LANES), F32),
            pltpu.VMEM((nest_rows // 8, 8 * chan, nest_cols), F32),
            pltpu.SemaphoreType.DMA((nest_rows // 8,)),
        ],
    )

    return parent_new.reshape(parent_old.shape), nest_new.reshape(nest_state.shape)


def solution(mesh):
    placed = (P("tile", None, "sec"), P("sec", "tile", None, None), P(), P(), P(), P(), P())
    return jax.shard_map(
        body,
        mesh=mesh,
        in_specs=placed,
        out_specs=(P("tile", None, "sec"), P("sec", "tile", None, None)),
        check_vma=False,
    )
```
